32 devices in a mesh: acct: 8 (over z, y), merch: 4 (over x, core).
Axes of the slice: x: 2, y: 2, z: 4, core: 2. Of those that a mesh axis runs over, the one named last changes fastest.
Arguments:
- acct_feat: bfloat16 [131072, 512], P(('acct', 'merch')), may hold values from -6 to 6
- merch_feat: bfloat16 [1024, 512], P(('acct', 'merch')), may hold values from -6 to 6
- key_weight: bfloat16 [4, 512, 512], replicated, may hold values from -0.25 to 0.25
- msg_weight: bfloat16 [4, 512, 512], replicated, may hold values from -0.25 to 0.25
- query_weight: bfloat16 [512, 512], replicated, may hold values from -0.25 to 0.25
- out_weight: bfloat16 [512, 512], replicated, may hold values from -0.25 to 0.25
- rel_bias: float32 [4], replicated, may hold values from -2 to 2
- out_gain: float32 [512], replicated, may hold values from 0.5 to 1.5
- slot_acct: int32 [1024, 128], P(('acct', 'merch')), may hold values from 0 to 4095
- slot_merch: int32 [1024, 128], P(('acct', 'merch')), may hold values from 0 to 31
- block_rel: int32 [1024], P(('acct', 'merch')), may hold values from 0 to 3
- block_count: int32 [1024], P(('acct', 'merch')), may hold values from 32 to 128, as said below
Outputs:
- merch_out: bfloat16 [1024, 512], P(('acct', 'merch'))
The draws below stay inside these ranges and needn't reach their ends.
Inputs may be any that keep to these rules, and one draw needn't show every extreme that they name: `block_count`: slots at or after a block's count are padding; a count of 128 occurs in every draw.
All inputs are finite; a program needn't handle non-finite values.
Results may differ from the reference program's by a relative error of at most 0.0066.
Values may be sent and summed in bfloat16 or wider, within the bound.
No kernel may reach another device: no remote copies, remote signals or barrier semaphores. Data moves between devices by JAX's collectives and lax.ppermute only.
A program may use at most 192 MiB of HBM per device.

```python
import math
import jax
import jax.numpy as jnp
import numpy as np
from jax import lax

D = 512
RELS = 4
BLOCK = 128
BPD = 1
ACC_DEV = 4096
MER_DEV = 32
ACCTS = 131072
MERCH = 1024
NBLOCKS = 1024
DEVICES = 32


def draw_block_count(key, part):
    key = jax.random.fold_in(key, 11)
    counts = jax.random.randint(key, (NBLOCKS,), BLOCK // 4, BLOCK + 1)
    place = jnp.arange(NBLOCKS) % 8
    counts = jnp.where(place == 0, BLOCK, counts)
    counts = jnp.where(place == 5, BLOCK // 4, counts)
    return counts.astype(jnp.int32)


def with_ends(values, key, low, largest):
    longest = values.shape.index(max(values.shape))
    spots = []
    for shift in (0, 1):
        where = [jax.random.randint(jax.random.fold_in(key, axis), (), 0, length) for axis, length in enumerate(values.shape)]
        where[longest] = (where[longest] + shift) % values.shape[longest]
        spots.append(tuple(where))
    return values.at[spots[0]].set(low).at[spots[1]].set(largest)


def shard_levels(key, shape, shards, smallest, largest):
    loudness, own = 1.0, jax.random.fold_in(key, 6)
    for axis_at, parts in shards:
        heights = jnp.exp(jax.random.uniform(jax.random.fold_in(own, axis_at), (parts,), jnp.float32, smallest / len(shards), largest / len(shards)))
        loudness = loudness * jnp.repeat(heights, shape[axis_at] // parts).reshape([-1 if axis == axis_at else 1 for axis in range(len(shape))])
    return loudness


def rank_bounds(count, lean):
    loads = [(1 << 20) // math.isqrt(rank ** lean) + 1 for rank in range(1, count + 1)]
    spread = 1 + sum(loads) // (1 << 30)
    return np.cumsum(np.array([max(1, weight // spread) for weight in loads]))


def ranked(stream_key, shape, number_of, slope):
    table = rank_bounds(number_of, slope)
    ticket = jax.random.randint(jax.random.fold_in(stream_key, 1), shape, 0, int(table[number_of - 1]))
    grade = jnp.searchsorted(jnp.asarray(table, jnp.int32), ticket, side="right")
    return jax.random.permutation(jax.random.fold_in(stream_key, 2), number_of)[grade].astype(jnp.int32)


def centred(own_key, shape, scale, limit, split=(), kind=jnp.bfloat16):
    drawn = jax.random.normal(own_key, shape, jnp.float32) * scale
    if len(split) > 0:
        drawn = shard_levels(own_key, shape, split, -0.22, 0.18) * drawn
    return jnp.clip(drawn, min=-limit, max=limit).astype(kind)


def setup_inputs(seed: int = 0) -> dict:
    key_list = jax.random.split(jax.random.key(seed), 13)
    acct_feat = centred(key_list[0], (ACCTS, D), 1.0, 6.0, ((0, 32),))
    merch_feat = centred(key_list[1], (MERCH, D), 1.0, 6.0, ((0, 32),))
    key_weight = centred(key_list[2], (RELS, D, D), D ** -0.5, 0.25)
    msg_weight = centred(key_list[3], (RELS, D, D), D ** -0.5, 0.25)
    query_weight = centred(key_list[4], (D, D), D ** -0.5, 0.25)
    out_weight = centred(key_list[5], (D, D), D ** -0.5, 0.25)
    rel_bias = jnp.clip(jax.random.uniform(key_list[6], (RELS,), jnp.float32, -2.0, 2.0), -2.0, 2.0)
    out_gain = jnp.clip(1.0 + 0.1 * jax.random.normal(key_list[7], (D,), jnp.float32), 0.5, 1.5)
    slot_acct = with_ends(jax.random.randint(key_list[8], (NBLOCKS, BLOCK), 0, ACC_DEV), jax.random.fold_in(key_list[8], 1), 0, ACC_DEV - 1).astype(jnp.int32)
    slot_merch = with_ends(ranked(key_list[9], (NBLOCKS, BLOCK), MER_DEV, 2), jax.random.fold_in(key_list[9], 3), 0, MER_DEV - 1).astype(jnp.int32)
    block_rel = with_ends(jax.random.randint(key_list[10], (NBLOCKS,), 0, RELS), jax.random.fold_in(key_list[10], 1), 0, RELS - 1).astype(jnp.int32)
    block_count = draw_block_count(jax.random.fold_in(key_list[12], 71), 0)
    return {"acct_feat": acct_feat, "merch_feat": merch_feat, "key_weight": key_weight, "msg_weight": msg_weight, "query_weight": query_weight, "out_weight": out_weight, "rel_bias": rel_bias, "out_gain": out_gain, "slot_acct": slot_acct, "slot_merch": slot_merch, "block_rel": block_rel, "block_count": block_count}


def reference(acct_feat, merch_feat, key_weight, msg_weight, query_weight, out_weight, rel_bias, out_gain, slot_acct, slot_merch, block_rel, block_count):
    query = jnp.dot(merch_feat, query_weight, preferred_element_type=jnp.float32).astype(jnp.bfloat16)
    per_device = DEVICES * BPD
    owner = jnp.arange(per_device, dtype=jnp.int32) // BPD
    live_all = (jnp.arange(BLOCK, dtype=jnp.int32)[None, :] < block_count[:, None]).astype(jnp.float32)
    key_f = key_weight.astype(jnp.float32)
    msg_f = msg_weight.astype(jnp.float32)

    def step(total, source):
        feats = lax.dynamic_slice_in_dim(acct_feat, source * ACC_DEV, ACC_DEV, 0).astype(jnp.float32)
        keys = jnp.einsum('ad,rde->rae', feats, key_f).astype(jnp.bfloat16).reshape(RELS * ACC_DEV, D)
        values = jnp.einsum('ad,rde->rae', feats, msg_f).astype(jnp.bfloat16).reshape(RELS * ACC_DEV, D)
        keys = lax.optimization_barrier(keys)
        values = lax.optimization_barrier(values)
        first = source * per_device
        accounts = lax.dynamic_slice_in_dim(slot_acct, first, per_device, 0)
        merchants = lax.dynamic_slice_in_dim(slot_merch, first, per_device, 0)
        relation = lax.dynamic_slice_in_dim(block_rel, first, per_device, 0)
        live = lax.dynamic_slice_in_dim(live_all, first, per_device, 0).reshape(-1)
        rows = (relation[:, None] * ACC_DEV + accounts).reshape(-1)
        target = (owner[:, None] * MER_DEV + merchants).reshape(-1)
        key_e = keys[rows].astype(jnp.float32)
        value_e = values[rows].astype(jnp.float32)
        query_e = query[target].astype(jnp.float32)
        bias = jnp.repeat(rel_bias[relation], BLOCK)
        score = lax.optimization_barrier(jnp.sum(key_e * query_e, axis=-1)) / math.sqrt(D) + bias
        gate = jax.nn.sigmoid(score) * live
        message = (gate[:, None] * value_e).astype(jnp.bfloat16)
        message = lax.optimization_barrier(message).astype(jnp.float32)
        return (total + jax.ops.segment_sum(message, target, MERCH), None)
    total = lax.scan(step, jnp.zeros((MERCH, D), jnp.float32), jnp.arange(DEVICES, dtype=jnp.int32))[0]
    update = merch_feat.astype(jnp.float32) + jnp.dot(total.astype(jnp.bfloat16), out_weight, preferred_element_type=jnp.float32)
    scale = lax.rsqrt(lax.optimization_barrier(jnp.mean(update * update, axis=-1, keepdims=True)) + 1e-06)
    return (update * scale * out_gain).astype(jnp.bfloat16)
```

```python
import functools
import math

import jax
import jax.numpy as jnp
from jax import lax
from jax.experimental import pallas as pl
from jax.experimental.pallas import tpu as pltpu
from jax.sharding import PartitionSpec as P

AXES = ("acct", "merch")
LANES = 128
F32 = jnp.float32
BF16 = jnp.bfloat16


def _dot_nt(a, b):
    return lax.dot_general(a, b, (((1,), (1,)), ((), ())), preferred_element_type=F32)


def project_kernel(
    me_ref, slots_ref, rel_ref, acct_hbm, kw_hbm, mw_hbm, wq_hbm, wo_hbm,
    odd_hbm, even_hbm,
    acct, kw, mw, wq, wo, folded, table, rows0, rows1, out0, out1,
    w_sem, a_sem, o_sem,
):
    accounts, width = acct.shape
    relations = kw.shape[0]
    blocks, block_len = slots_ref.shape
    parts = width // LANES
    chunks = a_sem.shape[0]
    chunk = accounts // chunks
    me = me_ref[0]

    weight_copies = [
        pltpu.make_async_copy(src, dst, w_sem.at[i])
        for i, (src, dst) in enumerate(((kw_hbm, kw), (wq_hbm, wq), (mw_hbm, mw), (wo_hbm, wo)))
    ]
    acct_copies = [
        pltpu.make_async_copy(
            acct_hbm.at[pl.ds(i * chunk, chunk)], acct.at[pl.ds(i * chunk, chunk)], a_sem.at[i]
        )
        for i in range(chunks)
    ]
    for copy in weight_copies + acct_copies:
        copy.start()

    weight_copies[0].wait()
    weight_copies[1].wait()

    @pl.loop(0, relations)
    def _(r):
        folded[r, :, :width] = _dot_nt(kw[r], wq[...]).astype(BF16)

    weight_copies[2].wait()
    weight_copies[3].wait()

    @pl.loop(0, relations)
    def _(r):
        folded[r, :, width:] = jnp.dot(mw[r], wo[...], preferred_element_type=F32).astype(BF16)

    for i in range(chunks):
        acct_copies[i].wait()

        @pl.loop(0, chunk // 16, unroll=4)
        def _(g):
            first = pl.multiple_of(i * chunk + g * 16, 16)
            tile = acct[pl.ds(first, 16), :].astype(F32)
            for c in range(parts):
                table[pl.ds(first * parts + c, 16, stride=parts), :] = tile[
                    :, c * LANES : (c + 1) * LANES
                ]

    def collect(j, rows):
        block = jnp.bitwise_xor(me, j)
        for k in range(block_len):
            first = pl.multiple_of(slots_ref[block, k] * parts, parts)
            rows[k * parts : (k + 1) * parts, :] = table[pl.ds(first, parts), :]

    def multiply(j, rows, out):
        relation = rel_ref[jnp.bitwise_xor(me, j)]
        feats = jnp.concatenate(
            [rows[pl.ds(c, block_len, stride=parts), :].astype(BF16) for c in range(parts)], axis=1
        )
        for n in range(0, 2 * width, 256):
            out[:, n : n + 256] = jnp.dot(
                feats, folded[relation, :, n : n + 256], preferred_element_type=F32
            ).astype(BF16)

    collect(0, rows0)

    @pl.loop(0, blocks // 2)
    def _(i):
        even_copy = pltpu.make_async_copy(out0, even_hbm.at[i], o_sem.at[0])
        odd_copy = pltpu.make_async_copy(out1, odd_hbm.at[i], o_sem.at[1])

        @pl.when(i > 0)
        def _():
            even_copy.wait()
            odd_copy.wait()

        collect(2 * i + 1, rows1)
        multiply(2 * i, rows0, out0)
        even_copy.start()
        collect(jnp.minimum(2 * i + 2, blocks - 1), rows0)
        multiply(2 * i + 1, rows1, out1)
        odd_copy.start()

    pltpu.make_async_copy(out0, even_hbm.at[0], o_sem.at[0]).wait()
    pltpu.make_async_copy(out1, odd_hbm.at[0], o_sem.at[1]).wait()


def project(me, slots, rel, acct, kw, mw, wq, wo):
    blocks, block_len = slots.shape
    accounts, width = acct.shape
    relations = kw.shape[0]
    half = jax.ShapeDtypeStruct((blocks // 2, block_len, 2 * width), BF16)
    smem = pl.BlockSpec(memory_space=pltpu.SMEM)
    hbm = pl.BlockSpec(memory_space=pl.ANY)
    parts = width // LANES
    return pl.pallas_call(
        project_kernel,
        out_shape=(half, half),
        in_specs=[smem] * 3 + [hbm] * 5,
        out_specs=(hbm, hbm),
        scratch_shapes=[
            pltpu.VMEM(acct.shape, BF16),
            pltpu.VMEM(kw.shape, BF16),
            pltpu.VMEM(mw.shape, BF16),
            pltpu.VMEM(wq.shape, BF16),
            pltpu.VMEM(wo.shape, BF16),
            pltpu.VMEM((relations, width, 2 * width), BF16),
            pltpu.VMEM((accounts * parts, LANES), F32),
            pltpu.VMEM((block_len * parts, LANES), F32),
            pltpu.VMEM((block_len * parts, LANES), F32),
            pltpu.VMEM((block_len, 2 * width), BF16),
            pltpu.VMEM((block_len, 2 * width), BF16),
            pltpu.SemaphoreType.DMA((4,)),
            pltpu.SemaphoreType.DMA((8,)),
            pltpu.SemaphoreType.DMA((2,)),
        ],
        compiler_params=pltpu.CompilerParams(vmem_limit_bytes=32 * 2**20),
        cost_estimate=pl.CostEstimate(
            flops=2 * blocks * block_len * width * 2 * width + 4 * relations * width**3,
            bytes_accessed=20 * 2**20,
            transcendentals=0,
        ),
        name="project_slots",
    )(me, slots, rel, acct, kw, mw, wq, wo)


def aggregate_kernel(shift, combine, me_ref, rel_ref, count_ref, bias_ref, merch_slot, pairs, *refs):
    groups, block_len, twice = pairs.shape
    width = twice // 2
    feats, refs = refs[:groups], refs[groups:]
    me = me_ref[0]
    merchants = feats[0].shape[0]
    row = lax.broadcasted_iota(jnp.int32, (merchants, block_len), 0)
    lane = lax.broadcasted_iota(jnp.int32, (merchants, block_len), 1)
    for i in range(groups):
        block = jnp.bitwise_xor(me, 2 * i + shift)
        score = _dot_nt(feats[i][...], pairs[i, :, :width]) / math.sqrt(width)
        score = score + bias_ref[rel_ref[block]]
        mine = (merch_slot[pl.ds(block, 1), :] == row) & (lane < count_ref[block])
        gate = jnp.where(mine, jax.nn.sigmoid(score), 0.0).astype(BF16)
        total = jnp.dot(gate, pairs[i, :, width:], preferred_element_type=F32)
        if combine:
            refs[1 + i][...] = (total + refs[0][i].astype(F32)).astype(BF16)
        else:
            refs[0][i] = total.astype(BF16)


def aggregate(shift, me, rel, count, bias, merch_slot, pairs, feats, other=None):
    groups, block_len, twice = pairs.shape
    width = twice // 2
    merchants = feats[0].shape[0]
    smem = pl.BlockSpec(memory_space=pltpu.SMEM)
    vmem = pl.BlockSpec(memory_space=pltpu.VMEM)
    if other is None:
        out_shape = jax.ShapeDtypeStruct((groups, merchants, width), BF16)
        extra = ()
    else:
        out_shape = tuple(jax.ShapeDtypeStruct((merchants, width), BF16) for _ in range(groups))
        extra = (other,)
    return pl.pallas_call(
        functools.partial(aggregate_kernel, shift, other is not None),
        out_shape=out_shape,
        in_specs=[smem] * 4 + [vmem] * (2 + groups + len(extra)),
        out_specs=vmem if other is None else (vmem,) * groups,
        compiler_params=pltpu.CompilerParams(vmem_limit_bytes=24 * 2**20),
        cost_estimate=pl.CostEstimate(
            flops=4 * groups * merchants * block_len * width,
            bytes_accessed=groups * (block_len * twice + 2 * merchants * width) * 2,
            transcendentals=groups * merchants * block_len,
        ),
        name="aggregate_odd" if shift else "aggregate_even",
    )(me, rel, count, bias, merch_slot, pairs, *feats, *extra)


def finish_kernel(feat, gain, *refs):
    update = feat[...].astype(F32)
    for part in refs[:-1]:
        update = update + part[...].astype(F32)
    scale = lax.rsqrt(jnp.mean(update * update, axis=-1, keepdims=True) + 1e-06)
    refs[-1][...] = (update * scale * gain[...]).astype(BF16)


def finish(feat, gain, partials):
    vmem = pl.BlockSpec(memory_space=pltpu.VMEM)
    return pl.pallas_call(
        finish_kernel,
        out_shape=jax.ShapeDtypeStruct(feat.shape, BF16),
        in_specs=[vmem] * (2 + len(partials)),
        out_specs=vmem,
        name="finish",
    )(feat, gain.reshape(1, -1), *partials)


def per_device(
    acct_feat,
    merch_feat,
    key_weight,
    msg_weight,
    query_weight,
    out_weight,
    rel_bias,
    out_gain,
    slot_acct,
    slot_merch,
    block_rel,
    block_count,
):
    devices = lax.axis_size(AXES)
    me = lax.axis_index(AXES).astype(jnp.int32).reshape(1)

    def swap(value, mask):
        return lax.ppermute(value, AXES, [(s, s ^ mask) for s in range(devices)])

    half = devices // 2
    odd_feats = [swap(merch_feat, 2 * i + 1) for i in range(half)]
    even_feats = [merch_feat] + [swap(odd_feats[i], 1) for i in range(1, half)]
    odd_pairs, even_pairs = project(
        me, slot_acct, block_rel, acct_feat, key_weight, msg_weight, query_weight, out_weight
    )
    odd_sums = aggregate(1, me, block_rel, block_count, rel_bias, slot_merch, odd_pairs, odd_feats)
    other = swap(odd_sums, 1)
    sums = aggregate(
        0, me, block_rel, block_count, rel_bias, slot_merch, even_pairs, even_feats, other
    )
    partials = [sums[0]] + [swap(sums[i], 2 * i) for i in range(1, half)]
    return finish(merch_feat, out_gain, partials)


def solution(mesh):
    placed = (
        P(("acct", "merch"), None),
        P(("acct", "merch"), None),
        P(),
        P(),
        P(),
        P(),
        P(),
        P(),
        P(("acct", "merch"), None),
        P(("acct", "merch"), None),
        P(("acct", "merch")),
        P(("acct", "merch")),
    )
    return jax.shard_map(
        per_device,
        mesh=mesh,
        in_specs=placed,
        out_specs=P(("acct", "merch"), None),
        check_vma=False,
    )
```

```python
import functools
import math

import jax
import jax.numpy as jnp
from jax import lax
from jax.experimental import pallas as pl
from jax.experimental.pallas import tpu as pltpu
from jax.sharding import PartitionSpec as P

AXES = ("acct", "merch")
LANES = 128
F32 = jnp.float32
BF16 = jnp.bfloat16
SMEM = pl.BlockSpec(memory_space=pltpu.SMEM)
VMEM = pl.BlockSpec(memory_space=pltpu.VMEM)


def _mb(n):
    return pltpu.CompilerParams(vmem_limit_bytes=n * 2**20)


def _cost(flops, bytes_accessed, transcendentals=0):
    return pl.CostEstimate(
        flops=int(flops), bytes_accessed=int(bytes_accessed), transcendentals=transcendentals
    )


def _offset(i, masks):
    out = 0
    for bit, mask in enumerate(masks):
        out = out + ((i >> bit) & 1) * mask
    return out


def table_kernel(acct, table):
    accounts, width = acct.shape
    parts = width // LANES

    @pl.loop(0, accounts // 16, unroll=4)
    def _(g):
        first = pl.multiple_of(g * 16, 16)
        tile = acct[pl.ds(first, 16), :].astype(F32)
        for c in range(parts):
            table[pl.ds(first * parts + c, 16, stride=parts), :] = tile[
                :, c * LANES : (c + 1) * LANES
            ]


def make_table(acct):
    accounts, width = acct.shape
    return pl.pallas_call(
        table_kernel,
        out_shape=jax.ShapeDtypeStruct((accounts * width // LANES, LANES), F32),
        in_specs=[VMEM],
        out_specs=VMEM,
        compiler_params=_mb(2),
        cost_estimate=_cost(0, 8 * 2**20),
        name="make_table",
    )(acct)


def gather_kernel(masks, shift, me_ref, slots_ref, table, out, rows0, rows1):
    blocks, block_len, width = out.shape
    parts = width // LANES
    me = me_ref[0]

    def collect(i, rows):
        block = jnp.bitwise_xor(me, _offset(i, masks) + shift)
        for k in range(block_len):
            first = pl.multiple_of(slots_ref[block, k] * parts, parts)
            rows[k * parts : (k + 1) * parts, :] = table[pl.ds(first, parts), :]

    def emit(i, rows):
        for c in range(parts):
            out[i, :, c * LANES : (c + 1) * LANES] = rows[
                pl.ds(c, block_len, stride=parts), :
            ].astype(BF16)

    @pl.loop(0, blocks // 2)
    def _(h):
        collect(2 * h, rows0)
        collect(2 * h + 1, rows1)
        emit(2 * h, rows0)
        emit(2 * h + 1, rows1)


def gather(masks, shift, me, slots, table, width):
    blocks, block_len = slots.shape
    rows = pltpu.VMEM((block_len * width // LANES, LANES), F32)
    return pl.pallas_call(
        functools.partial(gather_kernel, masks, shift),
        out_shape=jax.ShapeDtypeStruct((blocks // 2, block_len, width), BF16),
        in_specs=[SMEM, SMEM, VMEM],
        out_specs=VMEM,
        scratch_shapes=[rows, rows],
        compiler_params=_mb(2),
        cost_estimate=_cost(0, 8 * 2**20),
        name="gather_odd" if shift else "gather_even",
    )(me, slots, table)


def project_kernel(masks, shift, me_ref, rel_ref, feats, kw, mw, keys, values):
    blocks = feats.shape[0]
    width = feats.shape[2]
    half = width // 2
    me = me_ref[0]

    @pl.loop(0, blocks)
    def _(i):
        relation = rel_ref[jnp.bitwise_xor(me, _offset(i, masks) + shift)]
        for n in range(0, width, half):
            key = jnp.dot(feats[i], kw[relation, :, n : n + half], preferred_element_type=F32)
            keys[i, n : n + half, :] = key.T.astype(BF16)
            value = jnp.dot(feats[i], mw[relation, :, n : n + half], preferred_element_type=F32)
            values[i, :, n : n + half] = value.astype(BF16)


def project(masks, shift, me, rel, feats, kw, mw):
    blocks, block_len, width = feats.shape
    return pl.pallas_call(
        functools.partial(project_kernel, masks, shift),
        out_shape=(
            jax.ShapeDtypeStruct((blocks, width, block_len), BF16),
            jax.ShapeDtypeStruct((blocks, block_len, width), BF16),
        ),
        in_specs=[SMEM, SMEM, VMEM, VMEM, VMEM],
        out_specs=(VMEM, VMEM),
        compiler_params=_mb(4),
        cost_estimate=_cost(4 * blocks * block_len * width * width, 12 * 2**20),
        name="project_odd" if shift else "project_even",
    )(me, rel, feats, kw, mw)


def aggregate_kernel(
    masks, shift, me_ref, rel_ref, count_ref, bias_ref, merch_slot, feats, wq, keys, values,
    sums, query, gates,
):
    blocks, width, block_len = keys.shape
    merchants = feats.shape[0] // blocks
    me = me_ref[0]
    row = lax.broadcasted_iota(jnp.int32, (merchants, block_len), 0)
    lane = lax.broadcasted_iota(jnp.int32, (merchants, block_len), 1)
    query[...] = jnp.dot(feats[...], wq[...], preferred_element_type=F32).astype(BF16)
    for i in range(blocks):
        block = jnp.bitwise_xor(me, _offset(i, masks) + shift)
        score = jnp.dot(
            query[i * merchants : (i + 1) * merchants, :], keys[i], preferred_element_type=F32
        ) / math.sqrt(width)
        score = score + bias_ref[rel_ref[block]]
        mine = (merch_slot[pl.ds(block, 1), :] == row) & (lane < count_ref[block])
        gates[i * merchants : (i + 1) * merchants, :] = jnp.where(
            mine, jax.nn.sigmoid(score), 0.0
        ).astype(BF16)
    for i in range(blocks):
        sums[i * merchants : (i + 1) * merchants, :] = jnp.dot(
            gates[i * merchants : (i + 1) * merchants, :], values[i], preferred_element_type=F32
        ).astype(sums.dtype)


def aggregate(masks, shift, me, rel, count, bias, merch_slot, feats, wq, keys, values, dtype):
    blocks, width, block_len = keys.shape
    merchants = feats.shape[0] // blocks
    return pl.pallas_call(
        functools.partial(aggregate_kernel, masks, shift),
        out_shape=jax.ShapeDtypeStruct(feats.shape, dtype),
        in_specs=[SMEM] * 4 + [VMEM] * 5,
        out_specs=VMEM,
        scratch_shapes=[
            pltpu.VMEM(feats.shape, BF16),
            pltpu.VMEM((feats.shape[0], block_len), BF16),
        ],
        compiler_params=_mb(6),
        cost_estimate=_cost(
            4 * blocks * merchants * block_len * width + 2 * feats.shape[0] * width * width,
            6 * 2**20,
            blocks * merchants * block_len,
        ),
        name="aggregate_odd" if shift else "aggregate_even",
    )(me, rel, count, bias, merch_slot, feats, wq, keys, values)


def combine_kernel(masks, me_ref, mine, other, out):
    rows = out.shape[0]
    blocks = 2 ** len(masks)
    merchants = rows // blocks
    me = me_ref[0]
    for i in range(blocks):
        place = jnp.bitwise_xor(me, _offset(i, masks)) >> 1
        first = pl.multiple_of(place * merchants, merchants)
        part = slice(i * merchants, (i + 1) * merchants)
        out[pl.ds(first, merchants), :] = (mine[part, :] + other[part, :].astype(F32)).astype(BF16)


def combine(masks, me, mine, other):
    return pl.pallas_call(
        functools.partial(combine_kernel, masks),
        out_shape=jax.ShapeDtypeStruct(other.shape, BF16),
        in_specs=[SMEM, VMEM, VMEM],
        out_specs=VMEM,
        compiler_params=_mb(2),
        cost_estimate=_cost(0, 2 * 2**20),
        name="combine",
    )(me, mine, other)


def finish_kernel(feat, gain, wo, parts, out):
    merchants = feat.shape[0]
    total = parts[:merchants, :].astype(F32)
    for i in range(1, parts.shape[0] // merchants):
        total = total + parts[i * merchants : (i + 1) * merchants, :].astype(F32)
    update = feat[...].astype(F32) + jnp.dot(
        total.astype(BF16), wo[...], preferred_element_type=F32
    )
    scale = lax.rsqrt(jnp.mean(update * update, axis=-1, keepdims=True) + 1e-06)
    out[...] = (update * scale * gain[...]).astype(BF16)


def finish(feat, gain, wo, parts):
    return pl.pallas_call(
        finish_kernel,
        out_shape=jax.ShapeDtypeStruct(feat.shape, BF16),
        in_specs=[VMEM] * 4,
        out_specs=VMEM,
        compiler_params=_mb(2),
        name="finish",
    )(feat, gain.reshape(1, -1), wo, parts)


def per_device(
    acct_feat,
    merch_feat,
    key_weight,
    msg_weight,
    query_weight,
    out_weight,
    rel_bias,
    out_gain,
    slot_acct,
    slot_merch,
    block_rel,
    block_count,
):
    devices = lax.axis_size(AXES)
    me = lax.axis_index(AXES).astype(jnp.int32).reshape(1)
    width = acct_feat.shape[1]
    masks = []
    while devices >> (len(masks) + 1) > 1:
        masks.append(devices >> (len(masks) + 1))

    def swap(value, mask):
        return lax.ppermute(value, AXES, [(s, s ^ mask) for s in range(devices)])

    def after(value, *others):
        return lax.optimization_barrier((value,) + others)[0]

    feats = jnp.concatenate([swap(merch_feat, 1), swap(merch_feat, masks[0] + 1)], axis=0)
    table = make_table(acct_feat)
    feats = after(feats, table)
    feats = jnp.concatenate([feats, swap(feats, masks[1])], axis=0)
    odd_rows = gather(masks, 1, me, slot_acct, table, width)
    feats = after(feats, odd_rows)
    feats = jnp.concatenate([feats, swap(feats, masks[2])], axis=0)
    even_rows = gather(masks, 0, me, slot_acct, table, width)
    feats = after(feats, even_rows)
    for mask in masks[3:]:
        feats = jnp.concatenate([feats, swap(feats, mask)], axis=0)
    odd_keys, odd_values = project(masks, 1, me, block_rel, odd_rows, key_weight, msg_weight)
    even_keys, even_values = project(masks, 0, me, block_rel, even_rows, key_weight, msg_weight)
    feats = after(feats, even_keys)

    shared = (me, block_rel, block_count, rel_bias, slot_merch)
    even_feats = swap(feats, 1)
    odd_sums = aggregate(masks, 1, *shared, feats, query_weight, odd_keys, odd_values, BF16)
    other = swap(odd_sums, 1)
    even_sums = aggregate(masks, 0, *shared, even_feats, query_weight, even_keys, even_values, F32)
    parts = combine(masks, me, even_sums, other)
    groups = [[s for s in range(devices) if s % 2 == core] for core in range(2)]
    parts = lax.all_to_all(
        parts, AXES, split_axis=0, concat_axis=0, tiled=True, axis_index_groups=groups
    )
    return finish(merch_feat, out_gain, out_weight, parts)


def solution(mesh):
    placed = (
        P(("acct", "merch"), None),
        P(("acct", "merch"), None),
        P(),
        P(),
        P(),
        P(),
        P(),
        P(),
        P(("acct", "merch"), None),
        P(("acct", "merch"), None),
        P(("acct", "merch")),
        P(("acct", "merch")),
    )
    return jax.shard_map(
        per_device,
        mesh=mesh,
        in_specs=placed,
        out_specs=P(("acct", "merch"), None),
        check_vma=False,
    )
```

```python
import functools
import math

import jax
import jax.numpy as jnp
from jax import lax
from jax.experimental import pallas as pl
from jax.experimental.pallas import tpu as pltpu
from jax.sharding import PartitionSpec as P

AXES = ("acct", "merch")
LANES = 128
F32 = jnp.float32
BF16 = jnp.bfloat16
SMEM = pl.BlockSpec(memory_space=pltpu.SMEM)
VMEM = pl.BlockSpec(memory_space=pltpu.VMEM)


def _mb(n):
    return pltpu.CompilerParams(vmem_limit_bytes=n * 2**20)


def _cost(flops, bytes_accessed, transcendentals=0):
    return pl.CostEstimate(
        flops=int(flops), bytes_accessed=int(bytes_accessed), transcendentals=transcendentals
    )


def _offset(i, outer):
    return (i // outer) * 2 + (i % outer) * 8


def gather_kernel(outer, me_ref, slots_ref, acct, odd, even, table, rows0, rows1):
    accounts, width = acct.shape
    blocks, block_len, _ = odd.shape
    parts = width // LANES
    pitch = table.shape[1]
    flat = table.reshape(accounts * pitch, LANES)
    me = me_ref[0]

    @pl.loop(0, accounts // 16, unroll=4)
    def _(g):
        first = pl.multiple_of(g * 16, 16)
        tile = acct[pl.ds(first, 16), :].astype(F32)
        for c in range(parts):
            flat[pl.ds(first * pitch + c, 16, stride=pitch), :] = tile[
                :, c * LANES : (c + 1) * LANES
            ]

    def collect(block, rows):
        for k in range(block_len):
            rows[k * parts : (k + 1) * parts, :] = table[slots_ref[block, k], :parts, :]

    def emit(i, rows, out):
        for c in range(parts):
            out[i, :, c * LANES : (c + 1) * LANES] = rows[
                pl.ds(c, block_len, stride=parts), :
            ].astype(BF16)

    @pl.loop(0, blocks)
    def _(i):
        offset = _offset(i, outer)
        collect(jnp.bitwise_xor(me, offset + 1), rows0)
        collect(jnp.bitwise_xor(me, offset), rows1)
        emit(i, rows0, odd)
        emit(i, rows1, even)


def gather(outer, me, slots, acct):
    blocks, block_len = slots.shape
    accounts, width = acct.shape
    parts = width // LANES
    rows = pltpu.VMEM((block_len * parts, LANES), F32)
    half = jax.ShapeDtypeStruct((blocks // 2, block_len, width), BF16)
    return pl.pallas_call(
        functools.partial(gather_kernel, outer),
        out_shape=(half, half),
        in_specs=[SMEM, SMEM, VMEM],
        out_specs=(VMEM, VMEM),
        scratch_shapes=[pltpu.VMEM((accounts, -(-parts // 8) * 8, LANES), F32), rows, rows],
        compiler_params=_mb(20),
        cost_estimate=_cost(0, 20 * 2**20),
        name="gather_slots",
    )(me, slots, acct)


def project_kernel(outer, shifts, me_ref, rel_ref, kw, mw, *refs):
    halves = len(shifts)
    blocks, _, width = refs[0].shape
    half = width // 2
    me = me_ref[0]

    def one(i, shift, feats, keys, values):
        relation = rel_ref[jnp.bitwise_xor(me, _offset(i, outer) + shift)]
        for n in range(0, width, half):
            key = jnp.dot(feats[i], kw[relation, :, n : n + half], preferred_element_type=F32)
            keys[i, n : n + half, :] = key.astype(BF16).T
            value = jnp.dot(feats[i], mw[relation, :, n : n + half], preferred_element_type=F32)
            values[i, :, n : n + half] = value.astype(BF16)

    @pl.loop(0, blocks, unroll=2)
    def _(i):
        for h, shift in enumerate(shifts):
            one(i, shift, refs[h], refs[halves + 2 * h], refs[halves + 2 * h + 1])


def project(outer, shifts, me, rel, feats, kw, mw):
    blocks, block_len, width = feats[0].shape
    keys = jax.ShapeDtypeStruct((blocks, width, block_len), BF16)
    values = jax.ShapeDtypeStruct((blocks, block_len, width), BF16)
    return pl.pallas_call(
        functools.partial(project_kernel, outer, shifts),
        out_shape=(keys, values) * len(shifts),
        in_specs=[SMEM, SMEM] + [VMEM] * (2 + len(shifts)),
        out_specs=(VMEM, VMEM) * len(shifts),
        compiler_params=_mb(4),
        cost_estimate=_cost(
            4 * len(shifts) * blocks * block_len * width * width, 8 * len(shifts) * 2**20
        ),
        name="project_slots",
    )(me, rel, kw, mw, *feats)


def aggregate_kernel(
    outer, shift, me_ref, rel_ref, count_ref, bias_ref, merch_slot, feats, wq, keys, values,
    sums, query, gates,
):
    blocks, width, block_len = keys.shape
    merchants = feats.shape[0] // blocks
    me = me_ref[0]
    row = lax.broadcasted_iota(jnp.int32, (merchants, block_len), 0)
    lane = lax.broadcasted_iota(jnp.int32, (merchants, block_len), 1)
    query[...] = jnp.dot(feats[...], wq[...], preferred_element_type=F32).astype(BF16)
    for i in range(blocks):
        block = jnp.bitwise_xor(me, _offset(i, outer) + shift)
        score = jnp.dot(
            query[i * merchants : (i + 1) * merchants, :], keys[i], preferred_element_type=F32
        ) / math.sqrt(width)
        score = score + bias_ref[rel_ref[block]]
        mine = (merch_slot[pl.ds(block, 1), :] == row) & (lane < count_ref[block])
        gates[i * merchants : (i + 1) * merchants, :] = jnp.where(
            mine, jax.nn.sigmoid(score), 0.0
        ).astype(BF16)
    for i in range(blocks):
        sums[i * merchants : (i + 1) * merchants, :] = jnp.dot(
            gates[i * merchants : (i + 1) * merchants, :], values[i], preferred_element_type=F32
        ).astype(sums.dtype)


def aggregate(outer, shift, me, rel, count, bias, merch_slot, feats, wq, keys, values, dtype):
    blocks, width, block_len = keys.shape
    merchants = feats.shape[0] // blocks
    return pl.pallas_call(
        functools.partial(aggregate_kernel, outer, shift),
        out_shape=jax.ShapeDtypeStruct(feats.shape, dtype),
        in_specs=[SMEM] * 4 + [VMEM] * 5,
        out_specs=VMEM,
        scratch_shapes=[
            pltpu.VMEM(feats.shape, BF16),
            pltpu.VMEM((feats.shape[0], block_len), BF16),
        ],
        compiler_params=_mb(6),
        cost_estimate=_cost(
            4 * blocks * merchants * block_len * width + 2 * feats.shape[0] * width * width,
            6 * 2**20,
            blocks * merchants * block_len,
        ),
        name="aggregate_odd" if shift else "aggregate_even",
    )(me, rel, count, bias, merch_slot, feats, wq, keys, values)


def combine_kernel(mine, other, *outs):
    rows = outs[0].shape[0]
    for j, out in enumerate(outs):
        part = slice(j * rows, (j + 1) * rows)
        out[...] = (mine[part, :] + other[part, :].astype(F32)).astype(out.dtype)


def combine(inner, mine, other):
    rows, width = mine.shape
    return pl.pallas_call(
        combine_kernel,
        out_shape=tuple(
            jax.ShapeDtypeStruct((rows // inner, width), F32 if j == 0 else BF16)
            for j in range(inner)
        ),
        in_specs=[VMEM, VMEM],
        out_specs=(VMEM,) * inner,
        compiler_params=_mb(2),
        cost_estimate=_cost(0, 2 * 2**20),
        name="combine_cores",
    )(mine, other)


def plane_kernel(inner, *refs):
    ins, outs = refs[:inner], refs[inner:]
    rows = outs[0].shape[0]
    for k, out in enumerate(outs):
        part = slice(k * rows, (k + 1) * rows)
        total = ins[0][part, :]
        for other in ins[1:]:
            total = total + other[part, :].astype(F32)
        out[...] = total.astype(out.dtype)


def combine_plane(outer, parts):
    rows, width = parts[0].shape
    return pl.pallas_call(
        functools.partial(plane_kernel, len(parts)),
        out_shape=tuple(
            jax.ShapeDtypeStruct((rows // outer, width), F32 if k == 0 else BF16)
            for k in range(outer)
        ),
        in_specs=[VMEM] * len(parts),
        out_specs=(VMEM,) * outer,
        compiler_params=_mb(2),
        cost_estimate=_cost(0, 2**20),
        name="combine_plane",
    )(*parts)


def finish_kernel(feat, gain, wo, *refs):
    out = refs[-1]
    total = refs[0][...]
    for part in refs[1:-1]:
        total = total + part[...].astype(F32)
    update = feat[...].astype(F32) + jnp.dot(
        total.astype(BF16), wo[...], preferred_element_type=F32
    )
    scale = lax.rsqrt(jnp.mean(update * update, axis=-1, keepdims=True) + 1e-06)
    out[...] = (update * scale * gain[...]).astype(BF16)


def finish(feat, gain, wo, parts):
    return pl.pallas_call(
        finish_kernel,
        out_shape=jax.ShapeDtypeStruct(feat.shape, BF16),
        in_specs=[VMEM] * (3 + len(parts)),
        out_specs=VMEM,
        compiler_params=_mb(2),
        name="finish",
    )(feat, gain.reshape(1, -1), wo, *parts)


def per_device(
    acct_feat,
    merch_feat,
    key_weight,
    msg_weight,
    query_weight,
    out_weight,
    rel_bias,
    out_gain,
    slot_acct,
    slot_merch,
    block_rel,
    block_count,
):
    devices = lax.axis_size(AXES)
    me = lax.axis_index(AXES).astype(jnp.int32).reshape(1)
    inner = 4
    outer = devices // (2 * inner)

    def swap(value, mask):
        return lax.ppermute(value, AXES, [(s, s ^ mask) for s in range(devices)])

    def after(value, *others):
        return lax.optimization_barrier((value,) + others)[0]

    feats = jnp.concatenate([swap(merch_feat, 8 * k + 1) for k in range(outer)], axis=0)
    odd_rows, even_rows = gather(outer, me, slot_acct, acct_feat)
    feats = after(feats, odd_rows)
    feats = jnp.concatenate([feats] + [swap(feats, 2 * j) for j in range(1, inner)], axis=0)
    rows = (odd_rows, even_rows)
    weights = (key_weight, msg_weight)
    if devices <= 32:
        projected = project(outer, (1, 0), me, block_rel, rows, *weights)
    else:
        projected = [
            out
            for shift, feat in zip((1, 0), rows)
            for out in project(outer, (shift,), me, block_rel, (feat,), *weights)
        ]
    odd_keys, odd_values, even_keys, even_values = projected
    feats = after(feats, even_keys)

    shared = (me, block_rel, block_count, rel_bias, slot_merch)
    even_feats = swap(feats, 1)
    odd_sums = aggregate(outer, 1, *shared, feats, query_weight, odd_keys, odd_values, BF16)
    other = swap(odd_sums, 1)
    even_sums = aggregate(outer, 0, *shared, even_feats, query_weight, even_keys, even_values, F32)
    parts = combine(inner, even_sums, other)
    parts = combine_plane(
        outer, [parts[0]] + [swap(parts[j], 2 * j) for j in reversed(range(1, inner))]
    )
    parts = [parts[0]] + [swap(parts[k], 8 * k) for k in reversed(range(1, outer))]
    return finish(merch_feat, out_gain, out_weight, parts)


def solution(mesh):
    placed = (
        P(("acct", "merch"), None),
        P(("acct", "merch"), None),
        P(),
        P(),
        P(),
        P(),
        P(),
        P(),
        P(("acct", "merch"), None),
        P(("acct", "merch"), None),
        P(("acct", "merch")),
        P(("acct", "merch")),
    )
    return jax.shard_map(
        per_device,
        mesh=mesh,
        in_specs=placed,
        out_specs=P(("acct", "merch"), None),
        check_vma=False,
    )
```

```python
import functools
import math

import jax
import jax.numpy as jnp
from jax import lax
from jax.experimental import pallas as pl
from jax.experimental.pallas import tpu as pltpu
from jax.sharding import PartitionSpec as P

AXES = ("acct", "merch")
LANES = 128
F32 = jnp.float32
BF16 = jnp.bfloat16
SMEM = pl.BlockSpec(memory_space=pltpu.SMEM)
ANY = pl.BlockSpec(memory_space=pl.ANY)
VMEM = pl.BlockSpec(memory_space=pltpu.VMEM)


def _mb(n):
    return pltpu.CompilerParams(vmem_limit_bytes=n * 2**20)


def _cost(flops, bytes_accessed, transcendentals=0):
    return pl.CostEstimate(
        flops=int(flops), bytes_accessed=int(bytes_accessed), transcendentals=transcendentals
    )


def _offset(i, outer):
    return (i // outer) * 2 + (i % outer) * 8


def _project(feats, relation, kw, mw, i, keys, values):
    width = feats.shape[1]
    half = width // 2
    for n in range(0, width, half):
        key = jnp.dot(feats[...], kw[relation, :, n : n + half], preferred_element_type=F32)
        keys[i, n : n + half, :] = key.astype(BF16).T
        value = jnp.dot(feats[...], mw[relation, :, n : n + half], preferred_element_type=F32)
        values[i, :, n : n + half] = value.astype(BF16)


def gather_kernel(
    outer, me_ref, rel_ref, slots_ref, acct_hbm, kw_hbm, mw_hbm,
    keys, values, even,
    kw, mw, acct, table, odd_rows, even_rows, odd_feats, a_sem, w_sem,
):
    accounts, width = acct.shape
    blocks, block_len, _ = even.shape
    parts = width // LANES
    pitch = table.shape[1]
    flat = table.reshape(accounts * pitch, LANES)
    me = me_ref[0]
    chunks = a_sem.shape[0]
    chunk = accounts // chunks
    acct_copies = [
        pltpu.make_async_copy(
            acct_hbm.at[pl.ds(i * chunk, chunk)], acct.at[pl.ds(i * chunk, chunk)], a_sem.at[i]
        )
        for i in range(chunks)
    ]
    weight_copies = [
        pltpu.make_async_copy(kw_hbm, kw, w_sem.at[0]),
        pltpu.make_async_copy(mw_hbm, mw, w_sem.at[1]),
    ]
    for copy in acct_copies + weight_copies:
        copy.start()
    for i in range(chunks):
        acct_copies[i].wait()

        @pl.loop(0, chunk // 16, unroll=4)
        def _(g):
            first = pl.multiple_of(i * chunk + g * 16, 16)
            tile = acct[pl.ds(first, 16), :].astype(F32)
            for c in range(parts):
                flat[pl.ds(first * pitch + c, 16, stride=pitch), :] = tile[
                    :, c * LANES : (c + 1) * LANES
                ]

    def collect(block, rows):
        for k in range(0, block_len, 16):
            found = [table[slots_ref[block, k + u], :parts, :] for u in range(16)]
            for u in range(16):
                rows[(k + u) * parts : (k + u + 1) * parts, :] = found[u]

    def emit(rows, out):
        for c in range(parts):
            out[:, c * LANES : (c + 1) * LANES] = rows[
                pl.ds(c, block_len, stride=parts), :
            ].astype(BF16)

    collect(jnp.bitwise_xor(me, 1), odd_rows)
    for copy in weight_copies:
        copy.wait()

    @pl.loop(0, blocks)
    def _(i):
        emit(odd_rows, odd_feats)
        ahead = _offset(jnp.minimum(i + 1, blocks - 1), outer) + 1
        collect(jnp.bitwise_xor(me, ahead), odd_rows)
        offset = _offset(i, outer)
        collect(jnp.bitwise_xor(me, offset), even_rows)
        relation = rel_ref[jnp.bitwise_xor(me, offset + 1)]
        _project(odd_feats, relation, kw, mw, i, keys, values)
        emit(even_rows, even.at[i])


def gather(outer, me, rel, slots, acct, kw, mw):
    blocks, block_len = slots.shape
    accounts, width = acct.shape
    parts = width // LANES
    rows = pltpu.VMEM((block_len * parts, LANES), F32)
    half = blocks // 2
    return pl.pallas_call(
        functools.partial(gather_kernel, outer),
        out_shape=(
            jax.ShapeDtypeStruct((half, width, block_len), BF16),
            jax.ShapeDtypeStruct((half, block_len, width), BF16),
            jax.ShapeDtypeStruct((half, block_len, width), BF16),
        ),
        in_specs=[SMEM] * 3 + [ANY] * 3,
        out_specs=(VMEM,) * 3,
        scratch_shapes=[
            pltpu.VMEM(kw.shape, BF16),
            pltpu.VMEM(mw.shape, BF16),
            pltpu.VMEM(acct.shape, BF16),
            pltpu.VMEM((accounts, -(-parts // 8) * 8, LANES), F32),
            rows,
            rows,
            pltpu.VMEM((block_len, width), BF16),
            pltpu.SemaphoreType.DMA((8,)),
            pltpu.SemaphoreType.DMA((2,)),
        ],
        compiler_params=_mb(47 if blocks <= 32 else 50),
        cost_estimate=_cost(4 * half * block_len * width * width, 20 * 2**20),
        name="gather_slots",
    )(me, rel, slots, acct, kw, mw)


def project_kernel(outer, me_ref, rel_ref, feats, kw, mw, keys, values):
    blocks = feats.shape[0]
    me = me_ref[0]

    @pl.loop(0, blocks, unroll=4)
    def _(i):
        relation = rel_ref[jnp.bitwise_xor(me, _offset(i, outer))]
        _project(feats.at[i], relation, kw, mw, i, keys, values)


def project(outer, me, rel, feats, kw, mw):
    blocks, block_len, width = feats.shape
    return pl.pallas_call(
        functools.partial(project_kernel, outer),
        out_shape=(
            jax.ShapeDtypeStruct((blocks, width, block_len), BF16),
            jax.ShapeDtypeStruct((blocks, block_len, width), BF16),
        ),
        in_specs=[SMEM, SMEM] + [VMEM] * 3,
        out_specs=(VMEM, VMEM),
        compiler_params=_mb(4),
        cost_estimate=_cost(4 * blocks * block_len * width * width, 8 * 2**20),
        name="project_even",
    )(me, rel, feats, kw, mw)


def aggregate_kernel(
    outer, shift, me_ref, rel_ref, count_ref, bias_ref, merch_slot, feats, wq, keys, values,
    sums, query, gates,
):
    blocks, width, block_len = keys.shape
    merchants = feats.shape[0] // blocks
    me = me_ref[0]
    row = lax.broadcasted_iota(jnp.int32, (merchants, block_len), 0)
    lane = lax.broadcasted_iota(jnp.int32, (merchants, block_len), 1)
    query[...] = jnp.dot(feats[...], wq[...], preferred_element_type=F32).astype(BF16)
    for i in range(blocks):
        block = jnp.bitwise_xor(me, _offset(i, outer) + shift)
        score = jnp.dot(
            query[i * merchants : (i + 1) * merchants, :], keys[i], preferred_element_type=F32
        ) / math.sqrt(width)
        score = score + bias_ref[rel_ref[block]]
        mine = (merch_slot[pl.ds(block, 1), :] == row) & (lane < count_ref[block])
        gates[i * merchants : (i + 1) * merchants, :] = jnp.where(
            mine, jax.nn.sigmoid(score), 0.0
        ).astype(BF16)
    for i in range(blocks):
        sums[i * merchants : (i + 1) * merchants, :] = jnp.dot(
            gates[i * merchants : (i + 1) * merchants, :], values[i], preferred_element_type=F32
        ).astype(sums.dtype)


def aggregate(outer, shift, me, rel, count, bias, merch_slot, feats, wq, keys, values, dtype):
    blocks, width, block_len = keys.shape
    merchants = feats.shape[0] // blocks
    return pl.pallas_call(
        functools.partial(aggregate_kernel, outer, shift),
        out_shape=jax.ShapeDtypeStruct(feats.shape, dtype),
        in_specs=[SMEM] * 4 + [VMEM] * 5,
        out_specs=VMEM,
        scratch_shapes=[
            pltpu.VMEM(feats.shape, BF16),
            pltpu.VMEM((feats.shape[0], block_len), BF16),
        ],
        compiler_params=_mb(6),
        cost_estimate=_cost(
            4 * blocks * merchants * block_len * width + 2 * feats.shape[0] * width * width,
            6 * 2**20,
            blocks * merchants * block_len,
        ),
        name="aggregate_odd" if shift else "aggregate_even",
    )(me, rel, count, bias, merch_slot, feats, wq, keys, values)


def combine_kernel(mine, other, *outs):
    rows = outs[0].shape[0]
    for j, out in enumerate(outs):
        part = slice(j * rows, (j + 1) * rows)
        out[...] = (mine[part, :] + other[part, :].astype(F32)).astype(out.dtype)


def combine(inner, mine, other):
    rows, width = mine.shape
    return pl.pallas_call(
        combine_kernel,
        out_shape=tuple(
            jax.ShapeDtypeStruct((rows // inner, width), F32 if j == 0 else BF16)
            for j in range(inner)
        ),
        in_specs=[VMEM, VMEM],
        out_specs=(VMEM,) * inner,
        compiler_params=_mb(2),
        cost_estimate=_cost(0, 2 * 2**20),
        name="combine_cores",
    )(mine, other)


def plane_kernel(inner, *refs):
    ins, outs = refs[:inner], refs[inner:]
    rows = outs[0].shape[0]
    for k, out in enumerate(outs):
        part = slice(k * rows, (k + 1) * rows)
        total = ins[0][part, :]
        for other in ins[1:]:
            total = total + other[part, :].astype(F32)
        out[...] = total.astype(out.dtype)


def combine_plane(outer, parts):
    rows, width = parts[0].shape
    return pl.pallas_call(
        functools.partial(plane_kernel, len(parts)),
        out_shape=tuple(
            jax.ShapeDtypeStruct((rows // outer, width), F32 if k == 0 else BF16)
            for k in range(outer)
        ),
        in_specs=[VMEM] * len(parts),
        out_specs=(VMEM,) * outer,
        compiler_params=_mb(2),
        cost_estimate=_cost(0, 2**20),
        name="combine_plane",
    )(*parts)


def finish_kernel(feat, gain, wo, *refs):
    out = refs[-1]
    total = refs[0][...]
    for part in refs[1:-1]:
        total = total + part[...].astype(F32)
    update = feat[...].astype(F32) + jnp.dot(
        total.astype(BF16), wo[...], preferred_element_type=F32
    )
    scale = lax.rsqrt(jnp.mean(update * update, axis=-1, keepdims=True) + 1e-06)
    out[...] = (update * scale * gain[...]).astype(BF16)


def finish(feat, gain, wo, parts):
    return pl.pallas_call(
        finish_kernel,
        out_shape=jax.ShapeDtypeStruct(feat.shape, BF16),
        in_specs=[VMEM] * (3 + len(parts)),
        out_specs=VMEM,
        compiler_params=_mb(2),
        name="finish",
    )(feat, gain.reshape(1, -1), wo, *parts)


def per_device(
    acct_feat,
    merch_feat,
    key_weight,
    msg_weight,
    query_weight,
    out_weight,
    rel_bias,
    out_gain,
    slot_acct,
    slot_merch,
    block_rel,
    block_count,
):
    devices = lax.axis_size(AXES)
    me = lax.axis_index(AXES).astype(jnp.int32).reshape(1)
    inner = 4
    outer = devices // (2 * inner)

    def swap(value, mask):
        return lax.ppermute(value, AXES, [(s, s ^ mask) for s in range(devices)])

    def after(value, *others):
        return lax.optimization_barrier((value,) + others)[0]

    feats = jnp.concatenate([swap(merch_feat, 8 * k + 1) for k in range(outer)], axis=0)
    odd_keys, odd_values, even_rows = gather(
        outer, me, block_rel, slot_acct, acct_feat, key_weight, msg_weight
    )
    feats = after(feats, even_rows)
    feats = jnp.concatenate([feats] + [swap(feats, 2 * j) for j in range(1, inner)], axis=0)
    even_keys, even_values = project(outer, me, block_rel, even_rows, key_weight, msg_weight)
    feats = after(feats, even_keys)

    shared = (me, block_rel, block_count, rel_bias, slot_merch)
    even_feats = swap(feats, 1)
    odd_sums = aggregate(outer, 1, *shared, feats, query_weight, odd_keys, odd_values, BF16)
    other = swap(odd_sums, 1)
    even_sums = aggregate(outer, 0, *shared, even_feats, query_weight, even_keys, even_values, F32)
    parts = combine(inner, even_sums, other)
    parts = combine_plane(
        outer, [parts[0]] + [swap(parts[j], 2 * j) for j in reversed(range(1, inner))]
    )
    parts = [parts[0]] + [swap(parts[k], 8 * k) for k in reversed(range(1, outer))]
    return finish(merch_feat, out_gain, out_weight, parts)


def solution(mesh):
    placed = (
        P(("acct", "merch"), None),
        P(("acct", "merch"), None),
        P(),
        P(),
        P(),
        P(),
        P(),
        P(),
        P(("acct", "merch"), None),
        P(("acct", "merch"), None),
        P(("acct", "merch")),
        P(("acct", "merch")),
    )
    return jax.shard_map(
        per_device,
        mesh=mesh,
        in_specs=placed,
        out_specs=P(("acct", "merch"), None),
        check_vma=False,
    )
```

```python
import functools
import math

import jax
import jax.numpy as jnp
from jax import lax
from jax.experimental import pallas as pl
from jax.experimental.pallas import tpu as pltpu
from jax.sharding import PartitionSpec as P

AXES = ("acct", "merch")
LANES = 128
F32 = jnp.float32
BF16 = jnp.bfloat16
SMEM = pl.BlockSpec(memory_space=pltpu.SMEM)
ANY = pl.BlockSpec(memory_space=pl.ANY)
VMEM = pl.BlockSpec(memory_space=pltpu.VMEM)


def _mb(n):
    return pltpu.CompilerParams(vmem_limit_bytes=n * 2**20)


def _cost(flops, bytes_accessed, transcendentals=0):
    return pl.CostEstimate(
        flops=int(flops), bytes_accessed=int(bytes_accessed), transcendentals=transcendentals
    )


def _offset(i, outer):
    return (i // outer) * 2 + (i % outer) * 8


def query_kernel(feat_hbm, wq_hbm, out, feat, wq, sem):
    copies = [
        pltpu.make_async_copy(feat_hbm, feat, sem.at[0]),
        pltpu.make_async_copy(wq_hbm, wq, sem.at[1]),
    ]
    for copy in copies:
        copy.start()
    for copy in copies:
        copy.wait()
    out[...] = jnp.dot(feat[...], wq[...], preferred_element_type=F32).astype(BF16)


def make_query(feat, wq):
    return pl.pallas_call(
        query_kernel,
        out_shape=jax.ShapeDtypeStruct(feat.shape, BF16),
        in_specs=[ANY, ANY],
        out_specs=VMEM,
        scratch_shapes=[
            pltpu.VMEM(feat.shape, BF16),
            pltpu.VMEM(wq.shape, BF16),
            pltpu.SemaphoreType.DMA((2,)),
        ],
        compiler_params=_mb(2),
        cost_estimate=_cost(2 * feat.shape[0] * wq.size, 24 * 2**20),
        name="make_query",
    )(feat, wq)


def gather_kernel(
    rel_ref, count_ref, slots_ref, acct, feats, place_ref, pair_rel_ref,
    table, rows0, rows1, next_ref,
):
    accounts, width = acct.shape
    blocks, block_len = slots_ref.shape
    relations = next_ref.shape[0]
    parts = width // LANES
    group = 16
    for r in range(relations):
        next_ref[r] = 0

    @pl.loop(0, blocks)
    def _(b):
        next_ref[rel_ref[b]] += 1

    @pl.loop(0, pair_rel_ref.shape[0])
    def _(p):
        pair_rel_ref[p] = 0

    first = jnp.int32(0)
    for r in range(relations):
        after = first + ((next_ref[r] + 1) // 2) * 2
        next_ref[r] = first
        first = after

    rows0[...] = jnp.zeros_like(rows0)
    rows1[...] = jnp.zeros_like(rows1)

    @pl.loop(0, accounts // 16, unroll=4)
    def _(g):
        start = pl.multiple_of(g * 16, 16)
        tile = acct[pl.ds(start, 16), :].astype(F32)
        for c in range(parts):
            table[pl.ds(start * parts + c, 16, stride=parts), :] = tile[
                :, c * LANES : (c + 1) * LANES
            ]

    def collect(b, rows):
        @pl.loop(0, (count_ref[b] + group - 1) // group)
        def _(g):
            base = g * group
            for u in range(group):
                source = pl.multiple_of(slots_ref[b, base + u] * parts, parts)
                target = pl.multiple_of(base * parts, group * parts) + u * parts
                rows[pl.ds(target, parts), :] = table[pl.ds(source, parts), :]

    def emit(b, rows):
        relation = rel_ref[b]
        place = next_ref[relation]
        next_ref[relation] = place + 1
        place_ref[b] = place
        pair_rel_ref[place // 2] = relation
        for c in range(parts):
            feats[place, :, c * LANES : (c + 1) * LANES] = rows[
                pl.ds(c, block_len, stride=parts), :
            ].astype(BF16)

    @pl.loop(0, blocks // 2)
    def _(h):
        collect(2 * h, rows0)
        collect(2 * h + 1, rows1)
        emit(2 * h, rows0)
        emit(2 * h + 1, rows1)


def gather(rel, count, slots, acct, relations):
    blocks, block_len = slots.shape
    accounts, width = acct.shape
    parts = width // LANES
    pairs = (blocks + relations) // 2
    rows = pltpu.VMEM((block_len * parts, LANES), F32)
    return pl.pallas_call(
        gather_kernel,
        out_shape=(
            jax.ShapeDtypeStruct((2 * pairs, block_len, width), BF16),
            jax.ShapeDtypeStruct((blocks,), jnp.int32),
            jax.ShapeDtypeStruct((pairs,), jnp.int32),
        ),
        in_specs=[SMEM] * 3 + [VMEM],
        out_specs=(VMEM, SMEM, SMEM),
        scratch_shapes=[
            pltpu.VMEM((accounts * parts, LANES), F32),
            rows,
            rows,
            pltpu.SMEM((relations,), jnp.int32),
        ],
        compiler_params=_mb(10),
        cost_estimate=_cost(0, 20 * 2**20),
        name="gather_slots",
    )(rel, count, slots, acct)


def _project_pair(feats, relation, kw, mw, keys, values):
    _, block_len, width = feats.shape
    both = feats[...].reshape(2 * block_len, width)
    for n in range(0, width, 256):
        key = jnp.dot(both, kw[relation, :, n : n + 256], preferred_element_type=F32).astype(BF16)
        value = jnp.dot(both, mw[relation, :, n : n + 256], preferred_element_type=F32).astype(BF16)
        for h in range(2):
            part = slice(h * block_len, (h + 1) * block_len)
            keys[h, n : n + 256, :] = key[part, :].T
            values[h, :, n : n + 256] = value[part, :]


def project_kernel(pair_rel_ref, feats, kw, mw, keys, values):
    @pl.loop(0, pair_rel_ref.shape[0], unroll=2)
    def _(p):
        pair = pl.ds(2 * p, 2)
        _project_pair(feats.at[pair], pair_rel_ref[p], kw, mw, keys.at[pair], values.at[pair])


def project_step_kernel(pair_rel_ref, feats, kw, mw, keys, values):
    _project_pair(feats, pair_rel_ref[pl.program_id(0)], kw, mw, keys, values)


def project(pair_rel, feats, kw, mw):
    places, block_len, width = feats.shape
    out_shape = (
        jax.ShapeDtypeStruct((places, width, block_len), BF16),
        jax.ShapeDtypeStruct((places, block_len, width), BF16),
    )
    cost = _cost(4 * places * block_len * width * width, 16 * 2**20)
    if places <= 40:
        return pl.pallas_call(
            project_kernel,
            out_shape=out_shape,
            in_specs=[SMEM] + [VMEM] * 3,
            out_specs=(VMEM, VMEM),
            compiler_params=_mb(4),
            cost_estimate=cost,
            name="project_slots",
        )(pair_rel, feats, kw, mw)
    whole = pl.BlockSpec(kw.shape, lambda p: (0, 0, 0))
    values = pl.BlockSpec((2, block_len, width), lambda p: (p, 0, 0))
    keys = pl.BlockSpec((2, width, block_len), lambda p: (p, 0, 0))
    return pl.pallas_call(
        project_step_kernel,
        grid=(places // 2,),
        out_shape=out_shape,
        in_specs=[SMEM, values, whole, whole],
        out_specs=(keys, values),
        compiler_params=_mb(20),
        cost_estimate=cost,
        name="project_slots",
    )(pair_rel, feats, kw, mw)


def aggregate_kernel(
    outer, shift, me_ref, rel_ref, count_ref, place_ref, bias_ref, merch_slot, query, keys,
    values, sums, gates,
):
    _, width, block_len = keys.shape
    blocks = merch_slot.shape[0] // 2
    merchants = query.shape[0] // blocks
    me = me_ref[0]
    row = lax.broadcasted_iota(jnp.int32, (merchants, block_len), 0)
    lane = lax.broadcasted_iota(jnp.int32, (merchants, block_len), 1)
    for i in range(blocks):
        block = jnp.bitwise_xor(me, _offset(i, outer) + shift)
        score = jnp.dot(
            query[i * merchants : (i + 1) * merchants, :],
            keys[place_ref[block]],
            preferred_element_type=F32,
        ) / math.sqrt(width)
        score = score + bias_ref[rel_ref[block]]
        mine = (merch_slot[pl.ds(block, 1), :] == row) & (lane < count_ref[block])
        gates[i * merchants : (i + 1) * merchants, :] = jnp.where(
            mine, jax.nn.sigmoid(score), 0.0
        ).astype(BF16)
    for i in range(blocks):
        block = jnp.bitwise_xor(me, _offset(i, outer) + shift)
        sums[i * merchants : (i + 1) * merchants, :] = jnp.dot(
            gates[i * merchants : (i + 1) * merchants, :],
            values[place_ref[block]],
            preferred_element_type=F32,
        ).astype(sums.dtype)


def aggregate(
    outer, shift, me, rel, count, place, bias, merch_slot, query, keys, values, dtype
):
    width, block_len = keys.shape[1:]
    rows = query.shape[0]
    return pl.pallas_call(
        functools.partial(aggregate_kernel, outer, shift),
        out_shape=jax.ShapeDtypeStruct(query.shape, dtype),
        in_specs=[SMEM] * 5 + [VMEM] * 4,
        out_specs=VMEM,
        scratch_shapes=[pltpu.VMEM((rows, block_len), BF16)],
        compiler_params=_mb(6),
        cost_estimate=_cost(
            4 * rows * block_len * width, 6 * 2**20, rows * block_len
        ),
        name="aggregate_odd" if shift else "aggregate_even",
    )(me, rel, count, place, bias, merch_slot, query, keys, values)


def combine_kernel(mine, other, *outs):
    rows = outs[0].shape[0]
    for j, out in enumerate(outs):
        part = slice(j * rows, (j + 1) * rows)
        out[...] = (mine[part, :] + other[part, :].astype(F32)).astype(out.dtype)


def combine(inner, mine, other):
    rows, width = mine.shape
    return pl.pallas_call(
        combine_kernel,
        out_shape=tuple(
            jax.ShapeDtypeStruct((rows // inner, width), F32 if j == 0 else BF16)
            for j in range(inner)
        ),
        in_specs=[VMEM, VMEM],
        out_specs=(VMEM,) * inner,
        compiler_params=_mb(2),
        cost_estimate=_cost(0, 2 * 2**20),
        name="combine_cores",
    )(mine, other)


def plane_kernel(inner, *refs):
    ins, outs = refs[:inner], refs[inner:]
    rows = outs[0].shape[0]
    for k, out in enumerate(outs):
        part = slice(k * rows, (k + 1) * rows)
        total = ins[0][part, :]
        for other in ins[1:]:
            total = total + other[part, :].astype(F32)
        out[...] = total.astype(out.dtype)


def combine_plane(outer, parts):
    rows, width = parts[0].shape
    return pl.pallas_call(
        functools.partial(plane_kernel, len(parts)),
        out_shape=tuple(
            jax.ShapeDtypeStruct((rows // outer, width), F32 if k == 0 else BF16)
            for k in range(outer)
        ),
        in_specs=[VMEM] * len(parts),
        out_specs=(VMEM,) * outer,
        compiler_params=_mb(2),
        cost_estimate=_cost(0, 2**20),
        name="combine_plane",
    )(*parts)


def finish_kernel(feat, gain, wo, *refs):
    out = refs[-1]
    total = refs[0][...]
    for part in refs[1:-1]:
        total = total + part[...].astype(F32)
    update = feat[...].astype(F32) + jnp.dot(
        total.astype(BF16), wo[...], preferred_element_type=F32
    )
    scale = lax.rsqrt(jnp.mean(update * update, axis=-1, keepdims=True) + 1e-06)
    out[...] = (update * scale * gain[...]).astype(BF16)


def finish(feat, gain, wo, parts):
    return pl.pallas_call(
        finish_kernel,
        out_shape=jax.ShapeDtypeStruct(feat.shape, BF16),
        in_specs=[VMEM] * (3 + len(parts)),
        out_specs=VMEM,
        compiler_params=_mb(2),
        name="finish",
    )(feat, gain.reshape(1, -1), wo, *parts)


def per_device(
    acct_feat,
    merch_feat,
    key_weight,
    msg_weight,
    query_weight,
    out_weight,
    rel_bias,
    out_gain,
    slot_acct,
    slot_merch,
    block_rel,
    block_count,
):
    devices = lax.axis_size(AXES)
    me = lax.axis_index(AXES).astype(jnp.int32).reshape(1)
    inner = 4
    outer = devices // (2 * inner)

    def swap(value, mask):
        return lax.ppermute(value, AXES, [(s, s ^ mask) for s in range(devices)])

    def after(value, *others):
        return lax.optimization_barrier((value,) + others)[0]

    query = make_query(merch_feat, query_weight)
    query = jnp.concatenate([swap(query, 8 * k + 1) for k in range(outer)], axis=0)
    rows, place, pair_rel = gather(
        block_rel, block_count, slot_acct, acct_feat, key_weight.shape[0]
    )
    query = after(query, rows)
    query = jnp.concatenate([query] + [swap(query, 2 * j) for j in range(1, inner)], axis=0)
    keys, values = project(pair_rel, rows, key_weight, msg_weight)
    query = after(query, keys)

    scalars = (me, block_rel, block_count, place, rel_bias, slot_merch)
    even_query = swap(query, 1)
    odd_sums = aggregate(outer, 1, *scalars, query, keys, values, BF16)
    other = swap(odd_sums, 1)
    even_sums = aggregate(outer, 0, *scalars, even_query, keys, values, F32)
    parts = combine(inner, even_sums, other)
    parts = combine_plane(
        outer, [parts[0]] + [swap(parts[j], 2 * j) for j in reversed(range(1, inner))]
    )
    parts = [parts[0]] + [swap(parts[k], 8 * k) for k in reversed(range(1, outer))]
    return finish(merch_feat, out_gain, out_weight, parts)


def solution(mesh):
    placed = (
        P(("acct", "merch"), None),
        P(("acct", "merch"), None),
        P(),
        P(),
        P(),
        P(),
        P(),
        P(),
        P(("acct", "merch"), None),
        P(("acct", "merch"), None),
        P(("acct", "merch")),
        P(("acct", "merch")),
    )
    return jax.shard_map(
        per_device,
        mesh=mesh,
        in_specs=placed,
        out_specs=P(("acct", "merch"), None),
        check_vma=False,
    )
```

```python
import functools
import math

import jax
import jax.numpy as jnp
from jax import lax
from jax.experimental import pallas as pl
from jax.experimental.pallas import tpu as pltpu
from jax.sharding import PartitionSpec as P

AXES = ("acct", "merch")
LANES = 128
F32 = jnp.float32
BF16 = jnp.bfloat16
SMEM = pl.BlockSpec(memory_space=pltpu.SMEM)
ANY = pl.BlockSpec(memory_space=pl.ANY)
VMEM = pl.BlockSpec(memory_space=pltpu.VMEM)


def _mb(n):
    return pltpu.CompilerParams(vmem_limit_bytes=n * 2**20)


def _cost(flops, bytes_accessed, transcendentals=0):
    return pl.CostEstimate(
        flops=int(flops), bytes_accessed=int(bytes_accessed), transcendentals=transcendentals
    )


def _offset(i, outer):
    return (i // outer) * 2 + (i % outer) * 8


def gather_kernel(
    outer, me_ref, slots_ref, acct_hbm, odd, even, acct, table, rows0, rows1, sem
):
    accounts, width = acct.shape
    blocks, block_len, _ = odd.shape
    parts = width // LANES
    pitch = table.shape[1]
    words = block_len // 2
    flat = table.reshape(accounts * pitch, LANES)
    me = me_ref[0]
    chunks = sem.shape[0]
    chunk = accounts // chunks
    copies = [
        pltpu.make_async_copy(
            acct_hbm.at[pl.ds(i * chunk, chunk)], acct.at[pl.ds(i * chunk, chunk)], sem.at[i]
        )
        for i in range(chunks)
    ]
    for copy in copies:
        copy.start()
    for i in range(chunks):
        copies[i].wait()

        @pl.loop(0, chunk // 16, unroll=4)
        def _(g):
            first = pl.multiple_of(i * chunk + g * 16, 16)
            tile = acct[pl.ds(first, 16), :].astype(F32)
            for c in range(parts):
                piece = tile[:, c * LANES : (c + 1) * LANES]
                for twin in (c, c + parts):
                    flat[pl.ds(first * pitch + twin, 16, stride=pitch), :] = piece

    lower = lax.broadcasted_iota(jnp.int32, (pitch, LANES), 0) < parts

    def collect(block, rows):
        for k in range(words):
            word = slots_ref[block, k]
            rows[k * pitch : (k + 1) * pitch, :] = jnp.where(
                lower, table[word & 0xFFFF], table[lax.shift_right_logical(word, 16)]
            )

    def emit(i, rows, out):
        for c in range(parts):
            for h in range(2):
                out[i, h * words : (h + 1) * words, c * LANES : (c + 1) * LANES] = rows[
                    pl.ds(h * parts + c, words, stride=pitch), :
                ].astype(BF16)

    @pl.loop(0, blocks)
    def _(i):
        offset = _offset(i, outer)
        collect(jnp.bitwise_xor(me, offset + 1), rows0)
        collect(jnp.bitwise_xor(me, offset), rows1)
        emit(i, rows0, odd)
        emit(i, rows1, even)


def gather(outer, me, slots, acct):
    blocks, block_len = slots.shape
    accounts, width = acct.shape
    words = block_len // 2
    packed = slots[:, :words] | (slots[:, words:] << 16)
    pitch = 2 * width // LANES
    rows = pltpu.VMEM((words * pitch, LANES), F32)
    half = jax.ShapeDtypeStruct((blocks // 2, block_len, width), BF16)
    return pl.pallas_call(
        functools.partial(gather_kernel, outer),
        out_shape=(half, half),
        in_specs=[SMEM, SMEM, ANY],
        out_specs=(VMEM, VMEM),
        scratch_shapes=[
            pltpu.VMEM(acct.shape, BF16),
            pltpu.VMEM((accounts, pitch, LANES), F32),
            rows,
            rows,
            pltpu.SemaphoreType.DMA((8,)),
        ],
        compiler_params=_mb(47 if blocks <= 32 else 28),
        cost_estimate=_cost(0, 20 * 2**20),
        name="gather_slots",
    )(me, packed, acct)


def project_kernel(outer, shifts, me_ref, rel_ref, kw, mw, *refs):
    halves = len(shifts)
    blocks, _, width = refs[0].shape
    half = width // 2
    me = me_ref[0]

    def one(i, shift, feats, keys, values):
        relation = rel_ref[jnp.bitwise_xor(me, _offset(i, outer) + shift)]
        for n in range(0, width, half):
            key = jnp.dot(feats[i], kw[relation, :, n : n + half], preferred_element_type=F32)
            keys[i, n : n + half, :] = key.astype(BF16).T
            value = jnp.dot(feats[i], mw[relation, :, n : n + half], preferred_element_type=F32)
            values[i, :, n : n + half] = value.astype(BF16)

    @pl.loop(0, blocks, unroll=2)
    def _(i):
        for h, shift in enumerate(shifts):
            one(i, shift, refs[h], refs[halves + 2 * h], refs[halves + 2 * h + 1])


def project(outer, shifts, me, rel, feats, kw, mw):
    blocks, block_len, width = feats[0].shape
    keys = jax.ShapeDtypeStruct((blocks, width, block_len), BF16)
    values = jax.ShapeDtypeStruct((blocks, block_len, width), BF16)
    return pl.pallas_call(
        functools.partial(project_kernel, outer, shifts),
        out_shape=(keys, values) * len(shifts),
        in_specs=[SMEM, SMEM] + [VMEM] * (2 + len(shifts)),
        out_specs=(VMEM, VMEM) * len(shifts),
        compiler_params=_mb(4),
        cost_estimate=_cost(
            4 * len(shifts) * blocks * block_len * width * width, 8 * len(shifts) * 2**20
        ),
        name="project_slots",
    )(me, rel, kw, mw, *feats)


def aggregate_kernel(
    outer, shift, me_ref, rel_ref, count_ref, bias_ref, merch_slot, feats, wq, keys, values,
    sums, query, gates,
):
    blocks, width, block_len = keys.shape
    merchants = feats.shape[0] // blocks
    me = me_ref[0]
    row = lax.broadcasted_iota(jnp.int32, (merchants, block_len), 0)
    lane = lax.broadcasted_iota(jnp.int32, (merchants, block_len), 1)
    query[...] = jnp.dot(feats[...], wq[...], preferred_element_type=F32).astype(BF16)
    for i in range(blocks):
        block = jnp.bitwise_xor(me, _offset(i, outer) + shift)
        score = jnp.dot(
            query[i * merchants : (i + 1) * merchants, :], keys[i], preferred_element_type=F32
        ) / math.sqrt(width)
        score = score + bias_ref[rel_ref[block]]
        mine = (merch_slot[pl.ds(block, 1), :] == row) & (lane < count_ref[block])
        gates[i * merchants : (i + 1) * merchants, :] = jnp.where(
            mine, jax.nn.sigmoid(score), 0.0
        ).astype(BF16)
    for i in range(blocks):
        sums[i * merchants : (i + 1) * merchants, :] = jnp.dot(
            gates[i * merchants : (i + 1) * merchants, :], values[i], preferred_element_type=F32
        ).astype(sums.dtype)


def aggregate(outer, shift, me, rel, count, bias, merch_slot, feats, wq, keys, values, dtype):
    blocks, width, block_len = keys.shape
    merchants = feats.shape[0] // blocks
    return pl.pallas_call(
        functools.partial(aggregate_kernel, outer, shift),
        out_shape=jax.ShapeDtypeStruct(feats.shape, dtype),
        in_specs=[SMEM] * 4 + [VMEM] * 5,
        out_specs=VMEM,
        scratch_shapes=[
            pltpu.VMEM(feats.shape, BF16),
            pltpu.VMEM((feats.shape[0], block_len), BF16),
        ],
        compiler_params=_mb(6),
        cost_estimate=_cost(
            4 * blocks * merchants * block_len * width + 2 * feats.shape[0] * width * width,
            6 * 2**20,
            blocks * merchants * block_len,
        ),
        name="aggregate_odd" if shift else "aggregate_even",
    )(me, rel, count, bias, merch_slot, feats, wq, keys, values)


def combine_kernel(mine, other, *outs):
    rows = outs[0].shape[0]
    for j, out in enumerate(outs):
        part = slice(j * rows, (j + 1) * rows)
        out[...] = (mine[part, :] + other[part, :].astype(F32)).astype(out.dtype)


def combine(inner, mine, other):
    rows, width = mine.shape
    return pl.pallas_call(
        combine_kernel,
        out_shape=tuple(
            jax.ShapeDtypeStruct((rows // inner, width), F32 if j == 0 else BF16)
            for j in range(inner)
        ),
        in_specs=[VMEM, VMEM],
        out_specs=(VMEM,) * inner,
        compiler_params=_mb(2),
        cost_estimate=_cost(0, 2 * 2**20),
        name="combine_cores",
    )(mine, other)


def plane_kernel(inner, *refs):
    ins, outs = refs[:inner], refs[inner:]
    rows = outs[0].shape[0]
    for k, out in enumerate(outs):
        part = slice(k * rows, (k + 1) * rows)
        total = ins[0][part, :]
        for other in ins[1:]:
            total = total + other[part, :].astype(F32)
        out[...] = total.astype(out.dtype)


def combine_plane(outer, parts):
    rows, width = parts[0].shape
    return pl.pallas_call(
        functools.partial(plane_kernel, len(parts)),
        out_shape=tuple(
            jax.ShapeDtypeStruct((rows // outer, width), F32 if k == 0 else BF16)
            for k in range(outer)
        ),
        in_specs=[VMEM] * len(parts),
        out_specs=(VMEM,) * outer,
        compiler_params=_mb(2),
        cost_estimate=_cost(0, 2**20),
        name="combine_plane",
    )(*parts)


def finish_kernel(feat, gain, wo, *refs):
    out = refs[-1]
    total = refs[0][...]
    for part in refs[1:-1]:
        total = total + part[...].astype(F32)
    update = feat[...].astype(F32) + jnp.dot(
        total.astype(BF16), wo[...], preferred_element_type=F32
    )
    scale = lax.rsqrt(jnp.mean(update * update, axis=-1, keepdims=True) + 1e-06)
    out[...] = (update * scale * gain[...]).astype(BF16)


def finish(feat, gain, wo, parts):
    return pl.pallas_call(
        finish_kernel,
        out_shape=jax.ShapeDtypeStruct(feat.shape, BF16),
        in_specs=[VMEM] * (3 + len(parts)),
        out_specs=VMEM,
        compiler_params=_mb(2),
        name="finish",
    )(feat, gain.reshape(1, -1), wo, *parts)


def per_device(
    acct_feat,
    merch_feat,
    key_weight,
    msg_weight,
    query_weight,
    out_weight,
    rel_bias,
    out_gain,
    slot_acct,
    slot_merch,
    block_rel,
    block_count,
):
    devices = lax.axis_size(AXES)
    me = lax.axis_index(AXES).astype(jnp.int32).reshape(1)
    inner = 4
    outer = devices // (2 * inner)

    def swap(value, mask):
        return lax.ppermute(value, AXES, [(s, s ^ mask) for s in range(devices)])

    def after(value, *others):
        return lax.optimization_barrier((value,) + others)[0]

    feats = jnp.concatenate([swap(merch_feat, 8 * k + 1) for k in range(outer)], axis=0)
    odd_rows, even_rows = gather(outer, me, slot_acct, acct_feat)
    feats = after(feats, odd_rows)
    feats = jnp.concatenate([feats] + [swap(feats, 2 * j) for j in range(1, inner)], axis=0)
    rows = (odd_rows, even_rows)
    weights = (key_weight, msg_weight)
    if devices <= 32:
        projected = project(outer, (1, 0), me, block_rel, rows, *weights)
    else:
        projected = [
            out
            for shift, feat in zip((1, 0), rows)
            for out in project(outer, (shift,), me, block_rel, (feat,), *weights)
        ]
    odd_keys, odd_values, even_keys, even_values = projected
    feats = after(feats, even_keys)

    shared = (me, block_rel, block_count, rel_bias, slot_merch)
    even_feats = swap(feats, 1)
    odd_sums = aggregate(outer, 1, *shared, feats, query_weight, odd_keys, odd_values, BF16)
    other = swap(odd_sums, 1)
    even_sums = aggregate(outer, 0, *shared, even_feats, query_weight, even_keys, even_values, F32)
    parts = combine(inner, even_sums, other)
    parts = combine_plane(
        outer, [parts[0]] + [swap(parts[j], 2 * j) for j in reversed(range(1, inner))]
    )
    parts = [parts[0]] + [swap(parts[k], 8 * k) for k in reversed(range(1, outer))]
    return finish(merch_feat, out_gain, out_weight, parts)


def solution(mesh):
    placed = (
        P(("acct", "merch"), None),
        P(("acct", "merch"), None),
        P(),
        P(),
        P(),
        P(),
        P(),
        P(),
        P(("acct", "merch"), None),
        P(("acct", "merch"), None),
        P(("acct", "merch")),
        P(("acct", "merch")),
    )
    return jax.shard_map(
        per_device,
        mesh=mesh,
        in_specs=placed,
        out_specs=P(("acct", "merch"), None),
        check_vma=False,
    )
```

```python
import functools
import math

import jax
import jax.numpy as jnp
from jax import lax
from jax.experimental import pallas as pl
from jax.experimental.pallas import tpu as pltpu
from jax.sharding import PartitionSpec as P

AXES = ("acct", "merch")
LANES = 128
F32 = jnp.float32
BF16 = jnp.bfloat16
SMEM = pl.BlockSpec(memory_space=pltpu.SMEM)
ANY = pl.BlockSpec(memory_space=pl.ANY)
VMEM = pl.BlockSpec(memory_space=pltpu.VMEM)


def _mb(n):
    return pltpu.CompilerParams(vmem_limit_bytes=n * 2**20)


def _cost(flops, bytes_accessed, transcendentals=0):
    return pl.CostEstimate(
        flops=int(flops), bytes_accessed=int(bytes_accessed), transcendentals=transcendentals
    )


def _offset(i, outer):
    return (i // outer) * 2 + (i % outer) * 8


def gather_kernel(
    outer, me_ref, slots_ref, acct_hbm, odd, even, acct, table, rows0, rows1, sem
):
    accounts, width = acct.shape
    blocks, block_len, _ = odd.shape
    parts = width // LANES
    pitch = table.shape[1]
    batch = 32
    flat = table.reshape(accounts * pitch, LANES)
    me = me_ref[0]
    chunks = sem.shape[0]
    chunk = accounts // chunks
    copies = [
        pltpu.make_async_copy(
            acct_hbm.at[pl.ds(i * chunk, chunk)], acct.at[pl.ds(i * chunk, chunk)], sem.at[i]
        )
        for i in range(chunks)
    ]
    for copy in copies:
        copy.start()
    for i in range(chunks):
        copies[i].wait()

        @pl.loop(0, chunk // 16, unroll=4)
        def _(g):
            first = pl.multiple_of(i * chunk + g * 16, 16)
            tile = acct[pl.ds(first, 16), :].astype(F32)
            for c in range(parts):
                flat[pl.ds(first * pitch + c, 16, stride=pitch), :] = tile[
                    :, c * LANES : (c + 1) * LANES
                ]

    def collect(block, rows):
        for k in range(0, block_len, batch):
            found = [table[slots_ref[block, k + u], :parts, :] for u in range(batch)]
            for u in range(batch):
                rows[(k + u) * parts : (k + u + 1) * parts, :] = found[u]

    def emit(i, rows, out):
        for c in range(parts):
            out[i, :, c * LANES : (c + 1) * LANES] = rows[
                pl.ds(c, block_len, stride=parts), :
            ].astype(BF16)

    @pl.loop(0, blocks)
    def _(i):
        offset = _offset(i, outer)
        collect(jnp.bitwise_xor(me, offset + 1), rows0)
        collect(jnp.bitwise_xor(me, offset), rows1)
        emit(i, rows0, odd)
        emit(i, rows1, even)


def gather(outer, me, slots, acct):
    blocks, block_len = slots.shape
    accounts, width = acct.shape
    parts = width // LANES
    pitch = -(-parts // 8) * 8
    rows = pltpu.VMEM((block_len * parts, LANES), F32)
    half = jax.ShapeDtypeStruct((blocks // 2, block_len, width), BF16)
    return pl.pallas_call(
        functools.partial(gather_kernel, outer),
        out_shape=(half, half),
        in_specs=[SMEM, SMEM, ANY],
        out_specs=(VMEM, VMEM),
        scratch_shapes=[
            pltpu.VMEM(acct.shape, BF16),
            pltpu.VMEM((accounts, pitch, LANES), F32),
            rows,
            rows,
            pltpu.SemaphoreType.DMA((8,)),
        ],
        compiler_params=_mb(47 if blocks <= 32 else 28),
        cost_estimate=_cost(0, 20 * 2**20),
        name="gather_slots",
    )(me, slots, acct)


def project_kernel(outer, shifts, me_ref, rel_ref, kw, mw, *refs):
    halves = len(shifts)
    blocks, _, width = refs[0].shape
    half = width // 2
    me = me_ref[0]

    def one(i, shift, feats, keys, values):
        relation = rel_ref[jnp.bitwise_xor(me, _offset(i, outer) + shift)]
        for n in range(0, width, half):
            key = jnp.dot(feats[i], kw[relation, :, n : n + half], preferred_element_type=F32)
            keys[i, :, n : n + half] = key.astype(BF16)
            value = jnp.dot(feats[i], mw[relation, :, n : n + half], preferred_element_type=F32)
            values[i, :, n : n + half] = value.astype(BF16)

    @pl.loop(0, blocks, unroll=2)
    def _(i):
        for h, shift in enumerate(shifts):
            one(i, shift, refs[h], refs[halves + 2 * h], refs[halves + 2 * h + 1])


def project(outer, shifts, me, rel, feats, kw, mw):
    blocks, block_len, width = feats[0].shape
    keys = values = jax.ShapeDtypeStruct(feats[0].shape, BF16)
    return pl.pallas_call(
        functools.partial(project_kernel, outer, shifts),
        out_shape=(keys, values) * len(shifts),
        in_specs=[SMEM, SMEM] + [VMEM] * (2 + len(shifts)),
        out_specs=(VMEM, VMEM) * len(shifts),
        compiler_params=_mb(4),
        cost_estimate=_cost(
            4 * len(shifts) * blocks * block_len * width * width, 8 * len(shifts) * 2**20
        ),
        name="project_slots",
    )(me, rel, kw, mw, *feats)


def aggregate_kernel(
    outer, shift, me_ref, rel_ref, count_ref, bias_ref, merch_slot, feats, wq, keys, values,
    sums, query,
):
    blocks, block_len, width = keys.shape
    merchants = feats.shape[0] // blocks
    me = me_ref[0]
    row = lax.broadcasted_iota(jnp.int32, (merchants, block_len), 0)
    lane = lax.broadcasted_iota(jnp.int32, (merchants, block_len), 1)
    query[...] = jnp.dot(feats[...], wq[...], preferred_element_type=F32).astype(BF16)
    for i in range(blocks):
        block = jnp.bitwise_xor(me, _offset(i, outer) + shift)
        part = slice(i * merchants, (i + 1) * merchants)
        mine = (merch_slot[pl.ds(block, 1), :] == row) & (lane < count_ref[block])
        mine = jnp.where(mine, 1.0, 0.0)
        queries = jnp.dot(mine.T.astype(BF16), query[part, :], preferred_element_type=F32)
        score = jnp.sum(keys[i].astype(F32) * queries, axis=1, keepdims=True) / math.sqrt(width)
        gate = jax.nn.sigmoid(score + bias_ref[rel_ref[block]])
        message = (gate * values[i].astype(F32)).astype(BF16)
        sums[part, :] = jnp.dot(
            mine.astype(BF16), message, preferred_element_type=F32
        ).astype(sums.dtype)


def aggregate(outer, shift, me, rel, count, bias, merch_slot, feats, wq, keys, values, dtype):
    blocks, block_len, width = keys.shape
    rows = feats.shape[0]
    return pl.pallas_call(
        functools.partial(aggregate_kernel, outer, shift),
        out_shape=jax.ShapeDtypeStruct(feats.shape, dtype),
        in_specs=[SMEM] * 4 + [VMEM] * 5,
        out_specs=VMEM,
        scratch_shapes=[pltpu.VMEM(feats.shape, BF16)],
        compiler_params=_mb(6),
        cost_estimate=_cost(
            4 * rows * block_len * width + 2 * rows * width * width,
            6 * 2**20,
            blocks * block_len,
        ),
        name="aggregate_odd" if shift else "aggregate_even",
    )(me, rel, count, bias, merch_slot, feats, wq, keys, values)


def combine_kernel(mine, other, *outs):
    rows = outs[0].shape[0]
    for j, out in enumerate(outs):
        part = slice(j * rows, (j + 1) * rows)
        out[...] = (mine[part, :] + other[part, :].astype(F32)).astype(out.dtype)


def combine(inner, mine, other):
    rows, width = mine.shape
    return pl.pallas_call(
        combine_kernel,
        out_shape=tuple(
            jax.ShapeDtypeStruct((rows // inner, width), F32 if j == 0 else BF16)
            for j in range(inner)
        ),
        in_specs=[VMEM, VMEM],
        out_specs=(VMEM,) * inner,
        compiler_params=_mb(2),
        cost_estimate=_cost(0, 2 * 2**20),
        name="combine_cores",
    )(mine, other)


def plane_kernel(inner, *refs):
    ins, outs = refs[:inner], refs[inner:]
    rows = outs[0].shape[0]
    for k, out in enumerate(outs):
        part = slice(k * rows, (k + 1) * rows)
        total = ins[0][part, :]
        for other in ins[1:]:
            total = total + other[part, :].astype(F32)
        out[...] = total.astype(out.dtype)


def combine_plane(outer, parts):
    rows, width = parts[0].shape
    return pl.pallas_call(
        functools.partial(plane_kernel, len(parts)),
        out_shape=tuple(
            jax.ShapeDtypeStruct((rows // outer, width), F32 if k == 0 else BF16)
            for k in range(outer)
        ),
        in_specs=[VMEM] * len(parts),
        out_specs=(VMEM,) * outer,
        compiler_params=_mb(2),
        cost_estimate=_cost(0, 2**20),
        name="combine_plane",
    )(*parts)


def finish_kernel(feat, gain, wo, *refs):
    out = refs[-1]
    total = refs[0][...]
    for part in refs[1:-1]:
        total = total + part[...].astype(F32)
    update = feat[...].astype(F32) + jnp.dot(
        total.astype(BF16), wo[...], preferred_element_type=F32
    )
    scale = lax.rsqrt(jnp.mean(update * update, axis=-1, keepdims=True) + 1e-06)
    out[...] = (update * scale * gain[...]).astype(BF16)


def finish(feat, gain, wo, parts):
    return pl.pallas_call(
        finish_kernel,
        out_shape=jax.ShapeDtypeStruct(feat.shape, BF16),
        in_specs=[VMEM] * (3 + len(parts)),
        out_specs=VMEM,
        compiler_params=_mb(2),
        name="finish",
    )(feat, gain.reshape(1, -1), wo, *parts)


def per_device(
    acct_feat,
    merch_feat,
    key_weight,
    msg_weight,
    query_weight,
    out_weight,
    rel_bias,
    out_gain,
    slot_acct,
    slot_merch,
    block_rel,
    block_count,
):
    devices = lax.axis_size(AXES)
    me = lax.axis_index(AXES).astype(jnp.int32).reshape(1)
    inner = 4
    outer = devices // (2 * inner)

    def swap(value, mask):
        return lax.ppermute(value, AXES, [(s, s ^ mask) for s in range(devices)])

    def after(value, *others):
        return lax.optimization_barrier((value,) + others)[0]

    feats = jnp.concatenate([swap(merch_feat, 8 * k + 1) for k in range(outer)], axis=0)
    odd_rows, even_rows = gather(outer, me, slot_acct, acct_feat)
    feats = after(feats, odd_rows)
    feats = jnp.concatenate([feats] + [swap(feats, 2 * j) for j in range(1, inner)], axis=0)
    rows = (odd_rows, even_rows)
    weights = (key_weight, msg_weight)
    if devices <= 32:
        projected = project(outer, (1, 0), me, block_rel, rows, *weights)
    else:
        projected = [
            out
            for shift, feat in zip((1, 0), rows)
            for out in project(outer, (shift,), me, block_rel, (feat,), *weights)
        ]
    odd_keys, odd_values, even_keys, even_values = projected
    feats = after(feats, even_keys)

    shared = (me, block_rel, block_count, rel_bias, slot_merch)
    even_feats = swap(feats, 1)
    odd_sums = aggregate(outer, 1, *shared, feats, query_weight, odd_keys, odd_values, BF16)
    other = swap(odd_sums, 1)
    even_sums = aggregate(outer, 0, *shared, even_feats, query_weight, even_keys, even_values, F32)
    parts = combine(inner, even_sums, other)
    parts = combine_plane(
        outer, [parts[0]] + [swap(parts[j], 2 * j) for j in reversed(range(1, inner))]
    )
    parts = [parts[0]] + [swap(parts[k], 8 * k) for k in reversed(range(1, outer))]
    return finish(merch_feat, out_gain, out_weight, parts)


def solution(mesh):
    placed = (
        P(("acct", "merch"), None),
        P(("acct", "merch"), None),
        P(),
        P(),
        P(),
        P(),
        P(),
        P(),
        P(("acct", "merch"), None),
        P(("acct", "merch"), None),
        P(("acct", "merch")),
        P(("acct", "merch")),
    )
    return jax.shard_map(
        per_device,
        mesh=mesh,
        in_specs=placed,
        out_specs=P(("acct", "merch"), None),
        check_vma=False,
    )
```

```python
import functools
import math

import jax
import jax.numpy as jnp
from jax import lax
from jax.experimental import pallas as pl
from jax.experimental.pallas import tpu as pltpu
from jax.sharding import PartitionSpec as P

AXES = ("acct", "merch")
LANES = 128
F32 = jnp.float32
BF16 = jnp.bfloat16
SMEM = pl.BlockSpec(memory_space=pltpu.SMEM)
ANY = pl.BlockSpec(memory_space=pl.ANY)
VMEM = pl.BlockSpec(memory_space=pltpu.VMEM)


def _mb(n):
    return pltpu.CompilerParams(vmem_limit_bytes=n * 2**20)


def _cost(flops, bytes_accessed, transcendentals=0):
    return pl.CostEstimate(
        flops=int(flops), bytes_accessed=int(bytes_accessed), transcendentals=transcendentals
    )


def _offset(i, outer):
    return (i // outer) * 2 + (i % outer) * 8


def gather_kernel(
    outer, me_ref, slots_ref, acct_hbm, odd, even, acct, table, rows0, rows1, sem
):
    accounts, width = acct.shape
    blocks, block_len, _ = odd.shape
    parts = width // LANES
    pitch = table.shape[1]
    batch = 16
    flat = table.reshape(accounts * pitch, LANES)
    me = me_ref[0]
    chunks = sem.shape[0]
    chunk = accounts // chunks
    copies = [
        pltpu.make_async_copy(
            acct_hbm.at[pl.ds(i * chunk, chunk)], acct.at[pl.ds(i * chunk, chunk)], sem.at[i]
        )
        for i in range(chunks)
    ]
    for copy in copies:
        copy.start()
    for i in range(chunks):
        copies[i].wait()

        @pl.loop(0, chunk // 16, unroll=4)
        def _(g):
            first = pl.multiple_of(i * chunk + g * 16, 16)
            tile = acct[pl.ds(first, 16), :].astype(F32)
            for c in range(parts):
                flat[pl.ds(first * pitch + c, 16, stride=pitch), :] = tile[
                    :, c * LANES : (c + 1) * LANES
                ]

    def collect(block, rows):
        for k in range(0, block_len, batch):
            found = [table[slots_ref[block, k + u], :parts, :] for u in range(batch)]
            for u in range(batch):
                rows[pl.ds(k + u, parts, stride=block_len), :] = found[u]

    def emit(i, rows, out):
        for c in range(parts):
            out[i, :, c * LANES : (c + 1) * LANES] = rows[
                c * block_len : (c + 1) * block_len, :
            ].astype(BF16)

    @pl.loop(0, blocks)
    def _(i):
        offset = _offset(i, outer)
        collect(jnp.bitwise_xor(me, offset + 1), rows0)
        collect(jnp.bitwise_xor(me, offset), rows1)
        emit(i, rows0, odd)
        emit(i, rows1, even)


def gather(outer, me, slots, acct):
    blocks, block_len = slots.shape
    accounts, width = acct.shape
    parts = width // LANES
    pitch = -(-parts // 8) * 8
    rows = pltpu.VMEM((block_len * parts, LANES), F32)
    half = jax.ShapeDtypeStruct((blocks // 2, block_len, width), BF16)
    return pl.pallas_call(
        functools.partial(gather_kernel, outer),
        out_shape=(half, half),
        in_specs=[SMEM, SMEM, ANY],
        out_specs=(VMEM, VMEM),
        scratch_shapes=[
            pltpu.VMEM(acct.shape, BF16),
            pltpu.VMEM((accounts, pitch, LANES), F32),
            rows,
            rows,
            pltpu.SemaphoreType.DMA((8,)),
        ],
        compiler_params=_mb(47 if blocks <= 32 else 28),
        cost_estimate=_cost(0, 20 * 2**20),
        name="gather_slots",
    )(me, slots, acct)


def project_kernel(outer, shifts, me_ref, rel_ref, kw, mw, *refs):
    halves = len(shifts)
    blocks, _, width = refs[0].shape
    half = width // 2
    me = me_ref[0]

    def one(i, shift, feats, keys, values):
        relation = rel_ref[jnp.bitwise_xor(me, _offset(i, outer) + shift)]
        for n in range(0, width, half):
            key = jnp.dot(feats[i], kw[relation, :, n : n + half], preferred_element_type=F32)
            keys[i, n : n + half, :] = key.astype(BF16).T
            value = jnp.dot(feats[i], mw[relation, :, n : n + half], preferred_element_type=F32)
            values[i, :, n : n + half] = value.astype(BF16)

    @pl.loop(0, blocks, unroll=2)
    def _(i):
        for h, shift in enumerate(shifts):
            one(i, shift, refs[h], refs[halves + 2 * h], refs[halves + 2 * h + 1])


def project(outer, shifts, me, rel, feats, kw, mw):
    blocks, block_len, width = feats[0].shape
    keys = jax.ShapeDtypeStruct((blocks, width, block_len), BF16)
    values = jax.ShapeDtypeStruct((blocks, block_len, width), BF16)
    return pl.pallas_call(
        functools.partial(project_kernel, outer, shifts),
        out_shape=(keys, values) * len(shifts),
        in_specs=[SMEM, SMEM] + [VMEM] * (2 + len(shifts)),
        out_specs=(VMEM, VMEM) * len(shifts),
        compiler_params=_mb(4),
        cost_estimate=_cost(
            4 * len(shifts) * blocks * block_len * width * width, 8 * len(shifts) * 2**20
        ),
        name="project_slots",
    )(me, rel, kw, mw, *feats)


def aggregate_kernel(
    outer, shift, me_ref, rel_ref, count_ref, bias_ref, merch_slot, feats, wq, keys, values,
    sums, query, gates,
):
    blocks, width, block_len = keys.shape
    merchants = feats.shape[0] // blocks
    me = me_ref[0]
    row = lax.broadcasted_iota(jnp.int32, (merchants, block_len), 0)
    lane = lax.broadcasted_iota(jnp.int32, (merchants, block_len), 1)
    query[...] = jnp.dot(feats[...], wq[...], preferred_element_type=F32).astype(BF16)
    for i in range(blocks):
        block = jnp.bitwise_xor(me, _offset(i, outer) + shift)
        score = jnp.dot(
            query[i * merchants : (i + 1) * merchants, :], keys[i], preferred_element_type=F32
        ) / math.sqrt(width)
        score = score + bias_ref[rel_ref[block]]
        mine = (merch_slot[pl.ds(block, 1), :] == row) & (lane < count_ref[block])
        gates[i * merchants : (i + 1) * merchants, :] = jnp.where(
            mine, jax.nn.sigmoid(score), 0.0
        ).astype(BF16)
    for i in range(blocks):
        sums[i * merchants : (i + 1) * merchants, :] = jnp.dot(
            gates[i * merchants : (i + 1) * merchants, :], values[i], preferred_element_type=F32
        ).astype(sums.dtype)


def aggregate(outer, shift, me, rel, count, bias, merch_slot, feats, wq, keys, values, dtype):
    blocks, width, block_len = keys.shape
    merchants = feats.shape[0] // blocks
    return pl.pallas_call(
        functools.partial(aggregate_kernel, outer, shift),
        out_shape=jax.ShapeDtypeStruct(feats.shape, dtype),
        in_specs=[SMEM] * 4 + [VMEM] * 5,
        out_specs=VMEM,
        scratch_shapes=[
            pltpu.VMEM(feats.shape, BF16),
            pltpu.VMEM((feats.shape[0], block_len), BF16),
        ],
        compiler_params=_mb(6),
        cost_estimate=_cost(
            4 * blocks * merchants * block_len * width + 2 * feats.shape[0] * width * width,
            6 * 2**20,
            blocks * merchants * block_len,
        ),
        name="aggregate_odd" if shift else "aggregate_even",
    )(me, rel, count, bias, merch_slot, feats, wq, keys, values)


def combine_kernel(mine, other, *outs):
    rows = outs[0].shape[0]
    for j, out in enumerate(outs):
        part = slice(j * rows, (j + 1) * rows)
        out[...] = (mine[part, :] + other[part, :].astype(F32)).astype(out.dtype)


def combine(inner, mine, other):
    rows, width = mine.shape
    return pl.pallas_call(
        combine_kernel,
        out_shape=tuple(
            jax.ShapeDtypeStruct((rows // inner, width), F32 if j == 0 else BF16)
            for j in range(inner)
        ),
        in_specs=[VMEM, VMEM],
        out_specs=(VMEM,) * inner,
        compiler_params=_mb(2),
        cost_estimate=_cost(0, 2 * 2**20),
        name="combine_cores",
    )(mine, other)


def plane_kernel(inner, *refs):
    ins, outs = refs[:inner], refs[inner:]
    rows = outs[0].shape[0]
    for k, out in enumerate(outs):
        part = slice(k * rows, (k + 1) * rows)
        total = ins[0][part, :]
        for other in ins[1:]:
            total = total + other[part, :].astype(F32)
        out[...] = total.astype(out.dtype)


def combine_plane(outer, parts):
    rows, width = parts[0].shape
    return pl.pallas_call(
        functools.partial(plane_kernel, len(parts)),
        out_shape=tuple(
            jax.ShapeDtypeStruct((rows // outer, width), F32 if k == 0 else BF16)
            for k in range(outer)
        ),
        in_specs=[VMEM] * len(parts),
        out_specs=(VMEM,) * outer,
        compiler_params=_mb(2),
        cost_estimate=_cost(0, 2**20),
        name="combine_plane",
    )(*parts)


def finish_kernel(feat, gain, wo, *refs):
    out = refs[-1]
    total = refs[0][...]
    for part in refs[1:-1]:
        total = total + part[...].astype(F32)
    update = feat[...].astype(F32) + jnp.dot(
        total.astype(BF16), wo[...], preferred_element_type=F32
    )
    scale = lax.rsqrt(jnp.mean(update * update, axis=-1, keepdims=True) + 1e-06)
    out[...] = (update * scale * gain[...]).astype(BF16)


def finish(feat, gain, wo, parts):
    return pl.pallas_call(
        finish_kernel,
        out_shape=jax.ShapeDtypeStruct(feat.shape, BF16),
        in_specs=[VMEM] * (3 + len(parts)),
        out_specs=VMEM,
        compiler_params=_mb(2),
        name="finish",
    )(feat, gain.reshape(1, -1), wo, *parts)


def per_device(
    acct_feat,
    merch_feat,
    key_weight,
    msg_weight,
    query_weight,
    out_weight,
    rel_bias,
    out_gain,
    slot_acct,
    slot_merch,
    block_rel,
    block_count,
):
    devices = lax.axis_size(AXES)
    me = lax.axis_index(AXES).astype(jnp.int32).reshape(1)
    inner = 4
    outer = devices // (2 * inner)

    def swap(value, mask):
        return lax.ppermute(value, AXES, [(s, s ^ mask) for s in range(devices)])

    def after(value, *others):
        return lax.optimization_barrier((value,) + others)[0]

    feats = jnp.concatenate([swap(merch_feat, 8 * k + 1) for k in range(outer)], axis=0)
    odd_rows, even_rows = gather(outer, me, slot_acct, acct_feat)
    feats = after(feats, odd_rows)
    feats = jnp.concatenate([feats] + [swap(feats, 2 * j) for j in range(1, inner)], axis=0)
    rows = (odd_rows, even_rows)
    weights = (key_weight, msg_weight)
    if devices <= 32:
        projected = project(outer, (1, 0), me, block_rel, rows, *weights)
    else:
        projected = [
            out
            for shift, feat in zip((1, 0), rows)
            for out in project(outer, (shift,), me, block_rel, (feat,), *weights)
        ]
    odd_keys, odd_values, even_keys, even_values = projected
    feats = after(feats, even_keys)

    shared = (me, block_rel, block_count, rel_bias, slot_merch)
    even_feats = swap(feats, 1)
    odd_sums = aggregate(outer, 1, *shared, feats, query_weight, odd_keys, odd_values, BF16)
    other = swap(odd_sums, 1)
    even_sums = aggregate(outer, 0, *shared, even_feats, query_weight, even_keys, even_values, F32)
    parts = combine(inner, even_sums, other)
    parts = combine_plane(
        outer, [parts[0]] + [swap(parts[j], 2 * j) for j in reversed(range(1, inner))]
    )
    parts = [parts[0]] + [swap(parts[k], 8 * k) for k in reversed(range(1, outer))]
    return finish(merch_feat, out_gain, out_weight, parts)


def solution(mesh):
    placed = (
        P(("acct", "merch"), None),
        P(("acct", "merch"), None),
        P(),
        P(),
        P(),
        P(),
        P(),
        P(),
        P(("acct", "merch"), None),
        P(("acct", "merch"), None),
        P(("acct", "merch")),
        P(("acct", "merch")),
    )
    return jax.shard_map(
        per_device,
        mesh=mesh,
        in_specs=placed,
        out_specs=P(("acct", "merch"), None),
        check_vma=False,
    )
```

```python
import functools
import math

import jax
import jax.numpy as jnp
from jax import lax
from jax.experimental import pallas as pl
from jax.experimental.pallas import tpu as pltpu
from jax.sharding import PartitionSpec as P

AXES = ("acct", "merch")
LANES = 128
F32 = jnp.float32
BF16 = jnp.bfloat16
SMEM = pl.BlockSpec(memory_space=pltpu.SMEM)
ANY = pl.BlockSpec(memory_space=pl.ANY)
VMEM = pl.BlockSpec(memory_space=pltpu.VMEM)


def _mb(n):
    return pltpu.CompilerParams(vmem_limit_bytes=n * 2**20)


def _cost(flops, bytes_accessed, transcendentals=0):
    return pl.CostEstimate(
        flops=int(flops), bytes_accessed=int(bytes_accessed), transcendentals=transcendentals
    )


def _offset(i, outer):
    return (i // outer) * 2 + (i % outer) * 8


def gather_kernel(
    outer, me_ref, count_ref, slots_ref, acct_hbm, odd, even, acct, table, rows0, rows1, sem
):
    accounts, width = acct.shape
    blocks, block_len, _ = odd.shape
    parts = width // LANES
    pitch = table.shape[1]
    group = 32
    flat = table.reshape(accounts * pitch, LANES)
    me = me_ref[0]
    chunks = sem.shape[0]
    chunk = accounts // chunks
    copies = [
        pltpu.make_async_copy(
            acct_hbm.at[pl.ds(i * chunk, chunk)], acct.at[pl.ds(i * chunk, chunk)], sem.at[i]
        )
        for i in range(chunks)
    ]
    for copy in copies:
        copy.start()
    rows0[...] = jnp.zeros_like(rows0)
    rows1[...] = jnp.zeros_like(rows1)
    for i in range(chunks):
        copies[i].wait()

        @pl.loop(0, chunk // 16, unroll=4)
        def _(g):
            first = pl.multiple_of(i * chunk + g * 16, 16)
            tile = acct[pl.ds(first, 16), :].astype(F32)
            for c in range(parts):
                flat[pl.ds(first * pitch + c, 16, stride=pitch), :] = tile[
                    :, c * LANES : (c + 1) * LANES
                ]

    def collect(block, rows):
        count = count_ref[block]
        start = block * block_len
        for k in range(0, block_len, group):

            @pl.when(count > k)
            def _():
                for u in range(k, k + group):
                    rows[u * parts : (u + 1) * parts, :] = table[slots_ref[start + u], :parts, :]

    def emit(i, rows, out):
        for c in range(parts):
            out[i, :, c * LANES : (c + 1) * LANES] = rows[
                pl.ds(c, block_len, stride=parts), :
            ].astype(BF16)

    @pl.loop(0, blocks)
    def _(i):
        offset = _offset(i, outer)
        collect(jnp.bitwise_xor(me, offset + 1), rows0)
        collect(jnp.bitwise_xor(me, offset), rows1)
        emit(i, rows0, odd)
        emit(i, rows1, even)


def gather(outer, me, count, slots, acct):
    blocks, block_len = slots.shape
    accounts, width = acct.shape
    parts = width // LANES
    pitch = -(-parts // 8) * 8
    rows = pltpu.VMEM((block_len * parts, LANES), F32)
    half = jax.ShapeDtypeStruct((blocks // 2, block_len, width), BF16)
    return pl.pallas_call(
        functools.partial(gather_kernel, outer),
        out_shape=(half, half),
        in_specs=[SMEM, SMEM, SMEM, ANY],
        out_specs=(VMEM, VMEM),
        scratch_shapes=[
            pltpu.VMEM(acct.shape, BF16),
            pltpu.VMEM((accounts, pitch, LANES), F32),
            rows,
            rows,
            pltpu.SemaphoreType.DMA((8,)),
        ],
        compiler_params=_mb(47 if blocks <= 32 else 28),
        cost_estimate=_cost(0, 20 * 2**20),
        name="gather_slots",
    )(me, count, slots.reshape(-1), acct)


def project_kernel(outer, shifts, me_ref, rel_ref, kw, mw, *refs):
    halves = len(shifts)
    blocks, _, width = refs[0].shape
    half = width // 2
    me = me_ref[0]

    def one(i, shift, feats, keys, values):
        relation = rel_ref[jnp.bitwise_xor(me, _offset(i, outer) + shift)]
        for n in range(0, width, half):
            key = jnp.dot(feats[i], kw[relation, :, n : n + half], preferred_element_type=F32)
            keys[i, n : n + half, :] = key.astype(BF16).T
            value = jnp.dot(feats[i], mw[relation, :, n : n + half], preferred_element_type=F32)
            values[i, :, n : n + half] = value.astype(BF16)

    @pl.loop(0, blocks, unroll=2)
    def _(i):
        for h, shift in enumerate(shifts):
            one(i, shift, refs[h], refs[halves + 2 * h], refs[halves + 2 * h + 1])


def project(outer, shifts, me, rel, feats, kw, mw):
    blocks, block_len, width = feats[0].shape
    keys = jax.ShapeDtypeStruct((blocks, width, block_len), BF16)
    values = jax.ShapeDtypeStruct((blocks, block_len, width), BF16)
    return pl.pallas_call(
        functools.partial(project_kernel, outer, shifts),
        out_shape=(keys, values) * len(shifts),
        in_specs=[SMEM, SMEM] + [VMEM] * (2 + len(shifts)),
        out_specs=(VMEM, VMEM) * len(shifts),
        compiler_params=_mb(4),
        cost_estimate=_cost(
            4 * len(shifts) * blocks * block_len * width * width, 8 * len(shifts) * 2**20
        ),
        name="project_slots",
    )(me, rel, kw, mw, *feats)


def aggregate_kernel(
    outer, shift, me_ref, rel_ref, count_ref, bias_ref, merch_slot, feats, wq, keys, values,
    sums, query, gates,
):
    blocks, width, block_len = keys.shape
    merchants = feats.shape[0] // blocks
    me = me_ref[0]
    row = lax.broadcasted_iota(jnp.int32, (merchants, block_len), 0)
    lane = lax.broadcasted_iota(jnp.int32, (merchants, block_len), 1)
    query[...] = jnp.dot(feats[...], wq[...], preferred_element_type=F32).astype(BF16)
    for i in range(blocks):
        block = jnp.bitwise_xor(me, _offset(i, outer) + shift)
        score = jnp.dot(
            query[i * merchants : (i + 1) * merchants, :], keys[i], preferred_element_type=F32
        ) / math.sqrt(width)
        score = score + bias_ref[rel_ref[block]]
        mine = (merch_slot[pl.ds(block, 1), :] == row) & (lane < count_ref[block])
        gates[i * merchants : (i + 1) * merchants, :] = jnp.where(
            mine, jax.nn.sigmoid(score), 0.0
        ).astype(BF16)
    for i in range(blocks):
        sums[i * merchants : (i + 1) * merchants, :] = jnp.dot(
            gates[i * merchants : (i + 1) * merchants, :], values[i], preferred_element_type=F32
        ).astype(sums.dtype)


def aggregate(outer, shift, me, rel, count, bias, merch_slot, feats, wq, keys, values, dtype):
    blocks, width, block_len = keys.shape
    merchants = feats.shape[0] // blocks
    return pl.pallas_call(
        functools.partial(aggregate_kernel, outer, shift),
        out_shape=jax.ShapeDtypeStruct(feats.shape, dtype),
        in_specs=[SMEM] * 4 + [VMEM] * 5,
        out_specs=VMEM,
        scratch_shapes=[
            pltpu.VMEM(feats.shape, BF16),
            pltpu.VMEM((feats.shape[0], block_len), BF16),
        ],
        compiler_params=_mb(6),
        cost_estimate=_cost(
            4 * blocks * merchants * block_len * width + 2 * feats.shape[0] * width * width,
            6 * 2**20,
            blocks * merchants * block_len,
        ),
        name="aggregate_odd" if shift else "aggregate_even",
    )(me, rel, count, bias, merch_slot, feats, wq, keys, values)


def combine_kernel(mine, other, *outs):
    rows = outs[0].shape[0]
    for j, out in enumerate(outs):
        part = slice(j * rows, (j + 1) * rows)
        out[...] = (mine[part, :] + other[part, :].astype(F32)).astype(out.dtype)


def combine(inner, mine, other):
    rows, width = mine.shape
    return pl.pallas_call(
        combine_kernel,
        out_shape=tuple(
            jax.ShapeDtypeStruct((rows // inner, width), F32 if j == 0 else BF16)
            for j in range(inner)
        ),
        in_specs=[VMEM, VMEM],
        out_specs=(VMEM,) * inner,
        compiler_params=_mb(2),
        cost_estimate=_cost(0, 2 * 2**20),
        name="combine_cores",
    )(mine, other)


def plane_kernel(inner, *refs):
    ins, outs = refs[:inner], refs[inner:]
    rows = outs[0].shape[0]
    for k, out in enumerate(outs):
        part = slice(k * rows, (k + 1) * rows)
        total = ins[0][part, :]
        for other in ins[1:]:
            total = total + other[part, :].astype(F32)
        out[...] = total.astype(out.dtype)


def combine_plane(outer, parts):
    rows, width = parts[0].shape
    return pl.pallas_call(
        functools.partial(plane_kernel, len(parts)),
        out_shape=tuple(
            jax.ShapeDtypeStruct((rows // outer, width), F32 if k == 0 else BF16)
            for k in range(outer)
        ),
        in_specs=[VMEM] * len(parts),
        out_specs=(VMEM,) * outer,
        compiler_params=_mb(2),
        cost_estimate=_cost(0, 2**20),
        name="combine_plane",
    )(*parts)


def finish_kernel(feat, gain, wo, *refs):
    out = refs[-1]
    total = refs[0][...]
    for part in refs[1:-1]:
        total = total + part[...].astype(F32)
    update = feat[...].astype(F32) + jnp.dot(
        total.astype(BF16), wo[...], preferred_element_type=F32
    )
    scale = lax.rsqrt(jnp.mean(update * update, axis=-1, keepdims=True) + 1e-06)
    out[...] = (update * scale * gain[...]).astype(BF16)


def finish(feat, gain, wo, parts):
    return pl.pallas_call(
        finish_kernel,
        out_shape=jax.ShapeDtypeStruct(feat.shape, BF16),
        in_specs=[VMEM] * (3 + len(parts)),
        out_specs=VMEM,
        compiler_params=_mb(2),
        name="finish",
    )(feat, gain.reshape(1, -1), wo, *parts)


def per_device(
    acct_feat,
    merch_feat,
    key_weight,
    msg_weight,
    query_weight,
    out_weight,
    rel_bias,
    out_gain,
    slot_acct,
    slot_merch,
    block_rel,
    block_count,
):
    devices = lax.axis_size(AXES)
    me = lax.axis_index(AXES).astype(jnp.int32).reshape(1)
    inner = 4
    outer = devices // (2 * inner)

    def swap(value, mask):
        return lax.ppermute(value, AXES, [(s, s ^ mask) for s in range(devices)])

    def after(value, *others):
        return lax.optimization_barrier((value,) + others)[0]

    feats = jnp.concatenate([swap(merch_feat, 8 * k + 1) for k in range(outer)], axis=0)
    odd_rows, even_rows = gather(outer, me, block_count, slot_acct, acct_feat)
    feats = after(feats, odd_rows)
    feats = jnp.concatenate([feats] + [swap(feats, 2 * j) for j in range(1, inner)], axis=0)
    rows = (odd_rows, even_rows)
    weights = (key_weight, msg_weight)
    if devices <= 32:
        projected = project(outer, (1, 0), me, block_rel, rows, *weights)
    else:
        projected = [
            out
            for shift, feat in zip((1, 0), rows)
            for out in project(outer, (shift,), me, block_rel, (feat,), *weights)
        ]
    odd_keys, odd_values, even_keys, even_values = projected
    feats = after(feats, even_keys)

    shared = (me, block_rel, block_count, rel_bias, slot_merch)
    even_feats = swap(feats, 1)
    odd_sums = aggregate(outer, 1, *shared, feats, query_weight, odd_keys, odd_values, BF16)
    other = swap(odd_sums, 1)
    even_sums = aggregate(outer, 0, *shared, even_feats, query_weight, even_keys, even_values, F32)
    parts = combine(inner, even_sums, other)
    parts = combine_plane(
        outer, [parts[0]] + [swap(parts[j], 2 * j) for j in reversed(range(1, inner))]
    )
    parts = [parts[0]] + [swap(parts[k], 8 * k) for k in reversed(range(1, outer))]
    return finish(merch_feat, out_gain, out_weight, parts)


def solution(mesh):
    placed = (
        P(("acct", "merch"), None),
        P(("acct", "merch"), None),
        P(),
        P(),
        P(),
        P(),
        P(),
        P(),
        P(("acct", "merch"), None),
        P(("acct", "merch"), None),
        P(("acct", "merch")),
        P(("acct", "merch")),
    )
    return jax.shard_map(
        per_device,
        mesh=mesh,
        in_specs=placed,
        out_specs=P(("acct", "merch"), None),
        check_vma=False,
    )
```

```python
import functools
import math

import jax
import jax.numpy as jnp
from jax import lax
from jax.experimental import pallas as pl
from jax.experimental.pallas import tpu as pltpu
from jax.sharding import PartitionSpec as P

AXES = ("acct", "merch")
LANES = 128
F32 = jnp.float32
BF16 = jnp.bfloat16
SMEM = pl.BlockSpec(memory_space=pltpu.SMEM)
ANY = pl.BlockSpec(memory_space=pl.ANY)
VMEM = pl.BlockSpec(memory_space=pltpu.VMEM)


def _mb(n):
    return pltpu.CompilerParams(vmem_limit_bytes=n * 2**20)


def _cost(flops, bytes_accessed, transcendentals=0):
    return pl.CostEstimate(
        flops=int(flops), bytes_accessed=int(bytes_accessed), transcendentals=transcendentals
    )


def _offset(i, outer):
    return (i // outer) * 2 + (i % outer) * 8


def gather_kernel(
    outer, me_ref, slots_ref, acct_hbm, odd, even, acct, table, rows0, rows1, sem
):
    accounts, width = acct.shape
    blocks, block_len, _ = odd.shape
    parts = width // LANES
    pitch = table.shape[1]
    apart = block_len + 2
    flat = table.reshape(accounts * pitch, LANES)
    me = me_ref[0]
    chunks = sem.shape[0]
    chunk = accounts // chunks
    copies = [
        pltpu.make_async_copy(
            acct_hbm.at[pl.ds(i * chunk, chunk)], acct.at[pl.ds(i * chunk, chunk)], sem.at[i]
        )
        for i in range(chunks)
    ]
    for copy in copies:
        copy.start()
    for i in range(chunks):
        copies[i].wait()

        @pl.loop(0, chunk // 16, unroll=4)
        def _(g):
            first = pl.multiple_of(i * chunk + g * 16, 16)
            tile = acct[pl.ds(first, 16), :].astype(F32)
            for c in range(parts):
                flat[pl.ds(first * pitch + c, 16, stride=pitch), :] = tile[
                    :, c * LANES : (c + 1) * LANES
                ]

    def collect(block, rows):
        start = block * block_len
        for k in range(block_len):
            rows[pl.ds(k, parts, stride=apart), :] = table[slots_ref[start + k], :parts, :]

    def emit(i, rows, out):
        origin = jnp.minimum(me, 0)
        for c in range(parts):
            out[i, :, c * LANES : (c + 1) * LANES] = rows[
                pl.ds(origin + c * apart, block_len), :
            ].astype(BF16)

    @pl.loop(0, blocks)
    def _(i):
        offset = _offset(i, outer)
        collect(jnp.bitwise_xor(me, offset + 1), rows0)
        collect(jnp.bitwise_xor(me, offset), rows1)
        emit(i, rows0, odd)
        emit(i, rows1, even)


def gather(outer, me, slots, acct):
    blocks, block_len = slots.shape
    accounts, width = acct.shape
    parts = width // LANES
    pitch = -(-parts // 8) * 8
    rows = pltpu.VMEM(((block_len + 2) * parts, LANES), F32)
    half = jax.ShapeDtypeStruct((blocks // 2, block_len, width), BF16)
    return pl.pallas_call(
        functools.partial(gather_kernel, outer),
        out_shape=(half, half),
        in_specs=[SMEM, SMEM, ANY],
        out_specs=(VMEM, VMEM),
        scratch_shapes=[
            pltpu.VMEM(acct.shape, BF16),
            pltpu.VMEM((accounts, pitch, LANES), F32),
            rows,
            rows,
            pltpu.SemaphoreType.DMA((8,)),
        ],
        compiler_params=_mb(47 if blocks <= 32 else 28),
        cost_estimate=_cost(0, 20 * 2**20),
        name="gather_slots",
    )(me, slots.reshape(-1), acct)


def project_kernel(outer, shifts, me_ref, rel_ref, kw, mw, *refs):
    halves = len(shifts)
    blocks, _, width = refs[0].shape
    half = width // 2
    me = me_ref[0]

    def one(i, shift, feats, keys, values):
        relation = rel_ref[jnp.bitwise_xor(me, _offset(i, outer) + shift)]
        for n in range(0, width, half):
            key = jnp.dot(feats[i], kw[relation, :, n : n + half], preferred_element_type=F32)
            keys[i, n : n + half, :] = key.astype(BF16).T
            value = jnp.dot(feats[i], mw[relation, :, n : n + half], preferred_element_type=F32)
            values[i, :, n : n + half] = value.astype(BF16)

    @pl.loop(0, blocks, unroll=2)
    def _(i):
        for h, shift in enumerate(shifts):
            one(i, shift, refs[h], refs[halves + 2 * h], refs[halves + 2 * h + 1])


def project(outer, shifts, me, rel, feats, kw, mw):
    blocks, block_len, width = feats[0].shape
    keys = jax.ShapeDtypeStruct((blocks, width, block_len), BF16)
    values = jax.ShapeDtypeStruct((blocks, block_len, width), BF16)
    return pl.pallas_call(
        functools.partial(project_kernel, outer, shifts),
        out_shape=(keys, values) * len(shifts),
        in_specs=[SMEM, SMEM] + [VMEM] * (2 + len(shifts)),
        out_specs=(VMEM, VMEM) * len(shifts),
        compiler_params=_mb(4),
        cost_estimate=_cost(
            4 * len(shifts) * blocks * block_len * width * width, 8 * len(shifts) * 2**20
        ),
        name="project_slots",
    )(me, rel, kw, mw, *feats)


def aggregate_kernel(
    outer, shift, me_ref, rel_ref, count_ref, bias_ref, merch_slot, feats, wq, keys, values,
    sums, query, gates,
):
    blocks, width, block_len = keys.shape
    merchants = feats.shape[0] // blocks
    me = me_ref[0]
    row = lax.broadcasted_iota(jnp.int32, (merchants, block_len), 0)
    lane = lax.broadcasted_iota(jnp.int32, (merchants, block_len), 1)
    query[...] = jnp.dot(feats[...], wq[...], preferred_element_type=F32).astype(BF16)
    for i in range(blocks):
        block = jnp.bitwise_xor(me, _offset(i, outer) + shift)
        score = jnp.dot(
            query[i * merchants : (i + 1) * merchants, :], keys[i], preferred_element_type=F32
        ) / math.sqrt(width)
        score = score + bias_ref[rel_ref[block]]
        mine = (merch_slot[pl.ds(block, 1), :] == row) & (lane < count_ref[block])
        gates[i * merchants : (i + 1) * merchants, :] = jnp.where(
            mine, jax.nn.sigmoid(score), 0.0
        ).astype(BF16)
    for i in range(blocks):
        sums[i * merchants : (i + 1) * merchants, :] = jnp.dot(
            gates[i * merchants : (i + 1) * merchants, :], values[i], preferred_element_type=F32
        ).astype(sums.dtype)


def aggregate(outer, shift, me, rel, count, bias, merch_slot, feats, wq, keys, values, dtype):
    blocks, width, block_len = keys.shape
    merchants = feats.shape[0] // blocks
    return pl.pallas_call(
        functools.partial(aggregate_kernel, outer, shift),
        out_shape=jax.ShapeDtypeStruct(feats.shape, dtype),
        in_specs=[SMEM] * 4 + [VMEM] * 5,
        out_specs=VMEM,
        scratch_shapes=[
            pltpu.VMEM(feats.shape, BF16),
            pltpu.VMEM((feats.shape[0], block_len), BF16),
        ],
        compiler_params=_mb(6),
        cost_estimate=_cost(
            4 * blocks * merchants * block_len * width + 2 * feats.shape[0] * width * width,
            6 * 2**20,
            blocks * merchants * block_len,
        ),
        name="aggregate_odd" if shift else "aggregate_even",
    )(me, rel, count, bias, merch_slot, feats, wq, keys, values)


def combine_kernel(mine, other, *outs):
    rows = outs[0].shape[0]
    for j, out in enumerate(outs):
        part = slice(j * rows, (j + 1) * rows)
        out[...] = (mine[part, :] + other[part, :].astype(F32)).astype(out.dtype)


def combine(inner, mine, other):
    rows, width = mine.shape
    return pl.pallas_call(
        combine_kernel,
        out_shape=tuple(
            jax.ShapeDtypeStruct((rows // inner, width), F32 if j == 0 else BF16)
            for j in range(inner)
        ),
        in_specs=[VMEM, VMEM],
        out_specs=(VMEM,) * inner,
        compiler_params=_mb(2),
        cost_estimate=_cost(0, 2 * 2**20),
        name="combine_cores",
    )(mine, other)


def plane_kernel(inner, *refs):
    ins, outs = refs[:inner], refs[inner:]
    rows = outs[0].shape[0]
    for k, out in enumerate(outs):
        part = slice(k * rows, (k + 1) * rows)
        total = ins[0][part, :]
        for other in ins[1:]:
            total = total + other[part, :].astype(F32)
        out[...] = total.astype(out.dtype)


def combine_plane(outer, parts):
    rows, width = parts[0].shape
    return pl.pallas_call(
        functools.partial(plane_kernel, len(parts)),
        out_shape=tuple(
            jax.ShapeDtypeStruct((rows // outer, width), F32 if k == 0 else BF16)
            for k in range(outer)
        ),
        in_specs=[VMEM] * len(parts),
        out_specs=(VMEM,) * outer,
        compiler_params=_mb(2),
        cost_estimate=_cost(0, 2**20),
        name="combine_plane",
    )(*parts)


def finish_kernel(feat, gain, wo, *refs):
    out = refs[-1]
    total = refs[0][...]
    for part in refs[1:-1]:
        total = total + part[...].astype(F32)
    update = feat[...].astype(F32) + jnp.dot(
        total.astype(BF16), wo[...], preferred_element_type=F32
    )
    scale = lax.rsqrt(jnp.mean(update * update, axis=-1, keepdims=True) + 1e-06)
    out[...] = (update * scale * gain[...]).astype(BF16)


def finish(feat, gain, wo, parts):
    return pl.pallas_call(
        finish_kernel,
        out_shape=jax.ShapeDtypeStruct(feat.shape, BF16),
        in_specs=[VMEM] * (3 + len(parts)),
        out_specs=VMEM,
        compiler_params=_mb(2),
        name="finish",
    )(feat, gain.reshape(1, -1), wo, *parts)


def per_device(
    acct_feat,
    merch_feat,
    key_weight,
    msg_weight,
    query_weight,
    out_weight,
    rel_bias,
    out_gain,
    slot_acct,
    slot_merch,
    block_rel,
    block_count,
):
    devices = lax.axis_size(AXES)
    me = lax.axis_index(AXES).astype(jnp.int32).reshape(1)
    inner = 4
    outer = devices // (2 * inner)

    def swap(value, mask):
        return lax.ppermute(value, AXES, [(s, s ^ mask) for s in range(devices)])

    def after(value, *others):
        return lax.optimization_barrier((value,) + others)[0]

    feats = jnp.concatenate([swap(merch_feat, 8 * k + 1) for k in range(outer)], axis=0)
    odd_rows, even_rows = gather(outer, me, slot_acct, acct_feat)
    feats = after(feats, odd_rows)
    feats = jnp.concatenate([feats] + [swap(feats, 2 * j) for j in range(1, inner)], axis=0)
    rows = (odd_rows, even_rows)
    weights = (key_weight, msg_weight)
    if devices <= 32:
        projected = project(outer, (1, 0), me, block_rel, rows, *weights)
    else:
        projected = [
            out
            for shift, feat in zip((1, 0), rows)
            for out in project(outer, (shift,), me, block_rel, (feat,), *weights)
        ]
    odd_keys, odd_values, even_keys, even_values = projected
    feats = after(feats, even_keys)

    shared = (me, block_rel, block_count, rel_bias, slot_merch)
    even_feats = swap(feats, 1)
    odd_sums = aggregate(outer, 1, *shared, feats, query_weight, odd_keys, odd_values, BF16)
    other = swap(odd_sums, 1)
    even_sums = aggregate(outer, 0, *shared, even_feats, query_weight, even_keys, even_values, F32)
    parts = combine(inner, even_sums, other)
    parts = combine_plane(
        outer, [parts[0]] + [swap(parts[j], 2 * j) for j in reversed(range(1, inner))]
    )
    parts = [parts[0]] + [swap(parts[k], 8 * k) for k in reversed(range(1, outer))]
    return finish(merch_feat, out_gain, out_weight, parts)


def solution(mesh):
    placed = (
        P(("acct", "merch"), None),
        P(("acct", "merch"), None),
        P(),
        P(),
        P(),
        P(),
        P(),
        P(),
        P(("acct", "merch"), None),
        P(("acct", "merch"), None),
        P(("acct", "merch")),
        P(("acct", "merch")),
    )
    return jax.shard_map(
        per_device,
        mesh=mesh,
        in_specs=placed,
        out_specs=P(("acct", "merch"), None),
        check_vma=False,
    )
```

```python
import functools
import math

import jax
import jax.numpy as jnp
from jax import lax
from jax.experimental import pallas as pl
from jax.experimental.pallas import tpu as pltpu
from jax.sharding import PartitionSpec as P

AXES = ("acct", "merch")
LANES = 128
F32 = jnp.float32
BF16 = jnp.bfloat16
SMEM = pl.BlockSpec(memory_space=pltpu.SMEM)
ANY = pl.BlockSpec(memory_space=pl.ANY)
VMEM = pl.BlockSpec(memory_space=pltpu.VMEM)


def _mb(n):
    return pltpu.CompilerParams(vmem_limit_bytes=n * 2**20)


def _cost(flops, bytes_accessed, transcendentals=0):
    return pl.CostEstimate(
        flops=int(flops), bytes_accessed=int(bytes_accessed), transcendentals=transcendentals
    )


def _offset(i, outer):
    return (i // outer) * 2 + (i % outer) * 8


def gather_kernel(
    outer, me_ref, slots_ref, acct_hbm, odd, even, acct, table, rows0, rows1, sem
):
    accounts, width = acct.shape
    blocks, block_len, _ = odd.shape
    parts = width // LANES
    pitch = table.shape[1]
    batch = 32
    flat = table.reshape(accounts * pitch, LANES)
    me = me_ref[0]
    chunks = sem.shape[0]
    chunk = accounts // chunks
    copies = [
        pltpu.make_async_copy(
            acct_hbm.at[pl.ds(i * chunk, chunk)], acct.at[pl.ds(i * chunk, chunk)], sem.at[i]
        )
        for i in range(chunks)
    ]
    for copy in copies:
        copy.start()
    for i in range(chunks):
        copies[i].wait()

        @pl.loop(0, chunk // 16, unroll=4)
        def _(g):
            first = pl.multiple_of(i * chunk + g * 16, 16)
            tile = acct[pl.ds(first, 16), :].astype(F32)
            for c in range(parts):
                flat[pl.ds(first * pitch + c, 16, stride=pitch), :] = tile[
                    :, c * LANES : (c + 1) * LANES
                ]

    def collect(block, rows):
        for k in range(0, block_len, batch):
            found = [table[slots_ref[block, k + u], :parts, :] for u in range(batch)]
            for u in range(batch):
                rows[(k + u) * parts : (k + u + 1) * parts, :] = found[u]

    def emit(i, rows, out):
        for c in range(parts):
            out[i, :, c * LANES : (c + 1) * LANES] = rows[
                pl.ds(c, block_len, stride=parts), :
            ].astype(BF16)

    @pl.loop(0, blocks)
    def _(i):
        offset = _offset(i, outer)
        collect(jnp.bitwise_xor(me, offset + 1), rows0)
        collect(jnp.bitwise_xor(me, offset), rows1)
        emit(i, rows0, odd)
        emit(i, rows1, even)


def gather(outer, me, slots, acct):
    blocks, block_len = slots.shape
    accounts, width = acct.shape
    parts = width // LANES
    pitch = -(-parts // 8) * 8
    rows = pltpu.VMEM((block_len * parts, LANES), F32)
    half = jax.ShapeDtypeStruct((blocks // 2, block_len, width), BF16)
    return pl.pallas_call(
        functools.partial(gather_kernel, outer),
        out_shape=(half, half),
        in_specs=[SMEM, SMEM, ANY],
        out_specs=(VMEM, VMEM),
        scratch_shapes=[
            pltpu.VMEM(acct.shape, BF16),
            pltpu.VMEM((accounts, pitch, LANES), F32),
            rows,
            rows,
            pltpu.SemaphoreType.DMA((8,)),
        ],
        compiler_params=_mb(47 if blocks <= 32 else 28),
        cost_estimate=_cost(0, 20 * 2**20),
        name="gather_slots",
    )(me, slots, acct)


def sums_kernel(
    outer, group, shift, me_ref, rel_ref, count_ref, bias_ref, merch_slot, feats, wq, rows, kw, mw,
    sums, query, keys, values, gates,
):
    owners, width, block_len = keys.shape
    merchants = sums.shape[0] // owners
    half = width // 2
    me = me_ref[0]
    row = lax.broadcasted_iota(jnp.int32, (merchants, block_len), 0)
    lane = lax.broadcasted_iota(jnp.int32, (merchants, block_len), 1)
    blocks = [jnp.bitwise_xor(me, 2 * group + 8 * i + shift) for i in range(owners)]
    parts = [slice(i * merchants, (i + 1) * merchants) for i in range(owners)]
    mine = slice(group * owners * merchants, (group + 1) * owners * merchants)
    query[...] = jnp.dot(feats[mine, :], wq[...], preferred_element_type=F32).astype(BF16)
    for i in range(owners):
        relation = rel_ref[blocks[i]]
        found = rows.at[group * owners + i]
        for n in range(0, width, half):
            key = jnp.dot(found[...], kw[relation, :, n : n + half], preferred_element_type=F32)
            keys[i, n : n + half, :] = key.astype(BF16).T
            value = jnp.dot(found[...], mw[relation, :, n : n + half], preferred_element_type=F32)
            values[i, :, n : n + half] = value.astype(BF16)
    for i in range(owners):
        score = jnp.dot(query[parts[i], :], keys[i], preferred_element_type=F32) / math.sqrt(width)
        score = score + bias_ref[rel_ref[blocks[i]]]
        live = (merch_slot[pl.ds(blocks[i], 1), :] == row) & (lane < count_ref[blocks[i]])
        gates[parts[i], :] = jnp.where(live, jax.nn.sigmoid(score), 0.0).astype(BF16)
    for i in range(owners):
        sums[parts[i], :] = jnp.dot(
            gates[parts[i], :], values[i], preferred_element_type=F32
        ).astype(sums.dtype)


def group_sums(
    outer, inner, group, shift, me, rel, count, bias, merch_slot, feats, wq, rows, kw, mw, dtype
):
    _, block_len, width = rows.shape
    merchants = feats.shape[0] // (outer * inner)
    return pl.pallas_call(
        functools.partial(sums_kernel, outer, group, shift),
        out_shape=jax.ShapeDtypeStruct((outer * merchants, width), dtype),
        in_specs=[SMEM] * 4 + [VMEM] * 6,
        out_specs=VMEM,
        scratch_shapes=[
            pltpu.VMEM((outer * merchants, width), BF16),
            pltpu.VMEM((outer, width, block_len), BF16),
            pltpu.VMEM((outer, block_len, width), BF16),
            pltpu.VMEM((outer * merchants, block_len), BF16),
        ],
        compiler_params=_mb(8),
        cost_estimate=_cost(1000, 1000),
        name="group_sums",
    )(me, rel, count, bias, merch_slot, feats, wq, rows, kw, mw)


def combine_kernel(mine, other, out):
    out[...] = (mine[...] + other[...].astype(F32)).astype(out.dtype)


def combine(mine, other, dtype):
    return pl.pallas_call(
        combine_kernel,
        out_shape=jax.ShapeDtypeStruct(mine.shape, dtype),
        in_specs=[VMEM, VMEM],
        out_specs=VMEM,
        compiler_params=_mb(2),
        cost_estimate=_cost(0, 2**19),
        name="combine_cores",
    )(mine, other)


def plane_kernel(inner, *refs):
    ins, outs = refs[:inner], refs[inner:]
    rows = outs[0].shape[0]
    for k, out in enumerate(outs):
        part = slice(k * rows, (k + 1) * rows)
        total = ins[0][part, :]
        for other in ins[1:]:
            total = total + other[part, :].astype(F32)
        out[...] = total.astype(out.dtype)


def combine_plane(outer, parts):
    rows, width = parts[0].shape
    return pl.pallas_call(
        functools.partial(plane_kernel, len(parts)),
        out_shape=tuple(
            jax.ShapeDtypeStruct((rows // outer, width), F32 if k == 0 else BF16)
            for k in range(outer)
        ),
        in_specs=[VMEM] * len(parts),
        out_specs=(VMEM,) * outer,
        compiler_params=_mb(2),
        cost_estimate=_cost(0, 2**20),
        name="combine_plane",
    )(*parts)


def finish_kernel(feat, gain, wo, *refs):
    out = refs[-1]
    total = refs[0][...]
    for part in refs[1:-1]:
        total = total + part[...].astype(F32)
    update = feat[...].astype(F32) + jnp.dot(
        total.astype(BF16), wo[...], preferred_element_type=F32
    )
    scale = lax.rsqrt(jnp.mean(update * update, axis=-1, keepdims=True) + 1e-06)
    out[...] = (update * scale * gain[...]).astype(BF16)


def finish(feat, gain, wo, parts):
    return pl.pallas_call(
        finish_kernel,
        out_shape=jax.ShapeDtypeStruct(feat.shape, BF16),
        in_specs=[VMEM] * (3 + len(parts)),
        out_specs=VMEM,
        compiler_params=_mb(2),
        name="finish",
    )(feat, gain.reshape(1, -1), wo, *parts)


def per_device(
    acct_feat,
    merch_feat,
    key_weight,
    msg_weight,
    query_weight,
    out_weight,
    rel_bias,
    out_gain,
    slot_acct,
    slot_merch,
    block_rel,
    block_count,
):
    devices = lax.axis_size(AXES)
    me = lax.axis_index(AXES).astype(jnp.int32).reshape(1)
    inner = 4
    outer = devices // (2 * inner)

    def swap(value, mask):
        return lax.ppermute(value, AXES, [(s, s ^ mask) for s in range(devices)])

    def after(value, *others):
        return lax.optimization_barrier((value,) + others)[0]

    feats = jnp.concatenate([swap(merch_feat, 8 * k + 1) for k in range(outer)], axis=0)
    feats = jnp.concatenate(
        [feats] + [swap(feats, 2 * j) for j in reversed(range(1, inner))][::-1], axis=0
    )
    odd_rows, even_rows = gather(outer, me, slot_acct, acct_feat)
    feats = after(feats, odd_rows)
    even_feats = swap(feats, 1)

    weights = (key_weight, msg_weight)
    rest = (block_rel, block_count, rel_bias, slot_merch)
    parts = [None] * inner
    here = me
    for j in reversed(range(inner)):
        odd = group_sums(
            outer, inner, j, 1, here, *rest, feats, query_weight, odd_rows, *weights, BF16
        )
        here = after(here, odd)
        even = group_sums(
            outer, inner, j, 0, here, *rest, even_feats, query_weight, even_rows, *weights, F32
        )
        parts[j] = combine(even, swap(odd, 1), BF16 if j else F32)
        here = after(here, parts[j])
    parts = combine_plane(
        outer, [parts[0]] + [swap(parts[j], 2 * j) for j in reversed(range(1, inner))]
    )
    parts = [parts[0]] + [swap(parts[k], 8 * k) for k in reversed(range(1, outer))]
    return finish(merch_feat, out_gain, out_weight, parts)


def solution(mesh):
    placed = (
        P(("acct", "merch"), None),
        P(("acct", "merch"), None),
        P(),
        P(),
        P(),
        P(),
        P(),
        P(),
        P(("acct", "merch"), None),
        P(("acct", "merch"), None),
        P(("acct", "merch")),
        P(("acct", "merch")),
    )
    return jax.shard_map(
        per_device,
        mesh=mesh,
        in_specs=placed,
        out_specs=P(("acct", "merch"), None),
        check_vma=False,
    )
```

```python
import functools
import math

import jax
import jax.numpy as jnp
from jax import lax
from jax.experimental import pallas as pl
from jax.experimental.pallas import tpu as pltpu
from jax.sharding import PartitionSpec as P

AXES = ("acct", "merch")
LANES = 128
F32 = jnp.float32
BF16 = jnp.bfloat16
SMEM = pl.BlockSpec(memory_space=pltpu.SMEM)
ANY = pl.BlockSpec(memory_space=pl.ANY)
VMEM = pl.BlockSpec(memory_space=pltpu.VMEM)


def _mb(n):
    return pltpu.CompilerParams(vmem_limit_bytes=n * 2**20)


def _cost(flops, bytes_accessed, transcendentals=0):
    return pl.CostEstimate(
        flops=int(flops), bytes_accessed=int(bytes_accessed), transcendentals=transcendentals
    )


def _offset(i, outer):
    return (i // outer) * 2 + (i % outer) * 8


def gather_kernel(
    outer, me_ref, slots_ref, acct_hbm, odd, even, acct, table, rows0, rows1, sem
):
    accounts, width = acct.shape
    blocks, block_len, _ = odd.shape
    parts = width // LANES
    pitch = table.shape[1]
    batch = 32
    flat = table.reshape(accounts * pitch, LANES)
    me = me_ref[0]
    chunks = sem.shape[0]
    chunk = accounts // chunks
    copies = [
        pltpu.make_async_copy(
            acct_hbm.at[pl.ds(i * chunk, chunk)], acct.at[pl.ds(i * chunk, chunk)], sem.at[i]
        )
        for i in range(chunks)
    ]
    for copy in copies:
        copy.start()
    for i in range(chunks):
        copies[i].wait()

        @pl.loop(0, chunk // 16, unroll=4)
        def _(g):
            first = pl.multiple_of(i * chunk + g * 16, 16)
            tile = acct[pl.ds(first, 16), :].astype(F32)
            for c in range(parts):
                flat[pl.ds(first * pitch + c, 16, stride=pitch), :] = tile[
                    :, c * LANES : (c + 1) * LANES
                ]

    def collect(block, rows):
        for k in range(0, block_len, batch):
            found = [table[slots_ref[block, k + u], :parts, :] for u in range(batch)]
            for u in range(batch):
                rows[(k + u) * parts : (k + u + 1) * parts, :] = found[u]

    def emit(i, rows, out):
        for c in range(parts):
            out[i, :, c * LANES : (c + 1) * LANES] = rows[
                pl.ds(c, block_len, stride=parts), :
            ].astype(BF16)

    @pl.loop(0, blocks)
    def _(i):
        offset = _offset(i, outer)
        collect(jnp.bitwise_xor(me, offset + 1), rows0)
        collect(jnp.bitwise_xor(me, offset), rows1)
        emit(i, rows0, odd)
        emit(i, rows1, even)


def gather(outer, me, slots, acct):
    blocks, block_len = slots.shape
    accounts, width = acct.shape
    parts = width // LANES
    pitch = -(-parts // 8) * 8
    rows = pltpu.VMEM((block_len * parts, LANES), F32)
    half = jax.ShapeDtypeStruct((blocks // 2, block_len, width), BF16)
    return pl.pallas_call(
        functools.partial(gather_kernel, outer),
        out_shape=(half, half),
        in_specs=[SMEM, SMEM, ANY],
        out_specs=(VMEM, VMEM),
        scratch_shapes=[
            pltpu.VMEM(acct.shape, BF16),
            pltpu.VMEM((accounts, pitch, LANES), F32),
            rows,
            rows,
            pltpu.SemaphoreType.DMA((8,)),
        ],
        compiler_params=_mb(47 if blocks <= 32 else 28),
        cost_estimate=_cost(0, 20 * 2**20),
        name="gather_slots",
    )(me, slots, acct)


def project_kernel(outer, spans, me_ref, rel_ref, kw, mw, *refs):
    width = refs[0].shape[2]
    half = width // 2
    me = me_ref[0]
    count = len(spans)

    def one(i, first, shift, feats, keys, values):
        relation = rel_ref[jnp.bitwise_xor(me, _offset(first + i, outer) + shift)]
        for n in range(0, width, half):
            key = jnp.dot(
                feats[first + i], kw[relation, :, n : n + half], preferred_element_type=F32
            )
            keys[i, n : n + half, :] = key.astype(BF16).T
            value = jnp.dot(
                feats[first + i], mw[relation, :, n : n + half], preferred_element_type=F32
            )
            values[i, :, n : n + half] = value.astype(BF16)

    for s, (first, last, shift) in enumerate(spans):
        outs = refs[count + 2 * s : count + 2 * s + 2]

        @pl.loop(0, last - first, unroll=4)
        def _(i):
            one(i, first, shift, refs[s], *outs)


def project(outer, spans, me, rel, feats, kw, mw):
    _, block_len, width = feats[0].shape
    out_shape = []
    for first, last, _ in spans:
        out_shape.append(jax.ShapeDtypeStruct((last - first, width, block_len), BF16))
        out_shape.append(jax.ShapeDtypeStruct((last - first, block_len, width), BF16))
    blocks = sum(last - first for first, last, _ in spans)
    return pl.pallas_call(
        functools.partial(project_kernel, outer, spans),
        out_shape=tuple(out_shape),
        in_specs=[SMEM, SMEM] + [VMEM] * (2 + len(spans)),
        out_specs=(VMEM,) * len(out_shape),
        compiler_params=_mb(4),
        cost_estimate=_cost(4 * blocks * block_len * width * width, blocks * 2**19),
        name="project_slots",
    )(me, rel, kw, mw, *feats)


def aggregate_kernel(
    outer, first, shift, me_ref, rel_ref, count_ref, bias_ref, merch_slot, feats, wq, keys, values,
    sums, query, gates,
):
    blocks, width, block_len = keys.shape
    merchants = sums.shape[0] // blocks
    me = me_ref[0]
    row = lax.broadcasted_iota(jnp.int32, (merchants, block_len), 0)
    lane = lax.broadcasted_iota(jnp.int32, (merchants, block_len), 1)
    query[...] = jnp.dot(
        feats[first * merchants : (first + blocks) * merchants, :],
        wq[...],
        preferred_element_type=F32,
    ).astype(BF16)
    parts = [slice(i * merchants, (i + 1) * merchants) for i in range(blocks)]
    for i in range(blocks):
        block = jnp.bitwise_xor(me, _offset(first + i, outer) + shift)
        score = jnp.dot(query[parts[i], :], keys[i], preferred_element_type=F32) / math.sqrt(width)
        score = score + bias_ref[rel_ref[block]]
        mine = (merch_slot[pl.ds(block, 1), :] == row) & (lane < count_ref[block])
        gates[parts[i], :] = jnp.where(mine, jax.nn.sigmoid(score), 0.0).astype(BF16)
    for i in range(blocks):
        sums[parts[i], :] = jnp.dot(
            gates[parts[i], :], values[i], preferred_element_type=F32
        ).astype(sums.dtype)


def aggregate(outer, first, shift, me, rel, count, bias, merch_slot, feats, wq, keys, values, dtype):
    blocks, width, block_len = keys.shape
    rows = feats.shape[0] * blocks // (merch_slot.shape[0] // 2)
    return pl.pallas_call(
        functools.partial(aggregate_kernel, outer, first, shift),
        out_shape=jax.ShapeDtypeStruct((rows, width), dtype),
        in_specs=[SMEM] * 4 + [VMEM] * 5,
        out_specs=VMEM,
        scratch_shapes=[
            pltpu.VMEM((rows, width), BF16),
            pltpu.VMEM((rows, block_len), BF16),
        ],
        compiler_params=_mb(6),
        cost_estimate=_cost(
            4 * rows * block_len * width + 2 * rows * width * width, 6 * 2**20, rows * block_len
        ),
        name="aggregate_odd" if shift else "aggregate_even",
    )(me, rel, count, bias, merch_slot, feats, wq, keys, values)


def combine_kernel(skip, mine, other, *outs):
    rows = outs[0].shape[0]
    for j, out in enumerate(outs):
        part = slice(j * rows, (j + 1) * rows)
        theirs = slice(skip + j * rows, skip + (j + 1) * rows)
        out[...] = (mine[part, :] + other[theirs, :].astype(F32)).astype(out.dtype)


def combine(groups, skip, mine, other, dtype):
    rows, width = mine.shape
    return pl.pallas_call(
        functools.partial(combine_kernel, skip),
        out_shape=(jax.ShapeDtypeStruct((rows // groups, width), dtype),) * groups,
        in_specs=[VMEM, VMEM],
        out_specs=(VMEM,) * groups,
        compiler_params=_mb(2),
        cost_estimate=_cost(0, 2 * 2**20),
        name="combine_cores",
    )(mine, other)


def plane_kernel(outer, me_ref, *refs):
    ins, out = refs[:-1], refs[-1]
    rows = out.shape[0] // outer
    for k in range(outer):
        part = slice(k * rows, (k + 1) * rows)
        total = ins[0][part, :]
        for other in ins[1:]:
            total = total + other[part, :].astype(F32)
        place = jnp.bitwise_xor(me_ref[0] >> 3, k)
        out[pl.ds(pl.multiple_of(place * rows, rows), rows), :] = total.astype(BF16)


def combine_plane(outer, me, parts):
    return pl.pallas_call(
        functools.partial(plane_kernel, outer),
        out_shape=jax.ShapeDtypeStruct(parts[0].shape, BF16),
        in_specs=[SMEM] + [VMEM] * len(parts),
        out_specs=VMEM,
        compiler_params=_mb(2),
        cost_estimate=_cost(0, 2**20),
        name="combine_plane",
    )(me, *parts)


def finish_kernel(feat, gain, wo, parts, out):
    merchants = feat.shape[0]
    total = parts[:merchants, :].astype(F32)
    for k in range(1, parts.shape[0] // merchants):
        total = total + parts[k * merchants : (k + 1) * merchants, :].astype(F32)
    update = feat[...].astype(F32) + jnp.dot(
        total.astype(BF16), wo[...], preferred_element_type=F32
    )
    scale = lax.rsqrt(jnp.mean(update * update, axis=-1, keepdims=True) + 1e-06)
    out[...] = (update * scale * gain[...]).astype(BF16)


def finish(feat, gain, wo, parts):
    return pl.pallas_call(
        finish_kernel,
        out_shape=jax.ShapeDtypeStruct(feat.shape, BF16),
        in_specs=[VMEM] * 4,
        out_specs=VMEM,
        compiler_params=_mb(2),
        name="finish",
    )(feat, gain.reshape(1, -1), wo, parts)


def per_device(
    acct_feat,
    merch_feat,
    key_weight,
    msg_weight,
    query_weight,
    out_weight,
    rel_bias,
    out_gain,
    slot_acct,
    slot_merch,
    block_rel,
    block_count,
):
    devices = lax.axis_size(AXES)
    me = lax.axis_index(AXES).astype(jnp.int32).reshape(1)
    inner = 4
    outer = devices // (2 * inner)

    def swap(value, mask):
        return lax.ppermute(value, AXES, [(s, s ^ mask) for s in range(devices)])

    def after(value, *others):
        return lax.optimization_barrier((value,) + others)[0]

    feats = jnp.concatenate([swap(merch_feat, 8 * k + 1) for k in range(outer)], axis=0)
    rows = gather(outer, me, slot_acct, acct_feat)
    feats = after(feats, rows[0])
    feats = jnp.concatenate([feats] + [swap(feats, 2 * j) for j in range(1, inner)], axis=0)

    weights = (key_weight, msg_weight)
    rest = (block_rel, block_count, rel_bias, slot_merch)
    blocks = inner * outer
    odd_keys, odd_values, far_keys, far_values = project(
        outer, ((0, blocks, 1), (outer, blocks, 0)), me, block_rel, rows, *weights
    )
    feats = after(feats, far_keys)
    even_feats = swap(feats, 1)
    odd = aggregate(outer, 0, 1, me, *rest, feats, query_weight, odd_keys, odd_values, BF16)
    other = swap(odd, 1)
    far = aggregate(
        outer, outer, 0, me, *rest, even_feats, query_weight, far_keys, far_values, F32
    )
    parts = combine(inner - 1, outer * merch_feat.shape[0], far, other, BF16)

    here = after(me, *parts)
    near_keys, near_values = project(
        outer, ((0, outer, 0),), here, block_rel, rows[1:], *weights
    )
    near = aggregate(
        outer, 0, 0, here, *rest, even_feats, query_weight, near_keys, near_values, F32
    )
    (near,) = combine(1, 0, near, other, F32)
    parts = combine_plane(
        outer, me, [near] + [swap(parts[j - 1], 2 * j) for j in reversed(range(1, inner))]
    )
    groups = [[base + 8 * k for k in range(outer)] for base in range(8)]
    parts = lax.all_to_all(
        parts, AXES, split_axis=0, concat_axis=0, tiled=True, axis_index_groups=groups
    )
    return finish(merch_feat, out_gain, out_weight, parts)


def solution(mesh):
    placed = (
        P(("acct", "merch"), None),
        P(("acct", "merch"), None),
        P(),
        P(),
        P(),
        P(),
        P(),
        P(),
        P(("acct", "merch"), None),
        P(("acct", "merch"), None),
        P(("acct", "merch")),
        P(("acct", "merch")),
    )
    return jax.shard_map(
        per_device,
        mesh=mesh,
        in_specs=placed,
        out_specs=P(("acct", "merch"), None),
        check_vma=False,
    )
```

```python
import functools
import math

import jax
import jax.numpy as jnp
from jax import lax
from jax.experimental import pallas as pl
from jax.experimental.pallas import tpu as pltpu
from jax.sharding import PartitionSpec as P

AXES = ("acct", "merch")
LANES = 128
F32 = jnp.float32
BF16 = jnp.bfloat16
SMEM = pl.BlockSpec(memory_space=pltpu.SMEM)
ANY = pl.BlockSpec(memory_space=pl.ANY)
VMEM = pl.BlockSpec(memory_space=pltpu.VMEM)


def _mb(n):
    return pltpu.CompilerParams(vmem_limit_bytes=n * 2**20)


def _cost(flops, bytes_accessed, transcendentals=0):
    return pl.CostEstimate(
        flops=int(flops), bytes_accessed=int(bytes_accessed), transcendentals=transcendentals
    )


def _offset(i, outer):
    return (i // outer) * 2 + (i % outer) * 8


def gather_kernel(
    outer, me_ref, slots_ref, acct_hbm, odd, even, acct, table, rows0, rows1, sem
):
    accounts, width = acct.shape
    blocks, block_len, _ = odd.shape
    parts = width // LANES
    pitch = table.shape[1]
    batch = 32
    flat = table.reshape(accounts * pitch, LANES)
    me = me_ref[0]
    chunks = sem.shape[0]
    chunk = accounts // chunks
    copies = [
        pltpu.make_async_copy(
            acct_hbm.at[pl.ds(i * chunk, chunk)], acct.at[pl.ds(i * chunk, chunk)], sem.at[i]
        )
        for i in range(chunks)
    ]
    for copy in copies:
        copy.start()
    for i in range(chunks):
        copies[i].wait()

        @pl.loop(0, chunk // 16, unroll=4)
        def _(g):
            first = pl.multiple_of(i * chunk + g * 16, 16)
            tile = acct[pl.ds(first, 16), :].astype(F32)
            for c in range(parts):
                flat[pl.ds(first * pitch + c, 16, stride=pitch), :] = tile[
                    :, c * LANES : (c + 1) * LANES
                ]

    def collect(block, rows):
        for k in range(0, block_len, batch):
            found = [table[slots_ref[block, k + u], :parts, :] for u in range(batch)]
            for u in range(batch):
                rows[(k + u) * parts : (k + u + 1) * parts, :] = found[u]

    def emit(i, rows, out):
        for c in range(parts):
            out[i, :, c * LANES : (c + 1) * LANES] = rows[
                pl.ds(c, block_len, stride=parts), :
            ].astype(BF16)

    @pl.loop(0, blocks)
    def _(i):
        offset = _offset(i, outer)
        collect(jnp.bitwise_xor(me, offset + 1), rows0)
        collect(jnp.bitwise_xor(me, offset), rows1)
        emit(i, rows0, odd)
        emit(i, rows1, even)


def gather(outer, me, slots, acct):
    blocks, block_len = slots.shape
    accounts, width = acct.shape
    parts = width // LANES
    pitch = -(-parts // 8) * 8
    rows = pltpu.VMEM((block_len * parts, LANES), F32)
    half = jax.ShapeDtypeStruct((blocks // 2, block_len, width), BF16)
    return pl.pallas_call(
        functools.partial(gather_kernel, outer),
        out_shape=(half, half),
        in_specs=[SMEM, SMEM, ANY],
        out_specs=(VMEM, VMEM),
        scratch_shapes=[
            pltpu.VMEM(acct.shape, BF16),
            pltpu.VMEM((accounts, pitch, LANES), F32),
            rows,
            rows,
            pltpu.SemaphoreType.DMA((8,)),
        ],
        compiler_params=_mb(47 if blocks <= 32 else 28),
        cost_estimate=_cost(0, 20 * 2**20),
        name="gather_slots",
    )(me, slots, acct)


def project_kernel(outer, spans, me_ref, rel_ref, kw, mw, *refs):
    width = refs[0].shape[2]
    half = width // 2
    me = me_ref[0]
    count = len(spans)

    def one(i, first, shift, feats, keys, values):
        relation = rel_ref[jnp.bitwise_xor(me, _offset(first + i, outer) + shift)]
        for n in range(0, width, half):
            key = jnp.dot(
                feats[first + i], kw[relation, :, n : n + half], preferred_element_type=F32
            )
            keys[i, n : n + half, :] = key.astype(BF16).T
            value = jnp.dot(
                feats[first + i], mw[relation, :, n : n + half], preferred_element_type=F32
            )
            values[i, :, n : n + half] = value.astype(BF16)

    for s, (first, last, shift) in enumerate(spans):
        outs = refs[count + 2 * s : count + 2 * s + 2]

        @pl.loop(0, last - first, unroll=4)
        def _(i):
            one(i, first, shift, refs[s], *outs)


def project(outer, spans, me, rel, feats, kw, mw):
    _, block_len, width = feats[0].shape
    out_shape = []
    for first, last, _ in spans:
        out_shape.append(jax.ShapeDtypeStruct((last - first, width, block_len), BF16))
        out_shape.append(jax.ShapeDtypeStruct((last - first, block_len, width), BF16))
    blocks = sum(last - first for first, last, _ in spans)
    return pl.pallas_call(
        functools.partial(project_kernel, outer, spans),
        out_shape=tuple(out_shape),
        in_specs=[SMEM, SMEM] + [VMEM] * (2 + len(spans)),
        out_specs=(VMEM,) * len(out_shape),
        compiler_params=_mb(4),
        cost_estimate=_cost(4 * blocks * block_len * width * width, blocks * 2**19),
        name="project_slots",
    )(me, rel, kw, mw, *feats)


def aggregate_kernel(
    outer, first, shift, me_ref, rel_ref, count_ref, bias_ref, merch_slot, feats, wq, keys, values,
    sums, query, gates,
):
    blocks, width, block_len = keys.shape
    merchants = sums.shape[0] // blocks
    me = me_ref[0]
    row = lax.broadcasted_iota(jnp.int32, (merchants, block_len), 0)
    lane = lax.broadcasted_iota(jnp.int32, (merchants, block_len), 1)
    query[...] = jnp.dot(
        feats[first * merchants : (first + blocks) * merchants, :],
        wq[...],
        preferred_element_type=F32,
    ).astype(BF16)
    parts = [slice(i * merchants, (i + 1) * merchants) for i in range(blocks)]
    for i in range(blocks):
        block = jnp.bitwise_xor(me, _offset(first + i, outer) + shift)
        score = jnp.dot(query[parts[i], :], keys[i], preferred_element_type=F32) / math.sqrt(width)
        score = score + bias_ref[rel_ref[block]]
        mine = (merch_slot[pl.ds(block, 1), :] == row) & (lane < count_ref[block])
        gates[parts[i], :] = jnp.where(mine, jax.nn.sigmoid(score), 0.0).astype(BF16)
    for i in range(blocks):
        sums[parts[i], :] = jnp.dot(
            gates[parts[i], :], values[i], preferred_element_type=F32
        ).astype(sums.dtype)


def aggregate(outer, first, shift, me, rel, count, bias, merch_slot, feats, wq, keys, values, dtype):
    blocks, width, block_len = keys.shape
    rows = feats.shape[0] * blocks // (merch_slot.shape[0] // 2)
    return pl.pallas_call(
        functools.partial(aggregate_kernel, outer, first, shift),
        out_shape=jax.ShapeDtypeStruct((rows, width), dtype),
        in_specs=[SMEM] * 4 + [VMEM] * 5,
        out_specs=VMEM,
        scratch_shapes=[
            pltpu.VMEM((rows, width), BF16),
            pltpu.VMEM((rows, block_len), BF16),
        ],
        compiler_params=_mb(6),
        cost_estimate=_cost(
            4 * rows * block_len * width + 2 * rows * width * width, 6 * 2**20, rows * block_len
        ),
        name="aggregate_odd" if shift else "aggregate_even",
    )(me, rel, count, bias, merch_slot, feats, wq, keys, values)


def combine_kernel(skip, mine, other, *outs):
    rows = outs[0].shape[0]
    for j, out in enumerate(outs):
        part = slice(j * rows, (j + 1) * rows)
        theirs = slice(skip + j * rows, skip + (j + 1) * rows)
        out[...] = (mine[part, :] + other[theirs, :].astype(F32)).astype(out.dtype)


def combine(groups, skip, mine, other, dtype):
    rows, width = mine.shape
    return pl.pallas_call(
        functools.partial(combine_kernel, skip),
        out_shape=(jax.ShapeDtypeStruct((rows // groups, width), dtype),) * groups,
        in_specs=[VMEM, VMEM],
        out_specs=(VMEM,) * groups,
        compiler_params=_mb(2),
        cost_estimate=_cost(0, 2 * 2**20),
        name="combine_cores",
    )(mine, other)


def halve_kernel(rows, *refs):
    ins, keep, send = refs[:-2], refs[-2], refs[-1]
    for k in range(ins[0].shape[0] // rows):
        part = slice(k * rows, (k + 1) * rows)
        total = ins[0][part, :]
        for other in ins[1:]:
            total = total + other[part, :].astype(F32)
        to = slice(k // 2 * rows, (k // 2 + 1) * rows)
        if k % 2:
            send[to, :] = total.astype(BF16)
        else:
            keep[to, :] = total


def halve(rows, parts):
    held, width = parts[0].shape
    return pl.pallas_call(
        functools.partial(halve_kernel, rows),
        out_shape=(
            jax.ShapeDtypeStruct((held // 2, width), F32),
            jax.ShapeDtypeStruct((held // 2, width), BF16),
        ),
        in_specs=[VMEM] * len(parts),
        out_specs=(VMEM, VMEM),
        compiler_params=_mb(2),
        cost_estimate=_cost(0, 2**20),
        name="halve_sums",
    )(*parts)


def finish_kernel(feat, gain, wo, mine, other, out):
    total = mine[...] + other[...].astype(F32)
    update = feat[...].astype(F32) + jnp.dot(
        total.astype(BF16), wo[...], preferred_element_type=F32
    )
    scale = lax.rsqrt(jnp.mean(update * update, axis=-1, keepdims=True) + 1e-06)
    out[...] = (update * scale * gain[...]).astype(BF16)


def finish(feat, gain, wo, mine, other):
    return pl.pallas_call(
        finish_kernel,
        out_shape=jax.ShapeDtypeStruct(feat.shape, BF16),
        in_specs=[VMEM] * 5,
        out_specs=VMEM,
        compiler_params=_mb(2),
        name="finish",
    )(feat, gain.reshape(1, -1), wo, mine, other)


def per_device(
    acct_feat,
    merch_feat,
    key_weight,
    msg_weight,
    query_weight,
    out_weight,
    rel_bias,
    out_gain,
    slot_acct,
    slot_merch,
    block_rel,
    block_count,
):
    devices = lax.axis_size(AXES)
    me = lax.axis_index(AXES).astype(jnp.int32).reshape(1)
    inner = 4
    outer = devices // (2 * inner)

    def swap(value, mask):
        return lax.ppermute(value, AXES, [(s, s ^ mask) for s in range(devices)])

    def after(value, *others):
        return lax.optimization_barrier((value,) + others)[0]

    feats = jnp.concatenate([swap(merch_feat, 8 * k + 1) for k in range(outer)], axis=0)
    rows = gather(outer, me, slot_acct, acct_feat)
    feats = after(feats, rows[0])
    feats = jnp.concatenate([feats] + [swap(feats, 2 * j) for j in range(1, inner)], axis=0)

    weights = (key_weight, msg_weight)
    rest = (block_rel, block_count, rel_bias, slot_merch)
    blocks = inner * outer
    odd_keys, odd_values, far_keys, far_values = project(
        outer, ((0, blocks, 1), (outer, blocks, 0)), me, block_rel, rows, *weights
    )
    feats = after(feats, far_keys)
    even_feats = swap(feats, 1)
    odd = aggregate(outer, 0, 1, me, *rest, feats, query_weight, odd_keys, odd_values, BF16)
    other = swap(odd, 1)
    far = aggregate(
        outer, outer, 0, me, *rest, even_feats, query_weight, far_keys, far_values, F32
    )
    parts = combine(inner - 1, outer * merch_feat.shape[0], far, other, BF16)

    here = after(me, *parts)
    near_keys, near_values = project(
        outer, ((0, outer, 0),), here, block_rel, rows[1:], *weights
    )
    near = aggregate(
        outer, 0, 0, here, *rest, even_feats, query_weight, near_keys, near_values, F32
    )
    (near,) = combine(1, 0, near, other, F32)
    parts = [near] + [swap(parts[j - 1], 2 * j) for j in reversed(range(1, inner))]
    mask = 8
    while mask < devices:
        keep, send = halve(merch_feat.shape[0], parts)
        parts = [keep, swap(send, mask)]
        mask *= 2
    return finish(merch_feat, out_gain, out_weight, *parts)


def solution(mesh):
    placed = (
        P(("acct", "merch"), None),
        P(("acct", "merch"), None),
        P(),
        P(),
        P(),
        P(),
        P(),
        P(),
        P(("acct", "merch"), None),
        P(("acct", "merch"), None),
        P(("acct", "merch")),
        P(("acct", "merch")),
    )
    return jax.shard_map(
        per_device,
        mesh=mesh,
        in_specs=placed,
        out_specs=P(("acct", "merch"), None),
        check_vma=False,
    )
```

```python
import functools
import math

import jax
import jax.numpy as jnp
from jax import lax
from jax.experimental import pallas as pl
from jax.experimental.pallas import tpu as pltpu
from jax.sharding import PartitionSpec as P

AXES = ("acct", "merch")
LANES = 128
F32 = jnp.float32
BF16 = jnp.bfloat16
SMEM = pl.BlockSpec(memory_space=pltpu.SMEM)
ANY = pl.BlockSpec(memory_space=pl.ANY)
VMEM = pl.BlockSpec(memory_space=pltpu.VMEM)


def _mb(n):
    return pltpu.CompilerParams(vmem_limit_bytes=n * 2**20)


def _cost(flops, bytes_accessed, transcendentals=0):
    return pl.CostEstimate(
        flops=int(flops), bytes_accessed=int(bytes_accessed), transcendentals=transcendentals
    )


def _offset(i, outer):
    return (i // outer) * 2 + (i % outer) * 8


def project_kernel(
    outer, me_ref, rel_ref, slots_ref, acct_hbm, kw_hbm, mw_hbm,
    odd_keys, odd_values, even_keys, even_values,
    acct, kw, mw, table, odd_rows, even_rows, odd_feats, even_feats, a_sem, w_sem,
):
    accounts, width = acct.shape
    blocks, block_len, _ = odd_values.shape
    parts = width // LANES
    wide = 256
    group = 2 * block_len * wide // (4 * width)
    me = me_ref[0]
    chunks = a_sem.shape[0]
    chunk = accounts // chunks
    copies = [
        pltpu.make_async_copy(
            acct_hbm.at[pl.ds(i * chunk, chunk)], acct.at[pl.ds(i * chunk, chunk)], a_sem.at[i]
        )
        for i in range(chunks)
    ]
    weight_copies = [
        pltpu.make_async_copy(kw_hbm, kw, w_sem.at[0]),
        pltpu.make_async_copy(mw_hbm, mw, w_sem.at[1]),
    ]
    for copy in copies + weight_copies:
        copy.start()
    for i in range(chunks):
        copies[i].wait()

        @pl.loop(0, chunk // 16, unroll=4)
        def _(g):
            first = pl.multiple_of(i * chunk + g * 16, 16)
            tile = acct[pl.ds(first, 16), :].astype(F32)
            for c in range(parts):
                table[pl.ds(first * parts + c, 16, stride=parts), :] = tile[
                    :, c * LANES : (c + 1) * LANES
                ]

    def collect(block, rows, first, last):
        start = block * block_len
        found = []
        for k in range(first, last):
            source = pl.multiple_of(slots_ref[start + k] * parts, parts)
            found.append(table[pl.ds(source, parts), :])
        for k in range(first, last):
            rows[k * parts : (k + 1) * parts, :] = found[k - first]

    def emit(rows, out):
        for c in range(parts):
            out[:, c * LANES : (c + 1) * LANES] = rows[
                pl.ds(c, block_len, stride=parts), :
            ].astype(BF16)

    collect(jnp.bitwise_xor(me, 1), odd_rows, 0, block_len)
    collect(me, even_rows, 0, block_len)
    for copy in weight_copies:
        copy.wait()

    @pl.loop(0, blocks)
    def _(i):
        emit(odd_rows, odd_feats)
        emit(even_rows, even_feats)
        offset = _offset(i, outer)
        ahead = _offset(jnp.minimum(i + 1, blocks - 1), outer)
        step = 0
        for shift, feats, rows, keys, values in (
            (1, odd_feats, odd_rows, odd_keys, odd_values),
            (0, even_feats, even_rows, even_keys, even_values),
        ):
            relation = rel_ref[jnp.bitwise_xor(me, offset + shift)]
            nearby = jnp.bitwise_xor(me, ahead + shift)
            step = 0
            for weight, transposed, out in ((kw, True, keys), (mw, False, values)):
                for n in range(0, width, wide):
                    result = jnp.dot(
                        feats[...], weight[relation, :, n : n + wide], preferred_element_type=F32
                    ).astype(BF16)
                    collect(nearby, rows, step * group, (step + 1) * group)
                    step += 1
                    if transposed:
                        out[i, n : n + wide, :] = result.T
                    else:
                        out[i, :, n : n + wide] = result


def project(outer, me, rel, slots, acct, kw, mw):
    blocks, block_len = slots.shape
    accounts, width = acct.shape
    parts = width // LANES
    rows = pltpu.VMEM((block_len * parts, LANES), F32)
    feats = pltpu.VMEM((block_len, width), BF16)
    keys = jax.ShapeDtypeStruct((blocks // 2, width, block_len), BF16)
    values = jax.ShapeDtypeStruct((blocks // 2, block_len, width), BF16)
    return pl.pallas_call(
        functools.partial(project_kernel, outer),
        out_shape=(keys, values, keys, values),
        in_specs=[SMEM] * 3 + [ANY] * 3,
        out_specs=(VMEM,) * 4,
        scratch_shapes=[
            pltpu.VMEM(acct.shape, BF16),
            pltpu.VMEM(kw.shape, BF16),
            pltpu.VMEM(mw.shape, BF16),
            pltpu.VMEM((accounts * parts, LANES), F32),
            rows,
            rows,
            feats,
            feats,
            pltpu.SemaphoreType.DMA((8,)),
            pltpu.SemaphoreType.DMA((2,)),
        ],
        compiler_params=_mb(44 if blocks <= 32 else 50),
        cost_estimate=_cost(4 * blocks * block_len * width * width, 40 * 2**20),
        name="project_slots",
    )(me, rel, slots.reshape(-1), acct, kw, mw)


def assemble_kernel(*refs):
    rows = refs[0].shape[0]
    for i, part in enumerate(refs[:-1]):
        refs[-1][i * rows : (i + 1) * rows, :] = part[...]


def assemble(parts):
    rows, width = parts[0].shape
    return pl.pallas_call(
        assemble_kernel,
        out_shape=jax.ShapeDtypeStruct((len(parts) * rows, width), parts[0].dtype),
        in_specs=[VMEM] * len(parts),
        out_specs=VMEM,
        compiler_params=_mb(2),
        cost_estimate=_cost(1, 1),
        name="assemble",
    )(*parts)


def aggregate_kernel(
    outer, first, shift, me_ref, rel_ref, count_ref, bias_ref, merch_slot, feats, wq, keys, values,
    sums, query, gates,
):
    blocks, width, block_len = keys.shape
    merchants = sums.shape[0] // blocks
    me = me_ref[0]
    row = lax.broadcasted_iota(jnp.int32, (merchants, block_len), 0)
    lane = lax.broadcasted_iota(jnp.int32, (merchants, block_len), 1)
    query[...] = jnp.dot(
        feats[first * merchants : (first + blocks) * merchants, :],
        wq[...],
        preferred_element_type=F32,
    ).astype(BF16)
    parts = [slice(i * merchants, (i + 1) * merchants) for i in range(blocks)]
    for i in range(blocks):
        block = jnp.bitwise_xor(me, _offset(first + i, outer) + shift)
        score = jnp.dot(query[parts[i], :], keys[i], preferred_element_type=F32) / math.sqrt(width)
        score = score + bias_ref[rel_ref[block]]
        mine = (merch_slot[pl.ds(block, 1), :] == row) & (lane < count_ref[block])
        gates[parts[i], :] = jnp.where(mine, jax.nn.sigmoid(score), 0.0).astype(BF16)
    for i in range(blocks):
        sums[parts[i], :] = jnp.dot(
            gates[parts[i], :], values[i], preferred_element_type=F32
        ).astype(sums.dtype)


def aggregate(outer, first, shift, me, rel, count, bias, merch_slot, feats, wq, keys, values, dtype):
    blocks, width, block_len = keys.shape
    rows = feats.shape[0] * blocks // (merch_slot.shape[0] // 2)
    return pl.pallas_call(
        functools.partial(aggregate_kernel, outer, first, shift),
        out_shape=jax.ShapeDtypeStruct((rows, width), dtype),
        in_specs=[SMEM] * 4 + [VMEM] * 5,
        out_specs=VMEM,
        scratch_shapes=[
            pltpu.VMEM((rows, width), BF16),
            pltpu.VMEM((rows, block_len), BF16),
        ],
        compiler_params=_mb(6),
        cost_estimate=_cost(
            4 * rows * block_len * width + 2 * rows * width * width, 6 * 2**20, rows * block_len
        ),
        name="aggregate_odd" if shift else "aggregate_even",
    )(me, rel, count, bias, merch_slot, feats, wq, keys, values)


def combine_kernel(skip, mine, other, *outs):
    rows = outs[0].shape[0]
    for j, out in enumerate(outs):
        part = slice(j * rows, (j + 1) * rows)
        theirs = slice(skip + j * rows, skip + (j + 1) * rows)
        out[...] = (mine[part, :] + other[theirs, :].astype(F32)).astype(out.dtype)


def combine(groups, skip, mine, other):
    rows, width = mine.shape
    return pl.pallas_call(
        functools.partial(combine_kernel, skip),
        out_shape=tuple(
            jax.ShapeDtypeStruct((rows // groups, width), BF16 if j else F32)
            for j in range(groups)
        ),
        in_specs=[VMEM, VMEM],
        out_specs=(VMEM,) * groups,
        compiler_params=_mb(2),
        cost_estimate=_cost(0, 2 * 2**20),
        name="combine_cores",
    )(mine, other)


def plane_kernel(inner, *refs):
    ins, outs = refs[:inner], refs[inner:]
    rows = outs[0].shape[0]
    for k, out in enumerate(outs):
        part = slice(k * rows, (k + 1) * rows)
        total = ins[0][part, :]
        for other in ins[1:]:
            total = total + other[part, :].astype(F32)
        out[...] = total.astype(out.dtype)


def combine_plane(outer, parts):
    rows, width = parts[0].shape
    return pl.pallas_call(
        functools.partial(plane_kernel, len(parts)),
        out_shape=tuple(
            jax.ShapeDtypeStruct((rows // outer, width), F32 if k == 0 else BF16)
            for k in range(outer)
        ),
        in_specs=[VMEM] * len(parts),
        out_specs=(VMEM,) * outer,
        compiler_params=_mb(2),
        cost_estimate=_cost(0, 2**20),
        name="combine_plane",
    )(*parts)


def finish_kernel(feat, gain, wo, *refs):
    out = refs[-1]
    total = refs[0][...]
    for part in refs[1:-1]:
        total = total + part[...].astype(F32)
    update = feat[...].astype(F32) + jnp.dot(
        total.astype(BF16), wo[...], preferred_element_type=F32
    )
    scale = lax.rsqrt(jnp.mean(update * update, axis=-1, keepdims=True) + 1e-06)
    out[...] = (update * scale * gain[...]).astype(BF16)


def finish(feat, gain, wo, parts):
    return pl.pallas_call(
        finish_kernel,
        out_shape=jax.ShapeDtypeStruct(feat.shape, BF16),
        in_specs=[VMEM] * (3 + len(parts)),
        out_specs=VMEM,
        compiler_params=_mb(2),
        name="finish",
    )(feat, gain.reshape(1, -1), wo, *parts)


def per_device(
    acct_feat,
    merch_feat,
    key_weight,
    msg_weight,
    query_weight,
    out_weight,
    rel_bias,
    out_gain,
    slot_acct,
    slot_merch,
    block_rel,
    block_count,
):
    devices = lax.axis_size(AXES)
    me = lax.axis_index(AXES).astype(jnp.int32).reshape(1)
    inner = 4
    outer = devices // (2 * inner)

    def swap(value, mask):
        return lax.ppermute(value, AXES, [(s, s ^ mask) for s in range(devices)])

    def after(value, *others):
        return lax.optimization_barrier((value,) + others)[0]

    feats = jnp.concatenate([swap(merch_feat, 8 * k + 1) for k in range(outer)], axis=0)
    here = after(me, feats)
    feats = [feats] + [swap(feats, 2 * j) for j in range(1, inner)]
    odd_keys, odd_values, even_keys, even_values = project(
        outer, here, block_rel, slot_acct, acct_feat, key_weight, msg_weight
    )
    feats = assemble(after(tuple(feats), odd_keys))
    even_feats = swap(feats, 1)

    rest = (block_rel, block_count, rel_bias, slot_merch)
    odd = aggregate(outer, 0, 1, me, *rest, feats, query_weight, odd_keys, odd_values, BF16)
    other = swap(odd, 1)
    even = aggregate(
        outer, 0, 0, me, *rest, even_feats, query_weight, even_keys, even_values, F32
    )
    parts = combine(inner, 0, even, other)
    parts = combine_plane(
        outer, [parts[0]] + [swap(parts[j], 2 * j) for j in reversed(range(1, inner))]
    )
    parts = [parts[0]] + [swap(parts[k], 8 * k) for k in reversed(range(1, outer))]
    return finish(merch_feat, out_gain, out_weight, parts)


def solution(mesh):
    placed = (
        P(("acct", "merch"), None),
        P(("acct", "merch"), None),
        P(),
        P(),
        P(),
        P(),
        P(),
        P(),
        P(("acct", "merch"), None),
        P(("acct", "merch"), None),
        P(("acct", "merch")),
        P(("acct", "merch")),
    )
    return jax.shard_map(
        per_device,
        mesh=mesh,
        in_specs=placed,
        out_specs=P(("acct", "merch"), None),
        check_vma=False,
    )
```

```python
import functools
import math

import jax
import jax.numpy as jnp
from jax import lax
from jax.experimental import pallas as pl
from jax.experimental.pallas import tpu as pltpu
from jax.sharding import PartitionSpec as P

AXES = ("acct", "merch")
LANES = 128
F32 = jnp.float32
BF16 = jnp.bfloat16
SMEM = pl.BlockSpec(memory_space=pltpu.SMEM)
ANY = pl.BlockSpec(memory_space=pl.ANY)
VMEM = pl.BlockSpec(memory_space=pltpu.VMEM)


def _mb(n):
    return pltpu.CompilerParams(vmem_limit_bytes=n * 2**20)


def _cost(flops, bytes_accessed, transcendentals=0):
    return pl.CostEstimate(
        flops=int(flops), bytes_accessed=int(bytes_accessed), transcendentals=transcendentals
    )


def _offset(i, outer):
    return (i // outer) * 2 + (i % outer) * 8


def project_kernel(
    outer, me_ref, rel_ref, slots_ref, acct_hbm, kw_hbm, mw_hbm,
    odd_keys, odd_values, even_keys, even_values,
    acct, kw, mw, table, odd_rows, even_rows, odd_feats, even_feats, a_sem, w_sem,
):
    accounts, width = acct.shape
    blocks, block_len, _ = odd_values.shape
    parts = width // LANES
    wide = 256
    group = 2 * block_len * wide // (4 * width)
    me = me_ref[0]
    chunks = a_sem.shape[0]
    chunk = accounts // chunks
    copies = [
        pltpu.make_async_copy(
            acct_hbm.at[pl.ds(i * chunk, chunk)], acct.at[pl.ds(i * chunk, chunk)], a_sem.at[i]
        )
        for i in range(chunks)
    ]
    weight_copies = [
        pltpu.make_async_copy(kw_hbm, kw, w_sem.at[0]),
        pltpu.make_async_copy(mw_hbm, mw, w_sem.at[1]),
    ]
    for copy in copies + weight_copies:
        copy.start()
    for i in range(chunks):
        copies[i].wait()

        @pl.loop(0, chunk // 16, unroll=4)
        def _(g):
            first = pl.multiple_of(i * chunk + g * 16, 16)
            tile = acct[pl.ds(first, 16), :].astype(F32)
            for c in range(parts):
                table[pl.ds(first * parts + c, 16, stride=parts), :] = tile[
                    :, c * LANES : (c + 1) * LANES
                ]

    def collect(block, rows, first, last):
        start = block * block_len
        for k in range(first, last):
            source = pl.multiple_of(slots_ref[start + k] * parts, parts)
            rows[k * parts : (k + 1) * parts, :] = table[pl.ds(source, parts), :]

    def emit(rows, out, c):
        out[:, c * LANES : (c + 1) * LANES] = rows[pl.ds(c, block_len, stride=parts), :].astype(
            BF16
        )

    collect(jnp.bitwise_xor(me, 1), odd_rows, 0, block_len)
    collect(me, even_rows, 0, block_len)
    for c in range(parts):
        emit(odd_rows, odd_feats, c)
    for copy in weight_copies:
        copy.wait()

    def phase(i, shift, feats, rows, keys, values, idle_rows, idle_feats):
        relation = rel_ref[jnp.bitwise_xor(me, _offset(i, outer) + shift)]
        ahead = _offset(jnp.minimum(i + 1, blocks - 1), outer) + shift
        nearby = jnp.bitwise_xor(me, ahead)
        step = 0
        for weight, transposed, out in ((kw, True, keys), (mw, False, values)):
            for n in range(0, width, wide):
                result = jnp.dot(
                    feats[...], weight[relation, :, n : n + wide], preferred_element_type=F32
                ).astype(BF16)
                collect(nearby, rows, step * group, (step + 1) * group)
                for c in range(step * parts * wide // (2 * width), (step + 1) * parts * wide // (2 * width)):
                    emit(idle_rows, idle_feats, c)
                step += 1
                if transposed:
                    out[i, n : n + wide, :] = result.T
                else:
                    out[i, :, n : n + wide] = result

    @pl.loop(0, blocks)
    def _(i):
        phase(i, 1, odd_feats, odd_rows, odd_keys, odd_values, even_rows, even_feats)
        phase(i, 0, even_feats, even_rows, even_keys, even_values, odd_rows, odd_feats)


def project(outer, me, rel, slots, acct, kw, mw):
    blocks = rel.shape[0]
    block_len = slots.shape[0] // blocks
    accounts, width = acct.shape
    parts = width // LANES
    rows = pltpu.VMEM((block_len * parts, LANES), F32)
    feats = pltpu.VMEM((block_len, width), BF16)
    keys = jax.ShapeDtypeStruct((blocks // 2, width, block_len), BF16)
    values = jax.ShapeDtypeStruct((blocks // 2, block_len, width), BF16)
    return pl.pallas_call(
        functools.partial(project_kernel, outer),
        out_shape=(keys, values, keys, values),
        in_specs=[SMEM] * 3 + [ANY] * 3,
        out_specs=(VMEM,) * 4,
        scratch_shapes=[
            pltpu.VMEM(acct.shape, BF16),
            pltpu.VMEM(kw.shape, BF16),
            pltpu.VMEM(mw.shape, BF16),
            pltpu.VMEM((accounts * parts, LANES), F32),
            rows,
            rows,
            feats,
            feats,
            pltpu.SemaphoreType.DMA((8,)),
            pltpu.SemaphoreType.DMA((2,)),
        ],
        compiler_params=_mb(44 if blocks <= 32 else 50),
        cost_estimate=_cost(4 * blocks * block_len * width * width, 40 * 2**20),
        name="project_slots",
    )(me, rel, slots, acct, kw, mw)


def stage_kernel(rel, slots, rel_out, slots_out):
    rel_out[...] = rel[...]
    slots_out[...] = slots[...]


def stage(rel, slots):
    return pl.pallas_call(
        stage_kernel,
        out_shape=tuple(jax.ShapeDtypeStruct(x.shape, x.dtype) for x in (rel, slots)),
        in_specs=[VMEM, VMEM],
        out_specs=(VMEM, VMEM),
        compiler_params=_mb(2),
        cost_estimate=_cost(0, 2**16),
        name="stage_indices",
    )(rel, slots)


def assemble_kernel(*refs):
    rows = refs[0].shape[0]
    for i, part in enumerate(refs[:-1]):
        refs[-1][i * rows : (i + 1) * rows, :] = part[...]


def assemble(parts):
    rows, width = parts[0].shape
    return pl.pallas_call(
        assemble_kernel,
        out_shape=jax.ShapeDtypeStruct((len(parts) * rows, width), parts[0].dtype),
        in_specs=[VMEM] * len(parts),
        out_specs=VMEM,
        compiler_params=_mb(2),
        cost_estimate=_cost(1, 1),
        name="assemble",
    )(*parts)


def aggregate_kernel(
    outer, first, shift, me_ref, rel_ref, count_ref, bias_ref, merch_slot, feats, wq, keys, values,
    sums, query, gates,
):
    blocks, width, block_len = keys.shape
    merchants = sums.shape[0] // blocks
    me = me_ref[0]
    row = lax.broadcasted_iota(jnp.int32, (merchants, block_len), 0)
    lane = lax.broadcasted_iota(jnp.int32, (merchants, block_len), 1)
    query[...] = jnp.dot(
        feats[first * merchants : (first + blocks) * merchants, :],
        wq[...],
        preferred_element_type=F32,
    ).astype(BF16)
    parts = [slice(i * merchants, (i + 1) * merchants) for i in range(blocks)]
    for i in range(blocks):
        block = jnp.bitwise_xor(me, _offset(first + i, outer) + shift)
        score = jnp.dot(query[parts[i], :], keys[i], preferred_element_type=F32) / math.sqrt(width)
        score = score + bias_ref[rel_ref[block]]
        mine = (merch_slot[pl.ds(block, 1), :] == row) & (lane < count_ref[block])
        gates[parts[i], :] = jnp.where(mine, jax.nn.sigmoid(score), 0.0).astype(BF16)
    for i in range(blocks):
        sums[parts[i], :] = jnp.dot(
            gates[parts[i], :], values[i], preferred_element_type=F32
        ).astype(sums.dtype)


def aggregate(outer, first, shift, me, rel, count, bias, merch_slot, feats, wq, keys, values, dtype):
    blocks, width, block_len = keys.shape
    rows = feats.shape[0] * blocks // (merch_slot.shape[0] // 2)
    return pl.pallas_call(
        functools.partial(aggregate_kernel, outer, first, shift),
        out_shape=jax.ShapeDtypeStruct((rows, width), dtype),
        in_specs=[SMEM] * 4 + [VMEM] * 5,
        out_specs=VMEM,
        scratch_shapes=[
            pltpu.VMEM((rows, width), BF16),
            pltpu.VMEM((rows, block_len), BF16),
        ],
        compiler_params=_mb(6),
        cost_estimate=_cost(
            4 * rows * block_len * width + 2 * rows * width * width, 6 * 2**20, rows * block_len
        ),
        name="aggregate_odd" if shift else "aggregate_even",
    )(me, rel, count, bias, merch_slot, feats, wq, keys, values)


def combine_kernel(skip, mine, other, *outs):
    rows = outs[0].shape[0]
    for j, out in enumerate(outs):
        part = slice(j * rows, (j + 1) * rows)
        theirs = slice(skip + j * rows, skip + (j + 1) * rows)
        out[...] = (mine[part, :] + other[theirs, :].astype(F32)).astype(out.dtype)


def combine(groups, skip, mine, other):
    rows, width = mine.shape
    return pl.pallas_call(
        functools.partial(combine_kernel, skip),
        out_shape=tuple(
            jax.ShapeDtypeStruct((rows // groups, width), BF16 if j else F32)
            for j in range(groups)
        ),
        in_specs=[VMEM, VMEM],
        out_specs=(VMEM,) * groups,
        compiler_params=_mb(2),
        cost_estimate=_cost(0, 2 * 2**20),
        name="combine_cores",
    )(mine, other)


def plane_kernel(inner, *refs):
    ins, outs = refs[:inner], refs[inner:]
    rows = outs[0].shape[0]
    for k, out in enumerate(outs):
        part = slice(k * rows, (k + 1) * rows)
        total = ins[0][part, :]
        for other in ins[1:]:
            total = total + other[part, :].astype(F32)
        out[...] = total.astype(out.dtype)


def combine_plane(outer, parts):
    rows, width = parts[0].shape
    return pl.pallas_call(
        functools.partial(plane_kernel, len(parts)),
        out_shape=tuple(
            jax.ShapeDtypeStruct((rows // outer, width), F32 if k == 0 else BF16)
            for k in range(outer)
        ),
        in_specs=[VMEM] * len(parts),
        out_specs=(VMEM,) * outer,
        compiler_params=_mb(2),
        cost_estimate=_cost(0, 2**20),
        name="combine_plane",
    )(*parts)


def finish_kernel(feat, gain, wo, *refs):
    out = refs[-1]
    total = refs[0][...]
    for part in refs[1:-1]:
        total = total + part[...].astype(F32)
    update = feat[...].astype(F32) + jnp.dot(
        total.astype(BF16), wo[...], preferred_element_type=F32
    )
    scale = lax.rsqrt(jnp.mean(update * update, axis=-1, keepdims=True) + 1e-06)
    out[...] = (update * scale * gain[...]).astype(BF16)


def finish(feat, gain, wo, parts):
    return pl.pallas_call(
        finish_kernel,
        out_shape=jax.ShapeDtypeStruct(feat.shape, BF16),
        in_specs=[VMEM] * (3 + len(parts)),
        out_specs=VMEM,
        compiler_params=_mb(2),
        name="finish",
    )(feat, gain.reshape(1, -1), wo, *parts)


def per_device(
    acct_feat,
    merch_feat,
    key_weight,
    msg_weight,
    query_weight,
    out_weight,
    rel_bias,
    out_gain,
    slot_acct,
    slot_merch,
    block_rel,
    block_count,
):
    devices = lax.axis_size(AXES)
    me = lax.axis_index(AXES).astype(jnp.int32).reshape(1)
    inner = 4
    outer = devices // (2 * inner)

    def swap(value, mask):
        return lax.ppermute(value, AXES, [(s, s ^ mask) for s in range(devices)])

    def after(value, *others):
        return lax.optimization_barrier((value,) + others)[0]

    feats = jnp.concatenate([swap(merch_feat, 8 * k + 1) for k in range(outer)], axis=0)
    staged_rel, staged_slots = stage(block_rel, slot_acct)
    feats = after(feats, staged_rel)
    here = after(me, feats)
    feats = [feats] + [swap(feats, 2 * j) for j in range(1, inner)]
    odd_keys, odd_values, even_keys, even_values = project(
        outer, here, staged_rel, staged_slots.reshape(-1), acct_feat, key_weight, msg_weight
    )
    feats = assemble(after(tuple(feats), odd_keys))
    even_feats = swap(feats, 1)

    rest = (block_rel, block_count, rel_bias, slot_merch)
    odd = aggregate(outer, 0, 1, me, *rest, feats, query_weight, odd_keys, odd_values, BF16)
    other = swap(odd, 1)
    even = aggregate(
        outer, 0, 0, me, *rest, even_feats, query_weight, even_keys, even_values, F32
    )
    parts = combine(inner, 0, even, other)
    parts = combine_plane(
        outer, [parts[0]] + [swap(parts[j], 2 * j) for j in reversed(range(1, inner))]
    )
    parts = [parts[0]] + [swap(parts[k], 8 * k) for k in reversed(range(1, outer))]
    return finish(merch_feat, out_gain, out_weight, parts)


def solution(mesh):
    placed = (
        P(("acct", "merch"), None),
        P(("acct", "merch"), None),
        P(),
        P(),
        P(),
        P(),
        P(),
        P(),
        P(("acct", "merch"), None),
        P(("acct", "merch"), None),
        P(("acct", "merch")),
        P(("acct", "merch")),
    )
    return jax.shard_map(
        per_device,
        mesh=mesh,
        in_specs=placed,
        out_specs=P(("acct", "merch"), None),
        check_vma=False,
    )
```

```python
import functools
import math

import jax
import jax.numpy as jnp
from jax import lax
from jax.experimental import pallas as pl
from jax.experimental.pallas import tpu as pltpu
from jax.sharding import PartitionSpec as P

AXES = ("acct", "merch")
LANES = 128
F32 = jnp.float32
BF16 = jnp.bfloat16
SMEM = pl.BlockSpec(memory_space=pltpu.SMEM)
ANY = pl.BlockSpec(memory_space=pl.ANY)
VMEM = pl.BlockSpec(memory_space=pltpu.VMEM)


def _mb(n):
    return pltpu.CompilerParams(vmem_limit_bytes=n * 2**20)


def _cost(flops, bytes_accessed, transcendentals=0):
    return pl.CostEstimate(
        flops=int(flops), bytes_accessed=int(bytes_accessed), transcendentals=transcendentals
    )


def _offset(i, outer):
    return (i // outer) * 2 + (i % outer) * 8


def project_kernel(
    outer, me_ref, rel_ref, slots_ref, acct_hbm, kw_hbm, mw_hbm,
    odd_keys, odd_values, even_keys, even_values,
    acct, kw, mw, table, odd_rows, even_rows, odd_feats, even_feats, a_sem, w_sem,
):
    accounts, width = acct.shape
    blocks, block_len, _ = odd_values.shape
    parts = width // LANES
    wide = 256
    group = 2 * block_len * wide // (4 * width)
    me = me_ref[0]
    chunks = a_sem.shape[0]
    chunk = accounts // chunks
    copies = [
        pltpu.make_async_copy(
            acct_hbm.at[pl.ds(i * chunk, chunk)], acct.at[pl.ds(i * chunk, chunk)], a_sem.at[i]
        )
        for i in range(chunks)
    ]
    weight_copies = [
        pltpu.make_async_copy(kw_hbm, kw, w_sem.at[0]),
        pltpu.make_async_copy(mw_hbm, mw, w_sem.at[1]),
    ]
    for copy in copies + weight_copies:
        copy.start()
    for i in range(chunks):
        copies[i].wait()

        @pl.loop(0, chunk // 16, unroll=4)
        def _(g):
            first = pl.multiple_of(i * chunk + g * 16, 16)
            tile = acct[pl.ds(first, 16), :].astype(F32)
            for c in range(parts):
                table[pl.ds(first * parts + c, 16, stride=parts), :] = tile[
                    :, c * LANES : (c + 1) * LANES
                ]

    def collect(block, rows, first, last):
        start = block * block_len
        for low in range(first, last, 16):
            found = []
            for k in range(low, low + 16):
                source = pl.multiple_of(slots_ref[start + k] * parts, parts)
                found.append(table[pl.ds(source, parts), :])
            for k in range(low, low + 16):
                rows[k * parts : (k + 1) * parts, :] = found[k - low]

    def emit(rows, out, c):
        out[:, c * LANES : (c + 1) * LANES] = rows[pl.ds(c, block_len, stride=parts), :].astype(
            BF16
        )

    collect(jnp.bitwise_xor(me, 1), odd_rows, 0, block_len)
    collect(me, even_rows, 0, block_len)
    for c in range(parts):
        emit(odd_rows, odd_feats, c)
    for copy in weight_copies:
        copy.wait()

    def put(i, pending):
        out, n, transposed, result = pending
        if transposed:
            out[i, n : n + wide, :] = result.T
        else:
            out[i, :, n : n + wide] = result

    def phase(i, shift, feats, rows, keys, values, idle_rows, idle_feats, pending):
        relation = rel_ref[jnp.bitwise_xor(me, _offset(i, outer) + shift)]
        ahead = _offset(jnp.minimum(i + 1, blocks - 1), outer) + shift
        nearby = jnp.bitwise_xor(me, ahead)
        steps = 2 * width // wide
        for step in range(steps):
            transposed = step < steps // 2
            weight, out = (kw, keys) if transposed else (mw, values)
            n = step % (steps // 2) * wide
            result = jnp.dot(
                feats[...], weight[relation, :, n : n + wide], preferred_element_type=F32
            ).astype(BF16)
            collect(nearby, rows, step * group, (step + 1) * group)
            for c in range(step * parts // steps, (step + 1) * parts // steps):
                emit(idle_rows, idle_feats, c)
            if pending is not None:
                put(i, pending)
            pending = (out, n, transposed, result)
        return pending

    @pl.loop(0, blocks)
    def _(i):
        pending = phase(
            i, 1, odd_feats, odd_rows, odd_keys, odd_values, even_rows, even_feats, None
        )
        pending = phase(
            i, 0, even_feats, even_rows, even_keys, even_values, odd_rows, odd_feats, pending
        )
        put(i, pending)


def project(outer, me, rel, slots, acct, kw, mw):
    blocks = rel.shape[0]
    block_len = slots.shape[0] // blocks
    accounts, width = acct.shape
    parts = width // LANES
    rows = pltpu.VMEM((block_len * parts, LANES), F32)
    feats = pltpu.VMEM((block_len, width), BF16)
    keys = jax.ShapeDtypeStruct((blocks // 2, width, block_len), BF16)
    values = jax.ShapeDtypeStruct((blocks // 2, block_len, width), BF16)
    return pl.pallas_call(
        functools.partial(project_kernel, outer),
        out_shape=(keys, values, keys, values),
        in_specs=[SMEM] * 3 + [ANY] * 3,
        out_specs=(VMEM,) * 4,
        scratch_shapes=[
            pltpu.VMEM(acct.shape, BF16),
            pltpu.VMEM(kw.shape, BF16),
            pltpu.VMEM(mw.shape, BF16),
            pltpu.VMEM((accounts * parts, LANES), F32),
            rows,
            rows,
            feats,
            feats,
            pltpu.SemaphoreType.DMA((8,)),
            pltpu.SemaphoreType.DMA((2,)),
        ],
        compiler_params=_mb(44 if blocks <= 32 else 50),
        cost_estimate=_cost(4 * blocks * block_len * width * width, 40 * 2**20),
        name="project_slots",
    )(me, rel, slots, acct, kw, mw)


def stage_kernel(rel, slots, rel_out, slots_out):
    rel_out[...] = rel[...]
    slots_out[...] = slots[...]


def stage(rel, slots):
    return pl.pallas_call(
        stage_kernel,
        out_shape=tuple(jax.ShapeDtypeStruct(x.shape, x.dtype) for x in (rel, slots)),
        in_specs=[VMEM, VMEM],
        out_specs=(VMEM, VMEM),
        compiler_params=_mb(2),
        cost_estimate=_cost(0, 2**16),
        name="stage_indices",
    )(rel, slots)


def assemble_kernel(*refs):
    rows = refs[0].shape[0]
    for i, part in enumerate(refs[:-1]):
        refs[-1][i * rows : (i + 1) * rows, :] = part[...]


def assemble(parts):
    rows, width = parts[0].shape
    return pl.pallas_call(
        assemble_kernel,
        out_shape=jax.ShapeDtypeStruct((len(parts) * rows, width), parts[0].dtype),
        in_specs=[VMEM] * len(parts),
        out_specs=VMEM,
        compiler_params=_mb(2),
        cost_estimate=_cost(1, 1),
        name="assemble",
    )(*parts)


def aggregate_kernel(
    outer, first, shift, me_ref, rel_ref, count_ref, bias_ref, merch_slot, feats, wq, keys, values,
    sums, query, gates,
):
    blocks, width, block_len = keys.shape
    merchants = sums.shape[0] // blocks
    me = me_ref[0]
    row = lax.broadcasted_iota(jnp.int32, (merchants, block_len), 0)
    lane = lax.broadcasted_iota(jnp.int32, (merchants, block_len), 1)
    query[...] = jnp.dot(
        feats[first * merchants : (first + blocks) * merchants, :],
        wq[...],
        preferred_element_type=F32,
    ).astype(BF16)
    parts = [slice(i * merchants, (i + 1) * merchants) for i in range(blocks)]
    for i in range(blocks):
        block = jnp.bitwise_xor(me, _offset(first + i, outer) + shift)
        score = jnp.dot(query[parts[i], :], keys[i], preferred_element_type=F32) / math.sqrt(width)
        score = score + bias_ref[rel_ref[block]]
        mine = (merch_slot[pl.ds(block, 1), :] == row) & (lane < count_ref[block])
        gates[parts[i], :] = jnp.where(mine, jax.nn.sigmoid(score), 0.0).astype(BF16)
    for i in range(blocks):
        sums[parts[i], :] = jnp.dot(
            gates[parts[i], :], values[i], preferred_element_type=F32
        ).astype(sums.dtype)


def aggregate(outer, first, shift, me, rel, count, bias, merch_slot, feats, wq, keys, values, dtype):
    blocks, width, block_len = keys.shape
    rows = feats.shape[0] * blocks // (merch_slot.shape[0] // 2)
    return pl.pallas_call(
        functools.partial(aggregate_kernel, outer, first, shift),
        out_shape=jax.ShapeDtypeStruct((rows, width), dtype),
        in_specs=[SMEM] * 4 + [VMEM] * 5,
        out_specs=VMEM,
        scratch_shapes=[
            pltpu.VMEM((rows, width), BF16),
            pltpu.VMEM((rows, block_len), BF16),
        ],
        compiler_params=_mb(6),
        cost_estimate=_cost(
            4 * rows * block_len * width + 2 * rows * width * width, 6 * 2**20, rows * block_len
        ),
        name="aggregate_odd" if shift else "aggregate_even",
    )(me, rel, count, bias, merch_slot, feats, wq, keys, values)


def combine_kernel(skip, mine, other, *outs):
    rows = outs[0].shape[0]
    for j, out in enumerate(outs):
        part = slice(j * rows, (j + 1) * rows)
        theirs = slice(skip + j * rows, skip + (j + 1) * rows)
        out[...] = (mine[part, :] + other[theirs, :].astype(F32)).astype(out.dtype)


def combine(groups, skip, mine, other):
    rows, width = mine.shape
    return pl.pallas_call(
        functools.partial(combine_kernel, skip),
        out_shape=tuple(
            jax.ShapeDtypeStruct((rows // groups, width), BF16 if j else F32)
            for j in range(groups)
        ),
        in_specs=[VMEM, VMEM],
        out_specs=(VMEM,) * groups,
        compiler_params=_mb(2),
        cost_estimate=_cost(0, 2 * 2**20),
        name="combine_cores",
    )(mine, other)


def plane_kernel(inner, *refs):
    ins, outs = refs[:inner], refs[inner:]
    rows = outs[0].shape[0]
    for k, out in enumerate(outs):
        part = slice(k * rows, (k + 1) * rows)
        total = ins[0][part, :]
        for other in ins[1:]:
            total = total + other[part, :].astype(F32)
        out[...] = total.astype(out.dtype)


def combine_plane(outer, parts):
    rows, width = parts[0].shape
    return pl.pallas_call(
        functools.partial(plane_kernel, len(parts)),
        out_shape=tuple(
            jax.ShapeDtypeStruct((rows // outer, width), F32 if k == 0 else BF16)
            for k in range(outer)
        ),
        in_specs=[VMEM] * len(parts),
        out_specs=(VMEM,) * outer,
        compiler_params=_mb(2),
        cost_estimate=_cost(0, 2**20),
        name="combine_plane",
    )(*parts)


def finish_kernel(feat, gain, wo, *refs):
    out = refs[-1]
    total = refs[0][...]
    for part in refs[1:-1]:
        total = total + part[...].astype(F32)
    update = feat[...].astype(F32) + jnp.dot(
        total.astype(BF16), wo[...], preferred_element_type=F32
    )
    scale = lax.rsqrt(jnp.mean(update * update, axis=-1, keepdims=True) + 1e-06)
    out[...] = (update * scale * gain[...]).astype(BF16)


def finish(feat, gain, wo, parts):
    return pl.pallas_call(
        finish_kernel,
        out_shape=jax.ShapeDtypeStruct(feat.shape, BF16),
        in_specs=[VMEM] * (3 + len(parts)),
        out_specs=VMEM,
        compiler_params=_mb(2),
        name="finish",
    )(feat, gain.reshape(1, -1), wo, *parts)


def per_device(
    acct_feat,
    merch_feat,
    key_weight,
    msg_weight,
    query_weight,
    out_weight,
    rel_bias,
    out_gain,
    slot_acct,
    slot_merch,
    block_rel,
    block_count,
):
    devices = lax.axis_size(AXES)
    me = lax.axis_index(AXES).astype(jnp.int32).reshape(1)
    inner = 4
    outer = devices // (2 * inner)

    def swap(value, mask):
        return lax.ppermute(value, AXES, [(s, s ^ mask) for s in range(devices)])

    def after(value, *others):
        return lax.optimization_barrier((value,) + others)[0]

    feats = jnp.concatenate([swap(merch_feat, 8 * k + 1) for k in range(outer)], axis=0)
    staged_rel, staged_slots = stage(block_rel, slot_acct)
    feats = after(feats, staged_rel)
    here = after(me, feats)
    feats = [feats] + [swap(feats, 2 * j) for j in range(1, inner)]
    odd_keys, odd_values, even_keys, even_values = project(
        outer, here, staged_rel, staged_slots.reshape(-1), acct_feat, key_weight, msg_weight
    )
    feats = assemble(after(tuple(feats), odd_keys))
    even_feats = swap(feats, 1)

    rest = (block_rel, block_count, rel_bias, slot_merch)
    odd = aggregate(outer, 0, 1, me, *rest, feats, query_weight, odd_keys, odd_values, BF16)
    other = swap(odd, 1)
    even = aggregate(
        outer, 0, 0, me, *rest, even_feats, query_weight, even_keys, even_values, F32
    )
    parts = combine(inner, 0, even, other)
    parts = combine_plane(
        outer, [parts[0]] + [swap(parts[j], 2 * j) for j in reversed(range(1, inner))]
    )
    parts = [parts[0]] + [swap(parts[k], 8 * k) for k in reversed(range(1, outer))]
    return finish(merch_feat, out_gain, out_weight, parts)


def solution(mesh):
    placed = (
        P(("acct", "merch"), None),
        P(("acct", "merch"), None),
        P(),
        P(),
        P(),
        P(),
        P(),
        P(),
        P(("acct", "merch"), None),
        P(("acct", "merch"), None),
        P(("acct", "merch")),
        P(("acct", "merch")),
    )
    return jax.shard_map(
        per_device,
        mesh=mesh,
        in_specs=placed,
        out_specs=P(("acct", "merch"), None),
        check_vma=False,
    )
```

```python
import functools
import math

import jax
import jax.numpy as jnp
from jax import lax
from jax.experimental import pallas as pl
from jax.experimental.pallas import tpu as pltpu
from jax.sharding import PartitionSpec as P

AXES = ("acct", "merch")
LANES = 128
F32 = jnp.float32
BF16 = jnp.bfloat16
SMEM = pl.BlockSpec(memory_space=pltpu.SMEM)
ANY = pl.BlockSpec(memory_space=pl.ANY)
VMEM = pl.BlockSpec(memory_space=pltpu.VMEM)


def _mb(n):
    return pltpu.CompilerParams(vmem_limit_bytes=n * 2**20)


def _cost(flops, bytes_accessed, transcendentals=0):
    return pl.CostEstimate(
        flops=int(flops), bytes_accessed=int(bytes_accessed), transcendentals=transcendentals
    )


def _offset(i, outer):
    return (i // outer) * 2 + (i % outer) * 8


def gather_kernel(
    outer, me_ref, slots_ref, acct_hbm, odd, even, acct, table, rows0, rows1, sem
):
    accounts, width = acct.shape
    blocks, block_len, _ = odd.shape
    parts = width // LANES
    pitch = table.shape[1]
    batch = 32
    flat = table.reshape(accounts * pitch, LANES)
    me = me_ref[0]
    chunks = sem.shape[0]
    chunk = accounts // chunks
    copies = [
        pltpu.make_async_copy(
            acct_hbm.at[pl.ds(i * chunk, chunk)], acct.at[pl.ds(i * chunk, chunk)], sem.at[i]
        )
        for i in range(chunks)
    ]
    for copy in copies:
        copy.start()
    for i in range(chunks):
        copies[i].wait()

        @pl.loop(0, chunk // 16, unroll=4)
        def _(g):
            first = pl.multiple_of(i * chunk + g * 16, 16)
            tile = acct[pl.ds(first, 16), :].astype(F32)
            for c in range(parts):
                flat[pl.ds(first * pitch + c, 16, stride=pitch), :] = tile[
                    :, c * LANES : (c + 1) * LANES
                ]

    def collect(block, rows):
        for k in range(0, block_len, batch):
            found = [table[slots_ref[block, k + u], :parts, :] for u in range(batch)]
            for u in range(batch):
                rows[(k + u) * parts : (k + u + 1) * parts, :] = found[u]

    def emit(i, rows, out):
        for c in range(parts):
            out[i, :, c * LANES : (c + 1) * LANES] = rows[
                pl.ds(c, block_len, stride=parts), :
            ].astype(BF16)

    @pl.loop(0, blocks)
    def _(i):
        offset = _offset(i, outer)
        collect(jnp.bitwise_xor(me, offset + 1), rows0)
        collect(jnp.bitwise_xor(me, offset), rows1)
        emit(i, rows0, odd)
        emit(i, rows1, even)


def gather(outer, me, slots, acct):
    blocks, block_len = slots.shape
    accounts, width = acct.shape
    parts = width // LANES
    pitch = -(-parts // 8) * 8
    rows = pltpu.VMEM((block_len * parts, LANES), F32)
    half = jax.ShapeDtypeStruct((blocks // 2, block_len, width), BF16)
    return pl.pallas_call(
        functools.partial(gather_kernel, outer),
        out_shape=(half, half),
        in_specs=[SMEM, SMEM, ANY],
        out_specs=(VMEM, VMEM),
        scratch_shapes=[
            pltpu.VMEM(acct.shape, BF16),
            pltpu.VMEM((accounts, pitch, LANES), F32),
            rows,
            rows,
            pltpu.SemaphoreType.DMA((8,)),
        ],
        compiler_params=_mb(47 if blocks <= 32 else 28),
        cost_estimate=_cost(0, 20 * 2**20),
        name="gather_slots",
    )(me, slots, acct)


def project_kernel(outer, spans, me_ref, rel_ref, kw, mw, *refs):
    width = refs[0].shape[2]
    half = width // 2
    me = me_ref[0]
    count = len(spans)

    def one(i, first, shift, feats, keys, values):
        relation = rel_ref[jnp.bitwise_xor(me, _offset(first + i, outer) + shift)]
        for n in range(0, width, half):
            key = jnp.dot(
                feats[first + i], kw[relation, :, n : n + half], preferred_element_type=F32
            )
            keys[i, n : n + half, :] = key.astype(BF16).T
            value = jnp.dot(
                feats[first + i], mw[relation, :, n : n + half], preferred_element_type=F32
            )
            values[i, :, n : n + half] = value.astype(BF16)

    for s, (first, last, shift) in enumerate(spans):
        outs = refs[count + 2 * s : count + 2 * s + 2]

        @pl.loop(0, last - first, unroll=4)
        def _(i):
            one(i, first, shift, refs[s], *outs)


def project(outer, spans, me, rel, feats, kw, mw):
    _, block_len, width = feats[0].shape
    out_shape = []
    for first, last, _ in spans:
        out_shape.append(jax.ShapeDtypeStruct((last - first, width, block_len), BF16))
        out_shape.append(jax.ShapeDtypeStruct((last - first, block_len, width), BF16))
    blocks = sum(last - first for first, last, _ in spans)
    return pl.pallas_call(
        functools.partial(project_kernel, outer, spans),
        out_shape=tuple(out_shape),
        in_specs=[SMEM, SMEM] + [VMEM] * (2 + len(spans)),
        out_specs=(VMEM,) * len(out_shape),
        compiler_params=_mb(4),
        cost_estimate=_cost(4 * blocks * block_len * width * width, blocks * 2**19),
        name="project_slots",
    )(me, rel, kw, mw, *feats)


def aggregate_kernel(
    outer, first, shift, me_ref, rel_ref, count_ref, bias_ref, merch_slot, feats, wq, keys, values,
    sums, query, gates,
):
    blocks, width, block_len = keys.shape
    merchants = sums.shape[0] // blocks
    me = me_ref[0]
    row = lax.broadcasted_iota(jnp.int32, (merchants, block_len), 0)
    lane = lax.broadcasted_iota(jnp.int32, (merchants, block_len), 1)
    query[...] = jnp.dot(
        feats[first * merchants : (first + blocks) * merchants, :],
        wq[...],
        preferred_element_type=F32,
    ).astype(BF16)
    parts = [slice(i * merchants, (i + 1) * merchants) for i in range(blocks)]
    for i in range(blocks):
        block = jnp.bitwise_xor(me, _offset(first + i, outer) + shift)
        score = jnp.dot(query[parts[i], :], keys[i], preferred_element_type=F32) / math.sqrt(width)
        score = score + bias_ref[rel_ref[block]]
        mine = (merch_slot[pl.ds(block, 1), :] == row) & (lane < count_ref[block])
        gates[parts[i], :] = jnp.where(mine, jax.nn.sigmoid(score), 0.0).astype(BF16)
    for i in range(blocks):
        sums[parts[i], :] = jnp.dot(
            gates[parts[i], :], values[i], preferred_element_type=F32
        ).astype(sums.dtype)


def aggregate(outer, first, shift, me, rel, count, bias, merch_slot, feats, wq, keys, values, dtype):
    blocks, width, block_len = keys.shape
    rows = feats.shape[0] * blocks // (merch_slot.shape[0] // 2)
    return pl.pallas_call(
        functools.partial(aggregate_kernel, outer, first, shift),
        out_shape=jax.ShapeDtypeStruct((rows, width), dtype),
        in_specs=[SMEM] * 4 + [VMEM] * 5,
        out_specs=VMEM,
        scratch_shapes=[
            pltpu.VMEM((rows, width), BF16),
            pltpu.VMEM((rows, block_len), BF16),
        ],
        compiler_params=_mb(6),
        cost_estimate=_cost(
            4 * rows * block_len * width + 2 * rows * width * width, 6 * 2**20, rows * block_len
        ),
        name="aggregate_odd" if shift else "aggregate_even",
    )(me, rel, count, bias, merch_slot, feats, wq, keys, values)


def combine_kernel(skip, mine, other, *outs):
    rows = outs[0].shape[0]
    for j, out in enumerate(outs):
        part = slice(j * rows, (j + 1) * rows)
        theirs = slice(skip + j * rows, skip + (j + 1) * rows)
        out[...] = (mine[part, :] + other[theirs, :].astype(F32)).astype(out.dtype)


def combine(groups, skip, mine, other, dtype):
    rows, width = mine.shape
    return pl.pallas_call(
        functools.partial(combine_kernel, skip),
        out_shape=(jax.ShapeDtypeStruct((rows // groups, width), dtype),) * groups,
        in_specs=[VMEM, VMEM],
        out_specs=(VMEM,) * groups,
        compiler_params=_mb(2),
        cost_estimate=_cost(0, 2 * 2**20),
        name="combine_cores",
    )(mine, other)


def plane_kernel(inner, *refs):
    ins, outs = refs[:inner], refs[inner:]
    rows = outs[0].shape[0]
    for k, out in enumerate(outs):
        part = slice(k * rows, (k + 1) * rows)
        total = ins[0][part, :]
        for other in ins[1:]:
            total = total + other[part, :].astype(F32)
        out[...] = total.astype(out.dtype)


def combine_plane(outer, parts):
    rows, width = parts[0].shape
    return pl.pallas_call(
        functools.partial(plane_kernel, len(parts)),
        out_shape=tuple(
            jax.ShapeDtypeStruct((rows // outer, width), F32 if k == 0 else BF16)
            for k in range(outer)
        ),
        in_specs=[VMEM] * len(parts),
        out_specs=(VMEM,) * outer,
        compiler_params=_mb(2),
        cost_estimate=_cost(0, 2**20),
        name="combine_plane",
    )(*parts)


def finish_kernel(feat, gain, wo, *refs):
    out = refs[-1]
    total = refs[0][...]
    for part in refs[1:-1]:
        total = total + part[...].astype(F32)
    update = feat[...].astype(F32) + jnp.dot(
        total.astype(BF16), wo[...], preferred_element_type=F32
    )
    scale = lax.rsqrt(jnp.mean(update * update, axis=-1, keepdims=True) + 1e-06)
    out[...] = (update * scale * gain[...]).astype(BF16)


def finish(feat, gain, wo, parts):
    return pl.pallas_call(
        finish_kernel,
        out_shape=jax.ShapeDtypeStruct(feat.shape, BF16),
        in_specs=[VMEM] * (3 + len(parts)),
        out_specs=VMEM,
        compiler_params=_mb(2),
        name="finish",
    )(feat, gain.reshape(1, -1), wo, *parts)


def per_device(
    acct_feat,
    merch_feat,
    key_weight,
    msg_weight,
    query_weight,
    out_weight,
    rel_bias,
    out_gain,
    slot_acct,
    slot_merch,
    block_rel,
    block_count,
):
    devices = lax.axis_size(AXES)
    me = lax.axis_index(AXES).astype(jnp.int32).reshape(1)
    inner = 4
    outer = devices // (2 * inner)

    def swap(value, mask):
        return lax.ppermute(value, AXES, [(s, s ^ mask) for s in range(devices)])

    def after(value, *others):
        return lax.optimization_barrier((value,) + others)[0]

    feats = jnp.concatenate([swap(merch_feat, 8 * k + 1) for k in range(outer)], axis=0)
    rows = gather(outer, me, slot_acct, acct_feat)
    feats = after(feats, rows[0])
    feats = jnp.concatenate([feats] + [swap(feats, 2 * j) for j in range(1, inner)], axis=0)

    weights = (key_weight, msg_weight)
    rest = (block_rel, block_count, rel_bias, slot_merch)
    blocks = inner * outer
    odd_keys, odd_values, far_keys, far_values = project(
        outer, ((0, blocks, 1), (outer, blocks, 0)), me, block_rel, rows, *weights
    )
    feats = after(feats, far_keys)
    even_feats = swap(feats, 1)
    odd = aggregate(outer, 0, 1, me, *rest, feats, query_weight, odd_keys, odd_values, BF16)
    other = swap(odd, 1)
    far = aggregate(
        outer, outer, 0, me, *rest, even_feats, query_weight, far_keys, far_values, F32
    )
    parts = combine(inner - 1, outer * merch_feat.shape[0], far, other, BF16)

    here = after(me, *parts)
    near_keys, near_values = project(
        outer, ((0, outer, 0),), here, block_rel, rows[1:], *weights
    )
    near = aggregate(
        outer, 0, 0, here, *rest, even_feats, query_weight, near_keys, near_values, F32
    )
    (near,) = combine(1, 0, near, other, F32)
    parts = combine_plane(
        outer, [near] + [swap(parts[j - 1], 2 * j) for j in reversed(range(1, inner))]
    )
    parts = [parts[0]] + [swap(parts[k], 8 * k) for k in reversed(range(1, outer))]
    return finish(merch_feat, out_gain, out_weight, parts)


def solution(mesh):
    placed = (
        P(("acct", "merch"), None),
        P(("acct", "merch"), None),
        P(),
        P(),
        P(),
        P(),
        P(),
        P(),
        P(("acct", "merch"), None),
        P(("acct", "merch"), None),
        P(("acct", "merch")),
        P(("acct", "merch")),
    )
    return jax.shard_map(
        per_device,
        mesh=mesh,
        in_specs=placed,
        out_specs=P(("acct", "merch"), None),
        check_vma=False,
    )
```

```python
import functools
import math

import jax
import jax.numpy as jnp
from jax import lax
from jax.experimental import pallas as pl
from jax.experimental.pallas import tpu as pltpu
from jax.sharding import PartitionSpec as P

AXES = ("acct", "merch")
LANES = 128
F32 = jnp.float32
BF16 = jnp.bfloat16
SMEM = pl.BlockSpec(memory_space=pltpu.SMEM)
ANY = pl.BlockSpec(memory_space=pl.ANY)
VMEM = pl.BlockSpec(memory_space=pltpu.VMEM)


def _mb(n):
    return pltpu.CompilerParams(vmem_limit_bytes=n * 2**20)


def _cost(flops, bytes_accessed, transcendentals=0):
    return pl.CostEstimate(
        flops=int(flops), bytes_accessed=int(bytes_accessed), transcendentals=transcendentals
    )


def _offset(i, outer):
    return (i // outer) * 2 + (i % outer) * 8


def gather_kernel(
    outer, me_ref, slots_ref, acct_hbm, odd, even, acct, table, rows0, rows1, sem
):
    accounts, width = acct.shape
    blocks, block_len, _ = odd.shape
    parts = width // LANES
    pitch = table.shape[1]
    batch = 32
    flat = table.reshape(accounts * pitch, LANES)
    me = me_ref[0]
    chunks = sem.shape[0]
    chunk = accounts // chunks
    copies = [
        pltpu.make_async_copy(
            acct_hbm.at[pl.ds(i * chunk, chunk)], acct.at[pl.ds(i * chunk, chunk)], sem.at[i]
        )
        for i in range(chunks)
    ]
    for copy in copies:
        copy.start()
    for i in range(chunks):
        copies[i].wait()

        @pl.loop(0, chunk // 16, unroll=4)
        def _(g):
            first = pl.multiple_of(i * chunk + g * 16, 16)
            tile = acct[pl.ds(first, 16), :].astype(F32)
            for c in range(parts):
                flat[pl.ds(first * pitch + c, 16, stride=pitch), :] = tile[
                    :, c * LANES : (c + 1) * LANES
                ]

    def collect(block, rows):
        for k in range(0, block_len, batch):
            found = [table[slots_ref[block, k + u], :parts, :] for u in range(batch)]
            for u in range(batch):
                rows[(k + u) * parts : (k + u + 1) * parts, :] = found[u]

    def emit(i, rows, out):
        for c in range(parts):
            out[i, :, c * LANES : (c + 1) * LANES] = rows[
                pl.ds(c, block_len, stride=parts), :
            ].astype(BF16)

    @pl.loop(0, blocks)
    def _(i):
        offset = _offset(i, outer)
        collect(jnp.bitwise_xor(me, offset + 1), rows0)
        collect(jnp.bitwise_xor(me, offset), rows1)
        emit(i, rows0, odd)
        emit(i, rows1, even)


def gather(outer, me, slots, acct):
    blocks, block_len = slots.shape
    accounts, width = acct.shape
    parts = width // LANES
    pitch = -(-parts // 8) * 8
    rows = pltpu.VMEM((block_len * parts, LANES), F32)
    half = jax.ShapeDtypeStruct((blocks // 2, block_len, width), BF16)
    return pl.pallas_call(
        functools.partial(gather_kernel, outer),
        out_shape=(half, half),
        in_specs=[SMEM, SMEM, ANY],
        out_specs=(VMEM, VMEM),
        scratch_shapes=[
            pltpu.VMEM(acct.shape, BF16),
            pltpu.VMEM((accounts, pitch, LANES), F32),
            rows,
            rows,
            pltpu.SemaphoreType.DMA((8,)),
        ],
        compiler_params=_mb(47 if blocks <= 32 else 28),
        cost_estimate=_cost(0, 20 * 2**20),
        name="gather_slots",
    )(me, slots, acct)


def project_kernel(outer, spans, me_ref, rel_ref, kw, mw, *refs):
    width = refs[0].shape[2]
    half = width // 2
    me = me_ref[0]
    count = len(spans)

    def one(i, first, shift, feats, keys, values):
        relation = rel_ref[jnp.bitwise_xor(me, _offset(first + i, outer) + shift)]
        for n in range(0, width, half):
            key = jnp.dot(
                feats[first + i], kw[relation, :, n : n + half], preferred_element_type=F32
            )
            keys[i, n : n + half, :] = key.astype(BF16).T
            value = jnp.dot(
                feats[first + i], mw[relation, :, n : n + half], preferred_element_type=F32
            )
            values[i, :, n : n + half] = value.astype(BF16)

    for s, (first, last, shift) in enumerate(spans):
        outs = refs[count + 2 * s : count + 2 * s + 2]

        @pl.loop(0, last - first, unroll=4)
        def _(i):
            one(i, first, shift, refs[s], *outs)


def project(outer, spans, me, rel, feats, kw, mw):
    _, block_len, width = feats[0].shape
    out_shape = []
    for first, last, _ in spans:
        out_shape.append(jax.ShapeDtypeStruct((last - first, width, block_len), BF16))
        out_shape.append(jax.ShapeDtypeStruct((last - first, block_len, width), BF16))
    blocks = sum(last - first for first, last, _ in spans)
    return pl.pallas_call(
        functools.partial(project_kernel, outer, spans),
        out_shape=tuple(out_shape),
        in_specs=[SMEM, SMEM] + [VMEM] * (2 + len(spans)),
        out_specs=(VMEM,) * len(out_shape),
        compiler_params=_mb(4),
        cost_estimate=_cost(4 * blocks * block_len * width * width, blocks * 2**19),
        name="project_slots",
    )(me, rel, kw, mw, *feats)


def aggregate_kernel(
    outer, first, shift, me_ref, rel_ref, count_ref, bias_ref, merch_slot, feats, wq, keys, values,
    sums,
):
    blocks, width, block_len = keys.shape
    merchants = sums.shape[0] // blocks
    me = me_ref[0]
    row = lax.broadcasted_iota(jnp.int32, (merchants, block_len), 0)
    lane = lax.broadcasted_iota(jnp.int32, (merchants, block_len), 1)
    size = 4
    groups = blocks // size

    def project(g):
        start = (first + g * size) * merchants
        return jnp.dot(
            feats[start : start + size * merchants, :], wq[...], preferred_element_type=F32
        ).astype(BF16)

    def gate(g, query):
        gates = []
        for u in range(size):
            i = g * size + u
            block = jnp.bitwise_xor(me, _offset(first + i, outer) + shift)
            score = jnp.dot(
                query[u * merchants : (u + 1) * merchants, :],
                keys[i],
                preferred_element_type=F32,
            ) / math.sqrt(width)
            score = score + bias_ref[rel_ref[block]]
            mine = (merch_slot[pl.ds(block, 1), :] == row) & (lane < count_ref[block])
            gates.append(jnp.where(mine, jax.nn.sigmoid(score), 0.0).astype(BF16))
        return gates

    def add(g, gates):
        for u in range(size):
            i = g * size + u
            sums[i * merchants : (i + 1) * merchants, :] = jnp.dot(
                gates[u], values[i], preferred_element_type=F32
            ).astype(sums.dtype)

    queries, gates = {}, {}
    for g in range(groups + 2):
        if g < groups:
            queries[g] = project(g)
        if 0 <= g - 1 < groups:
            gates[g - 1] = gate(g - 1, queries.pop(g - 1))
        if g >= 2:
            add(g - 2, gates.pop(g - 2))


def aggregate(outer, first, shift, me, rel, count, bias, merch_slot, feats, wq, keys, values, dtype):
    blocks, width, block_len = keys.shape
    rows = feats.shape[0] * blocks // (merch_slot.shape[0] // 2)
    return pl.pallas_call(
        functools.partial(aggregate_kernel, outer, first, shift),
        out_shape=jax.ShapeDtypeStruct((rows, width), dtype),
        in_specs=[SMEM] * 4 + [VMEM] * 5,
        out_specs=VMEM,
        compiler_params=_mb(6),
        cost_estimate=_cost(
            4 * rows * block_len * width + 2 * rows * width * width, 6 * 2**20, rows * block_len
        ),
        name="aggregate_odd" if shift else "aggregate_even",
    )(me, rel, count, bias, merch_slot, feats, wq, keys, values)


def combine_kernel(skip, mine, other, *outs):
    rows = outs[0].shape[0]
    for j, out in enumerate(outs):
        part = slice(j * rows, (j + 1) * rows)
        theirs = slice(skip + j * rows, skip + (j + 1) * rows)
        out[...] = (mine[part, :] + other[theirs, :].astype(F32)).astype(out.dtype)


def combine(groups, skip, mine, other, dtype):
    rows, width = mine.shape
    return pl.pallas_call(
        functools.partial(combine_kernel, skip),
        out_shape=(jax.ShapeDtypeStruct((rows // groups, width), dtype),) * groups,
        in_specs=[VMEM, VMEM],
        out_specs=(VMEM,) * groups,
        compiler_params=_mb(2),
        cost_estimate=_cost(0, 2 * 2**20),
        name="combine_cores",
    )(mine, other)


def plane_kernel(inner, *refs):
    ins, outs = refs[:inner], refs[inner:]
    rows = outs[0].shape[0]
    for k, out in enumerate(outs):
        part = slice(k * rows, (k + 1) * rows)
        total = ins[0][part, :]
        for other in ins[1:]:
            total = total + other[part, :].astype(F32)
        out[...] = total.astype(out.dtype)


def combine_plane(outer, parts):
    rows, width = parts[0].shape
    return pl.pallas_call(
        functools.partial(plane_kernel, len(parts)),
        out_shape=tuple(
            jax.ShapeDtypeStruct((rows // outer, width), F32 if k == 0 else BF16)
            for k in range(outer)
        ),
        in_specs=[VMEM] * len(parts),
        out_specs=(VMEM,) * outer,
        compiler_params=_mb(2),
        cost_estimate=_cost(0, 2**20),
        name="combine_plane",
    )(*parts)


def finish_kernel(feat, gain, wo, *refs):
    out = refs[-1]
    total = refs[0][...]
    for part in refs[1:-1]:
        total = total + part[...].astype(F32)
    update = feat[...].astype(F32) + jnp.dot(
        total.astype(BF16), wo[...], preferred_element_type=F32
    )
    scale = lax.rsqrt(jnp.mean(update * update, axis=-1, keepdims=True) + 1e-06)
    out[...] = (update * scale * gain[...]).astype(BF16)


def finish(feat, gain, wo, parts):
    return pl.pallas_call(
        finish_kernel,
        out_shape=jax.ShapeDtypeStruct(feat.shape, BF16),
        in_specs=[VMEM] * (3 + len(parts)),
        out_specs=VMEM,
        compiler_params=_mb(2),
        name="finish",
    )(feat, gain.reshape(1, -1), wo, *parts)


def per_device(
    acct_feat,
    merch_feat,
    key_weight,
    msg_weight,
    query_weight,
    out_weight,
    rel_bias,
    out_gain,
    slot_acct,
    slot_merch,
    block_rel,
    block_count,
):
    devices = lax.axis_size(AXES)
    me = lax.axis_index(AXES).astype(jnp.int32).reshape(1)
    inner = 4
    outer = devices // (2 * inner)

    def swap(value, mask):
        return lax.ppermute(value, AXES, [(s, s ^ mask) for s in range(devices)])

    def after(value, *others):
        return lax.optimization_barrier((value,) + others)[0]

    feats = jnp.concatenate([swap(merch_feat, 8 * k + 1) for k in range(outer)], axis=0)
    rows = gather(outer, me, slot_acct, acct_feat)
    feats = after(feats, rows[0])
    feats = jnp.concatenate([feats] + [swap(feats, 2 * j) for j in range(1, inner)], axis=0)

    weights = (key_weight, msg_weight)
    rest = (block_rel, block_count, rel_bias, slot_merch)
    blocks = inner * outer
    odd_keys, odd_values, far_keys, far_values = project(
        outer, ((0, blocks, 1), (outer, blocks, 0)), me, block_rel, rows, *weights
    )
    feats = after(feats, far_keys)
    even_feats = swap(feats, 1)
    odd = aggregate(outer, 0, 1, me, *rest, feats, query_weight, odd_keys, odd_values, BF16)
    other = swap(odd, 1)
    far = aggregate(
        outer, outer, 0, me, *rest, even_feats, query_weight, far_keys, far_values, F32
    )
    parts = combine(inner - 1, outer * merch_feat.shape[0], far, other, BF16)

    here = after(me, *parts)
    near_keys, near_values = project(
        outer, ((0, outer, 0),), here, block_rel, rows[1:], *weights
    )
    near = aggregate(
        outer, 0, 0, here, *rest, even_feats, query_weight, near_keys, near_values, F32
    )
    (near,) = combine(1, 0, near, other, F32)
    parts = combine_plane(
        outer, [near] + [swap(parts[j - 1], 2 * j) for j in reversed(range(1, inner))]
    )
    parts = [parts[0]] + [swap(parts[k], 8 * k) for k in reversed(range(1, outer))]
    return finish(merch_feat, out_gain, out_weight, parts)


def solution(mesh):
    placed = (
        P(("acct", "merch"), None),
        P(("acct", "merch"), None),
        P(),
        P(),
        P(),
        P(),
        P(),
        P(),
        P(("acct", "merch"), None),
        P(("acct", "merch"), None),
        P(("acct", "merch")),
        P(("acct", "merch")),
    )
    return jax.shard_map(
        per_device,
        mesh=mesh,
        in_specs=placed,
        out_specs=P(("acct", "merch"), None),
        check_vma=False,
    )
```

```python
import functools
import math

import jax
import jax.numpy as jnp
from jax import lax
from jax.experimental import pallas as pl
from jax.experimental.pallas import tpu as pltpu
from jax.sharding import PartitionSpec as P

AXES = ("acct", "merch")
LANES = 128
F32 = jnp.float32
BF16 = jnp.bfloat16
SMEM = pl.BlockSpec(memory_space=pltpu.SMEM)
ANY = pl.BlockSpec(memory_space=pl.ANY)
VMEM = pl.BlockSpec(memory_space=pltpu.VMEM)


def _mb(n):
    return pltpu.CompilerParams(vmem_limit_bytes=n * 2**20)


def _cost(flops, bytes_accessed, transcendentals=0):
    return pl.CostEstimate(
        flops=int(flops), bytes_accessed=int(bytes_accessed), transcendentals=transcendentals
    )


def _offset(i, outer):
    return (i // outer) * 2 + (i % outer) * 8


def stage_kernel(slots, out):
    out[...] = slots[...]


def stage(slots):
    return pl.pallas_call(
        stage_kernel,
        out_shape=jax.ShapeDtypeStruct(slots.shape, slots.dtype),
        in_specs=[VMEM],
        out_specs=VMEM,
        compiler_params=_mb(2),
        cost_estimate=_cost(0, 2**16),
        name="stage_slots",
    )(slots)


def gather_kernel(
    outer, me_ref, slots_ref, acct_hbm, odd, even, acct, table, rows0, rows1, sem
):
    accounts, width = acct.shape
    blocks, block_len, _ = odd.shape
    parts = width // LANES
    pitch = table.shape[1]
    batch = 32
    flat = table.reshape(accounts * pitch, LANES)
    me = me_ref[0]
    chunks = sem.shape[0]
    chunk = accounts // chunks
    copies = [
        pltpu.make_async_copy(
            acct_hbm.at[pl.ds(i * chunk, chunk)], acct.at[pl.ds(i * chunk, chunk)], sem.at[i]
        )
        for i in range(chunks)
    ]
    for copy in copies:
        copy.start()
    for i in range(chunks):
        copies[i].wait()

        @pl.loop(0, chunk // 16, unroll=4)
        def _(g):
            first = pl.multiple_of(i * chunk + g * 16, 16)
            tile = acct[pl.ds(first, 16), :].astype(F32)
            for c in range(parts):
                flat[pl.ds(first * pitch + c, 16, stride=pitch), :] = tile[
                    :, c * LANES : (c + 1) * LANES
                ]

    def collect(block, rows):
        for k in range(0, block_len, batch):
            found = [table[slots_ref[block, k + u], :parts, :] for u in range(batch)]
            for u in range(batch):
                rows[(k + u) * parts : (k + u + 1) * parts, :] = found[u]

    def emit(i, rows, out):
        for c in range(parts):
            out[i, :, c * LANES : (c + 1) * LANES] = rows[
                pl.ds(c, block_len, stride=parts), :
            ].astype(BF16)

    @pl.loop(0, blocks)
    def _(i):
        offset = _offset(i, outer)
        collect(jnp.bitwise_xor(me, offset + 1), rows0)
        collect(jnp.bitwise_xor(me, offset), rows1)
        emit(i, rows0, odd)
        emit(i, rows1, even)


def gather(outer, me, slots, acct):
    blocks, block_len = slots.shape
    accounts, width = acct.shape
    parts = width // LANES
    pitch = -(-parts // 8) * 8
    rows = pltpu.VMEM((block_len * parts, LANES), F32)
    half = jax.ShapeDtypeStruct((blocks // 2, block_len, width), BF16)
    return pl.pallas_call(
        functools.partial(gather_kernel, outer),
        out_shape=(half, half),
        in_specs=[SMEM, SMEM, ANY],
        out_specs=(VMEM, VMEM),
        scratch_shapes=[
            pltpu.VMEM(acct.shape, BF16),
            pltpu.VMEM((accounts, pitch, LANES), F32),
            rows,
            rows,
            pltpu.SemaphoreType.DMA((8,)),
        ],
        compiler_params=_mb(47 if blocks <= 32 else 28),
        cost_estimate=_cost(0, 20 * 2**20),
        name="gather_slots",
    )(me, slots, acct)


def project_kernel(outer, spans, me_ref, rel_ref, kw, mw, *refs):
    width = refs[0].shape[2]
    half = width // 2
    me = me_ref[0]
    count = len(spans)

    def one(i, first, shift, feats, keys, values):
        relation = rel_ref[jnp.bitwise_xor(me, _offset(first + i, outer) + shift)]
        for n in range(0, width, half):
            key = jnp.dot(
                feats[first + i], kw[relation, :, n : n + half], preferred_element_type=F32
            )
            keys[i, n : n + half, :] = key.astype(BF16).T
            value = jnp.dot(
                feats[first + i], mw[relation, :, n : n + half], preferred_element_type=F32
            )
            values[i, :, n : n + half] = value.astype(BF16)

    for s, (first, last, shift) in enumerate(spans):
        outs = refs[count + 2 * s : count + 2 * s + 2]

        @pl.loop(0, last - first, unroll=4)
        def _(i):
            one(i, first, shift, refs[s], *outs)


def project(outer, spans, me, rel, feats, kw, mw):
    _, block_len, width = feats[0].shape
    out_shape = []
    for first, last, _ in spans:
        out_shape.append(jax.ShapeDtypeStruct((last - first, width, block_len), BF16))
        out_shape.append(jax.ShapeDtypeStruct((last - first, block_len, width), BF16))
    blocks = sum(last - first for first, last, _ in spans)
    return pl.pallas_call(
        functools.partial(project_kernel, outer, spans),
        out_shape=tuple(out_shape),
        in_specs=[SMEM, SMEM] + [VMEM] * (2 + len(spans)),
        out_specs=(VMEM,) * len(out_shape),
        compiler_params=_mb(4),
        cost_estimate=_cost(4 * blocks * block_len * width * width, blocks * 2**19),
        name="project_slots",
    )(me, rel, kw, mw, *feats)


def aggregate_kernel(
    outer, first, shift, me_ref, rel_ref, count_ref, bias_ref, merch_slot, feats, wq, keys, values,
    sums, query, gates,
):
    blocks, width, block_len = keys.shape
    merchants = sums.shape[0] // blocks
    me = me_ref[0]
    row = lax.broadcasted_iota(jnp.int32, (merchants, block_len), 0)
    lane = lax.broadcasted_iota(jnp.int32, (merchants, block_len), 1)
    query[...] = jnp.dot(
        feats[first * merchants : (first + blocks) * merchants, :],
        wq[...],
        preferred_element_type=F32,
    ).astype(BF16)
    parts = [slice(i * merchants, (i + 1) * merchants) for i in range(blocks)]
    for i in range(blocks):
        block = jnp.bitwise_xor(me, _offset(first + i, outer) + shift)
        score = jnp.dot(query[parts[i], :], keys[i], preferred_element_type=F32) / math.sqrt(width)
        score = score + bias_ref[rel_ref[block]]
        mine = (merch_slot[pl.ds(block, 1), :] == row) & (lane < count_ref[block])
        gates[parts[i], :] = jnp.where(mine, jax.nn.sigmoid(score), 0.0).astype(BF16)
    for i in range(blocks):
        sums[parts[i], :] = jnp.dot(
            gates[parts[i], :], values[i], preferred_element_type=F32
        ).astype(sums.dtype)


def aggregate(outer, first, shift, me, rel, count, bias, merch_slot, feats, wq, keys, values, dtype):
    blocks, width, block_len = keys.shape
    rows = feats.shape[0] * blocks // (merch_slot.shape[0] // 2)
    return pl.pallas_call(
        functools.partial(aggregate_kernel, outer, first, shift),
        out_shape=jax.ShapeDtypeStruct((rows, width), dtype),
        in_specs=[SMEM] * 4 + [VMEM] * 5,
        out_specs=VMEM,
        scratch_shapes=[
            pltpu.VMEM((rows, width), BF16),
            pltpu.VMEM((rows, block_len), BF16),
        ],
        compiler_params=_mb(6),
        cost_estimate=_cost(
            4 * rows * block_len * width + 2 * rows * width * width, 6 * 2**20, rows * block_len
        ),
        name="aggregate_odd" if shift else "aggregate_even",
    )(me, rel, count, bias, merch_slot, feats, wq, keys, values)


def combine_kernel(skip, mine, other, *outs):
    rows = outs[0].shape[0]
    for j, out in enumerate(outs):
        part = slice(j * rows, (j + 1) * rows)
        theirs = slice(skip + j * rows, skip + (j + 1) * rows)
        out[...] = (mine[part, :] + other[theirs, :].astype(F32)).astype(out.dtype)


def combine(groups, skip, mine, other, dtype):
    rows, width = mine.shape
    return pl.pallas_call(
        functools.partial(combine_kernel, skip),
        out_shape=(jax.ShapeDtypeStruct((rows // groups, width), dtype),) * groups,
        in_specs=[VMEM, VMEM],
        out_specs=(VMEM,) * groups,
        compiler_params=_mb(2),
        cost_estimate=_cost(0, 2 * 2**20),
        name="combine_cores",
    )(mine, other)


def plane_kernel(inner, *refs):
    ins, outs = refs[:inner], refs[inner:]
    rows = outs[0].shape[0]
    for k, out in enumerate(outs):
        part = slice(k * rows, (k + 1) * rows)
        total = ins[0][part, :]
        for other in ins[1:]:
            total = total + other[part, :].astype(F32)
        out[...] = total.astype(out.dtype)


def combine_plane(outer, parts):
    rows, width = parts[0].shape
    return pl.pallas_call(
        functools.partial(plane_kernel, len(parts)),
        out_shape=tuple(
            jax.ShapeDtypeStruct((rows // outer, width), F32 if k == 0 else BF16)
            for k in range(outer)
        ),
        in_specs=[VMEM] * len(parts),
        out_specs=(VMEM,) * outer,
        compiler_params=_mb(2),
        cost_estimate=_cost(0, 2**20),
        name="combine_plane",
    )(*parts)


def finish_kernel(feat, gain, wo, *refs):
    out = refs[-1]
    total = refs[0][...]
    for part in refs[1:-1]:
        total = total + part[...].astype(F32)
    update = feat[...].astype(F32) + jnp.dot(
        total.astype(BF16), wo[...], preferred_element_type=F32
    )
    scale = lax.rsqrt(jnp.mean(update * update, axis=-1, keepdims=True) + 1e-06)
    out[...] = (update * scale * gain[...]).astype(BF16)


def finish(feat, gain, wo, parts):
    return pl.pallas_call(
        finish_kernel,
        out_shape=jax.ShapeDtypeStruct(feat.shape, BF16),
        in_specs=[VMEM] * (3 + len(parts)),
        out_specs=VMEM,
        compiler_params=_mb(2),
        name="finish",
    )(feat, gain.reshape(1, -1), wo, *parts)


def per_device(
    acct_feat,
    merch_feat,
    key_weight,
    msg_weight,
    query_weight,
    out_weight,
    rel_bias,
    out_gain,
    slot_acct,
    slot_merch,
    block_rel,
    block_count,
):
    devices = lax.axis_size(AXES)
    me = lax.axis_index(AXES).astype(jnp.int32).reshape(1)
    inner = 4
    outer = devices // (2 * inner)

    def swap(value, mask):
        return lax.ppermute(value, AXES, [(s, s ^ mask) for s in range(devices)])

    def after(value, *others):
        return lax.optimization_barrier((value,) + others)[0]

    feats = jnp.concatenate([swap(merch_feat, 1), swap(merch_feat, 9)], axis=0)
    slots = stage(slot_acct)
    feats = after(feats, slots)
    mask = 16
    while mask < devices:
        feats = jnp.concatenate([feats, swap(feats, mask)], axis=0)
        mask *= 2
    rows = gather(outer, me, slots, acct_feat)
    feats = after(feats, rows[0])
    feats = jnp.concatenate([feats] + [swap(feats, 2 * j) for j in range(1, inner)], axis=0)

    weights = (key_weight, msg_weight)
    rest = (block_rel, block_count, rel_bias, slot_merch)
    blocks = inner * outer
    odd_keys, odd_values, far_keys, far_values = project(
        outer, ((0, blocks, 1), (outer, blocks, 0)), me, block_rel, rows, *weights
    )
    feats = after(feats, far_keys)
    even_feats = swap(feats, 1)
    odd = aggregate(outer, 0, 1, me, *rest, feats, query_weight, odd_keys, odd_values, BF16)
    other = swap(odd, 1)
    far = aggregate(
        outer, outer, 0, me, *rest, even_feats, query_weight, far_keys, far_values, F32
    )
    parts = combine(inner - 1, outer * merch_feat.shape[0], far, other, BF16)

    here = after(me, *parts)
    near_keys, near_values = project(
        outer, ((0, outer, 0),), here, block_rel, rows[1:], *weights
    )
    near = aggregate(
        outer, 0, 0, here, *rest, even_feats, query_weight, near_keys, near_values, F32
    )
    (near,) = combine(1, 0, near, other, F32)
    parts = combine_plane(
        outer, [near] + [swap(parts[j - 1], 2 * j) for j in reversed(range(1, inner))]
    )
    order = [2, 3, 1] + list(range(4, outer))
    parts = [parts[0]] + [swap(parts[k], 8 * k) for k in order]
    return finish(merch_feat, out_gain, out_weight, parts)


def solution(mesh):
    placed = (
        P(("acct", "merch"), None),
        P(("acct", "merch"), None),
        P(),
        P(),
        P(),
        P(),
        P(),
        P(),
        P(("acct", "merch"), None),
        P(("acct", "merch"), None),
        P(("acct", "merch")),
        P(("acct", "merch")),
    )
    return jax.shard_map(
        per_device,
        mesh=mesh,
        in_specs=placed,
        out_specs=P(("acct", "merch"), None),
        check_vma=False,
    )
```

```python
import functools
import math

import jax
import jax.numpy as jnp
from jax import lax
from jax.experimental import pallas as pl
from jax.experimental.pallas import tpu as pltpu
from jax.sharding import PartitionSpec as P

AXES = ("acct", "merch")
LANES = 128
F32 = jnp.float32
BF16 = jnp.bfloat16
SMEM = pl.BlockSpec(memory_space=pltpu.SMEM)
ANY = pl.BlockSpec(memory_space=pl.ANY)
VMEM = pl.BlockSpec(memory_space=pltpu.VMEM)


def _mb(n):
    return pltpu.CompilerParams(vmem_limit_bytes=n * 2**20)


def _cost(flops, bytes_accessed, transcendentals=0):
    return pl.CostEstimate(
        flops=int(flops), bytes_accessed=int(bytes_accessed), transcendentals=transcendentals
    )


def _offset(i, outer):
    return (i // outer) * 2 + (i % outer) * 8


def gather_kernel(
    outer, me_ref, slots_ref, acct_hbm, odd, even, acct, table, rows0, rows1, sem
):
    accounts, width = acct.shape
    blocks, block_len, _ = odd.shape
    parts = width // LANES
    pitch = table.shape[1]
    batch = 32
    flat = table.reshape(accounts * pitch, LANES)
    me = me_ref[0]
    chunks = sem.shape[0]
    chunk = accounts // chunks
    copies = [
        pltpu.make_async_copy(
            acct_hbm.at[pl.ds(i * chunk, chunk)], acct.at[pl.ds(i * chunk, chunk)], sem.at[i]
        )
        for i in range(chunks)
    ]
    for copy in copies:
        copy.start()
    for i in range(chunks):
        copies[i].wait()

        @pl.loop(0, chunk // 16, unroll=4)
        def _(g):
            first = pl.multiple_of(i * chunk + g * 16, 16)
            tile = acct[pl.ds(first, 16), :].astype(F32)
            for c in range(parts):
                flat[pl.ds(first * pitch + c, 16, stride=pitch), :] = tile[
                    :, c * LANES : (c + 1) * LANES
                ]

    def collect(block, rows):
        for k in range(0, block_len, batch):
            found = [table[slots_ref[block, k + u], :parts, :] for u in range(batch)]
            for u in range(batch):
                rows[(k + u) * parts : (k + u + 1) * parts, :] = found[u]

    def emit(i, rows, out):
        for c in range(parts):
            out[i, :, c * LANES : (c + 1) * LANES] = rows[
                pl.ds(c, block_len, stride=parts), :
            ].astype(BF16)

    @pl.loop(0, blocks)
    def _(i):
        offset = _offset(i, outer)
        collect(jnp.bitwise_xor(me, offset + 1), rows0)
        collect(jnp.bitwise_xor(me, offset), rows1)
        emit(i, rows0, odd)
        emit(i, rows1, even)


def gather(outer, me, slots, acct):
    blocks, block_len = slots.shape
    accounts, width = acct.shape
    parts = width // LANES
    pitch = -(-parts // 8) * 8
    rows = pltpu.VMEM((block_len * parts, LANES), F32)
    half = jax.ShapeDtypeStruct((blocks // 2, block_len, width), BF16)
    return pl.pallas_call(
        functools.partial(gather_kernel, outer),
        out_shape=(half, half),
        in_specs=[SMEM, SMEM, ANY],
        out_specs=(VMEM, VMEM),
        scratch_shapes=[
            pltpu.VMEM(acct.shape, BF16),
            pltpu.VMEM((accounts, pitch, LANES), F32),
            rows,
            rows,
            pltpu.SemaphoreType.DMA((8,)),
        ],
        compiler_params=_mb(47 if blocks <= 32 else 28),
        cost_estimate=_cost(0, 20 * 2**20),
        name="gather_slots",
    )(me, slots, acct)


def project_kernel(outer, spans, me_ref, rel_ref, kw, mw, *refs):
    width = refs[0].shape[2]
    half = width // 2
    me = me_ref[0]
    count = len(spans)

    def one(i, first, shift, feats, keys, values):
        relation = rel_ref[jnp.bitwise_xor(me, _offset(first + i, outer) + shift)]
        for n in range(0, width, half):
            key = jnp.dot(
                feats[first + i], kw[relation, :, n : n + half], preferred_element_type=F32
            )
            keys[i, n : n + half, :] = key.astype(BF16).T
            value = jnp.dot(
                feats[first + i], mw[relation, :, n : n + half], preferred_element_type=F32
            )
            values[i, :, n : n + half] = value.astype(BF16)

    for s, (first, last, shift) in enumerate(spans):
        outs = refs[count + 2 * s : count + 2 * s + 2]

        @pl.loop(0, last - first, unroll=4)
        def _(i):
            one(i, first, shift, refs[s], *outs)


def project(outer, spans, me, rel, feats, kw, mw):
    _, block_len, width = feats[0].shape
    out_shape = []
    for first, last, _ in spans:
        out_shape.append(jax.ShapeDtypeStruct((last - first, width, block_len), BF16))
        out_shape.append(jax.ShapeDtypeStruct((last - first, block_len, width), BF16))
    blocks = sum(last - first for first, last, _ in spans)
    return pl.pallas_call(
        functools.partial(project_kernel, outer, spans),
        out_shape=tuple(out_shape),
        in_specs=[SMEM, SMEM] + [VMEM] * (2 + len(spans)),
        out_specs=(VMEM,) * len(out_shape),
        compiler_params=_mb(4),
        cost_estimate=_cost(4 * blocks * block_len * width * width, blocks * 2**19),
        name="project_slots",
    )(me, rel, kw, mw, *feats)


def assemble_kernel(places, *refs):
    rows = refs[0].shape[0]
    for place, part in zip(places, refs[:-1]):
        refs[-1][place * rows : (place + 1) * rows, :] = part[...]


def assemble(places, parts):
    rows, width = parts[0].shape
    return pl.pallas_call(
        functools.partial(assemble_kernel, places),
        out_shape=jax.ShapeDtypeStruct((len(parts) * rows, width), parts[0].dtype),
        in_specs=[VMEM] * len(parts),
        out_specs=VMEM,
        compiler_params=_mb(2),
        cost_estimate=_cost(1, 1),
        name="assemble",
    )(*parts)


def aggregate_kernel(
    outer, first, shift, me_ref, rel_ref, count_ref, bias_ref, merch_slot, feats, wq, keys, values,
    sums, query, gates,
):
    blocks, width, block_len = keys.shape
    merchants = sums.shape[0] // blocks
    me = me_ref[0]
    row = lax.broadcasted_iota(jnp.int32, (merchants, block_len), 0)
    lane = lax.broadcasted_iota(jnp.int32, (merchants, block_len), 1)
    query[...] = jnp.dot(
        feats[first * merchants : (first + blocks) * merchants, :],
        wq[...],
        preferred_element_type=F32,
    ).astype(BF16)
    parts = [slice(i * merchants, (i + 1) * merchants) for i in range(blocks)]
    for i in range(blocks):
        block = jnp.bitwise_xor(me, _offset(first + i, outer) + shift)
        score = jnp.dot(query[parts[i], :], keys[i], preferred_element_type=F32) / math.sqrt(width)
        score = score + bias_ref[rel_ref[block]]
        mine = (merch_slot[pl.ds(block, 1), :] == row) & (lane < count_ref[block])
        gates[parts[i], :] = jnp.where(mine, jax.nn.sigmoid(score), 0.0).astype(BF16)
    for i in range(blocks):
        sums[parts[i], :] = jnp.dot(
            gates[parts[i], :], values[i], preferred_element_type=F32
        ).astype(sums.dtype)


def aggregate(outer, first, shift, me, rel, count, bias, merch_slot, feats, wq, keys, values, dtype):
    blocks, width, block_len = keys.shape
    rows = feats.shape[0] * blocks // (merch_slot.shape[0] // 2)
    return pl.pallas_call(
        functools.partial(aggregate_kernel, outer, first, shift),
        out_shape=jax.ShapeDtypeStruct((rows, width), dtype),
        in_specs=[SMEM] * 4 + [VMEM] * 5,
        out_specs=VMEM,
        scratch_shapes=[
            pltpu.VMEM((rows, width), BF16),
            pltpu.VMEM((rows, block_len), BF16),
        ],
        compiler_params=_mb(6),
        cost_estimate=_cost(
            4 * rows * block_len * width + 2 * rows * width * width, 6 * 2**20, rows * block_len
        ),
        name="aggregate_odd" if shift else "aggregate_even",
    )(me, rel, count, bias, merch_slot, feats, wq, keys, values)


def combine_kernel(skip, mine, other, *outs):
    rows = outs[0].shape[0]
    for j, out in enumerate(outs):
        part = slice(j * rows, (j + 1) * rows)
        theirs = slice(skip + j * rows, skip + (j + 1) * rows)
        out[...] = (mine[part, :] + other[theirs, :].astype(F32)).astype(out.dtype)


def combine(groups, skip, mine, other, dtype):
    rows, width = mine.shape
    return pl.pallas_call(
        functools.partial(combine_kernel, skip),
        out_shape=(jax.ShapeDtypeStruct((rows // groups, width), dtype),) * groups,
        in_specs=[VMEM, VMEM],
        out_specs=(VMEM,) * groups,
        compiler_params=_mb(2),
        cost_estimate=_cost(0, 2 * 2**20),
        name="combine_cores",
    )(mine, other)


def plane_kernel(inner, *refs):
    ins, outs = refs[:inner], refs[inner:]
    rows = outs[0].shape[0]
    for k, out in enumerate(outs):
        part = slice(k * rows, (k + 1) * rows)
        total = ins[0][part, :]
        for other in ins[1:]:
            total = total + other[part, :].astype(F32)
        out[...] = total.astype(out.dtype)


def combine_plane(outer, parts):
    rows, width = parts[0].shape
    return pl.pallas_call(
        functools.partial(plane_kernel, len(parts)),
        out_shape=tuple(
            jax.ShapeDtypeStruct((rows // outer, width), F32 if k == 0 else BF16)
            for k in range(outer)
        ),
        in_specs=[VMEM] * len(parts),
        out_specs=(VMEM,) * outer,
        compiler_params=_mb(2),
        cost_estimate=_cost(0, 2**20),
        name="combine_plane",
    )(*parts)


def finish_kernel(feat, gain, wo, *refs):
    out = refs[-1]
    total = refs[0][...]
    for part in refs[1:-1]:
        total = total + part[...].astype(F32)
    update = feat[...].astype(F32) + jnp.dot(
        total.astype(BF16), wo[...], preferred_element_type=F32
    )
    scale = lax.rsqrt(jnp.mean(update * update, axis=-1, keepdims=True) + 1e-06)
    out[...] = (update * scale * gain[...]).astype(BF16)


def finish(feat, gain, wo, parts):
    return pl.pallas_call(
        finish_kernel,
        out_shape=jax.ShapeDtypeStruct(feat.shape, BF16),
        in_specs=[VMEM] * (3 + len(parts)),
        out_specs=VMEM,
        compiler_params=_mb(2),
        name="finish",
    )(feat, gain.reshape(1, -1), wo, *parts)


def per_device(
    acct_feat,
    merch_feat,
    key_weight,
    msg_weight,
    query_weight,
    out_weight,
    rel_bias,
    out_gain,
    slot_acct,
    slot_merch,
    block_rel,
    block_count,
):
    devices = lax.axis_size(AXES)
    me = lax.axis_index(AXES).astype(jnp.int32).reshape(1)
    inner = 4
    outer = devices // (2 * inner)

    def swap(value, mask):
        return lax.ppermute(value, AXES, [(s, s ^ mask) for s in range(devices)])

    def after(value, *others):
        return lax.optimization_barrier((value,) + others)[0]

    order = [1, 3, 2, 0] + list(range(4, outer))
    feats = assemble(order, [swap(merch_feat, 8 * k + 1) for k in order])
    rows = gather(outer, me, slot_acct, acct_feat)
    feats = after(feats, rows[0])
    feats = jnp.concatenate([feats] + [swap(feats, 2 * j) for j in range(1, inner)], axis=0)

    weights = (key_weight, msg_weight)
    rest = (block_rel, block_count, rel_bias, slot_merch)
    blocks = inner * outer
    odd_keys, odd_values, far_keys, far_values = project(
        outer, ((0, blocks, 1), (outer, blocks, 0)), me, block_rel, rows, *weights
    )
    feats = after(feats, far_keys)
    even_feats = swap(feats, 1)
    odd = aggregate(outer, 0, 1, me, *rest, feats, query_weight, odd_keys, odd_values, BF16)
    other = swap(odd, 1)
    far = aggregate(
        outer, outer, 0, me, *rest, even_feats, query_weight, far_keys, far_values, F32
    )
    parts = combine(inner - 1, outer * merch_feat.shape[0], far, other, BF16)

    here = after(me, *parts)
    near_keys, near_values = project(
        outer, ((0, outer, 0),), here, block_rel, rows[1:], *weights
    )
    near = aggregate(
        outer, 0, 0, here, *rest, even_feats, query_weight, near_keys, near_values, F32
    )
    (near,) = combine(1, 0, near, other, F32)
    parts = combine_plane(
        outer, [near] + [swap(parts[j - 1], 2 * j) for j in reversed(range(1, inner))]
    )
    parts = [parts[0]] + [swap(parts[k], 8 * k) for k in reversed(range(1, outer))]
    return finish(merch_feat, out_gain, out_weight, parts)


def solution(mesh):
    placed = (
        P(("acct", "merch"), None),
        P(("acct", "merch"), None),
        P(),
        P(),
        P(),
        P(),
        P(),
        P(),
        P(("acct", "merch"), None),
        P(("acct", "merch"), None),
        P(("acct", "merch")),
        P(("acct", "merch")),
    )
    return jax.shard_map(
        per_device,
        mesh=mesh,
        in_specs=placed,
        out_specs=P(("acct", "merch"), None),
        check_vma=False,
    )
```

```python
import functools
import math

import jax
import jax.numpy as jnp
from jax import lax
from jax.experimental import pallas as pl
from jax.experimental.pallas import tpu as pltpu
from jax.sharding import PartitionSpec as P

AXES = ("acct", "merch")
LANES = 128
F32 = jnp.float32
BF16 = jnp.bfloat16
SMEM = pl.BlockSpec(memory_space=pltpu.SMEM)
ANY = pl.BlockSpec(memory_space=pl.ANY)
VMEM = pl.BlockSpec(memory_space=pltpu.VMEM)


def _mb(n):
    return pltpu.CompilerParams(vmem_limit_bytes=n * 2**20)


def _cost(flops, bytes_accessed, transcendentals=0):
    return pl.CostEstimate(
        flops=int(flops), bytes_accessed=int(bytes_accessed), transcendentals=transcendentals
    )


def _offset(i, outer):
    return (i // outer) * 2 + (i % outer) * 8


def gather_kernel(
    outer, me_ref, slots_ref, acct_hbm, odd, even, acct, table, rows0, rows1, sem
):
    accounts, width = acct.shape
    blocks, block_len, _ = odd.shape
    parts = width // LANES
    pitch = table.shape[1]
    batch = 32
    flat = table.reshape(accounts * pitch, LANES)
    me = me_ref[0]
    chunks = sem.shape[0]
    chunk = accounts // chunks
    copies = [
        pltpu.make_async_copy(
            acct_hbm.at[pl.ds(i * chunk, chunk)], acct.at[pl.ds(i * chunk, chunk)], sem.at[i]
        )
        for i in range(chunks)
    ]
    for copy in copies:
        copy.start()
    for i in range(chunks):
        copies[i].wait()

        @pl.loop(0, chunk // 16, unroll=4)
        def _(g):
            first = pl.multiple_of(i * chunk + g * 16, 16)
            tile = acct[pl.ds(first, 16), :].astype(F32)
            for c in range(parts):
                flat[pl.ds(first * pitch + c, 16, stride=pitch), :] = tile[
                    :, c * LANES : (c + 1) * LANES
                ]

    def collect(block, rows):
        for k in range(0, block_len, batch):
            found = [table[slots_ref[block, k + u], :parts, :] for u in range(batch)]
            for u in range(batch):
                rows[(k + u) * parts : (k + u + 1) * parts, :] = found[u]

    def emit(i, rows, out):
        for c in range(parts):
            out[i, :, c * LANES : (c + 1) * LANES] = rows[
                pl.ds(c, block_len, stride=parts), :
            ].astype(BF16)

    @pl.loop(0, blocks)
    def _(i):
        offset = _offset(i, outer)
        collect(jnp.bitwise_xor(me, offset + 1), rows0)
        collect(jnp.bitwise_xor(me, offset), rows1)
        emit(i, rows0, odd)
        emit(i, rows1, even)


def gather(outer, me, slots, acct):
    blocks, block_len = slots.shape
    accounts, width = acct.shape
    parts = width // LANES
    pitch = -(-parts // 8) * 8
    rows = pltpu.VMEM((block_len * parts, LANES), F32)
    half = jax.ShapeDtypeStruct((blocks // 2, block_len, width), BF16)
    return pl.pallas_call(
        functools.partial(gather_kernel, outer),
        out_shape=(half, half),
        in_specs=[SMEM, SMEM, ANY],
        out_specs=(VMEM, VMEM),
        scratch_shapes=[
            pltpu.VMEM(acct.shape, BF16),
            pltpu.VMEM((accounts, pitch, LANES), F32),
            rows,
            rows,
            pltpu.SemaphoreType.DMA((8,)),
        ],
        compiler_params=_mb(47 if blocks <= 32 else 28),
        cost_estimate=_cost(0, 20 * 2**20),
        name="gather_slots",
    )(me, slots, acct)


def project_kernel(outer, spans, me_ref, rel_ref, kw, mw, *refs):
    width = refs[0].shape[2]
    half = width // 2
    me = me_ref[0]
    count = len(spans)

    def one(i, first, shift, feats, keys, values):
        relation = rel_ref[jnp.bitwise_xor(me, _offset(first + i, outer) + shift)]
        for n in range(0, width, half):
            key = jnp.dot(
                feats[first + i], kw[relation, :, n : n + half], preferred_element_type=F32
            )
            keys[i, n : n + half, :] = key.astype(BF16).T
            value = jnp.dot(
                feats[first + i], mw[relation, :, n : n + half], preferred_element_type=F32
            )
            values[i, :, n : n + half] = value.astype(BF16)

    for s, (first, last, shift) in enumerate(spans):
        outs = refs[count + 2 * s : count + 2 * s + 2]

        @pl.loop(0, last - first, unroll=4)
        def _(i):
            one(i, first, shift, refs[s], *outs)


def project(outer, spans, me, rel, feats, kw, mw):
    _, block_len, width = feats[0].shape
    out_shape = []
    for first, last, _ in spans:
        out_shape.append(jax.ShapeDtypeStruct((last - first, width, block_len), BF16))
        out_shape.append(jax.ShapeDtypeStruct((last - first, block_len, width), BF16))
    blocks = sum(last - first for first, last, _ in spans)
    return pl.pallas_call(
        functools.partial(project_kernel, outer, spans),
        out_shape=tuple(out_shape),
        in_specs=[SMEM, SMEM] + [VMEM] * (2 + len(spans)),
        out_specs=(VMEM,) * len(out_shape),
        compiler_params=_mb(4),
        cost_estimate=_cost(4 * blocks * block_len * width * width, blocks * 2**19),
        name="project_slots",
    )(me, rel, kw, mw, *feats)


def assemble_kernel(places, *refs):
    rows = refs[0].shape[0]
    for place, part in zip(places, refs[:-1]):
        refs[-1][place * rows : (place + 1) * rows, :] = part[...]


def assemble(places, parts):
    rows, width = parts[0].shape
    return pl.pallas_call(
        functools.partial(assemble_kernel, places),
        out_shape=jax.ShapeDtypeStruct((len(parts) * rows, width), parts[0].dtype),
        in_specs=[VMEM] * len(parts),
        out_specs=VMEM,
        compiler_params=_mb(2),
        cost_estimate=_cost(1, 1),
        name="assemble",
    )(*parts)


def aggregate_kernel(
    outer, first, shift, me_ref, rel_ref, count_ref, bias_ref, merch_slot, feats, wq, keys, values,
    sums, query, gates,
):
    blocks, width, block_len = keys.shape
    merchants = sums.shape[0] // blocks
    me = me_ref[0]
    row = lax.broadcasted_iota(jnp.int32, (merchants, block_len), 0)
    lane = lax.broadcasted_iota(jnp.int32, (merchants, block_len), 1)
    query[...] = jnp.dot(
        feats[first * merchants : (first + blocks) * merchants, :],
        wq[...],
        preferred_element_type=F32,
    ).astype(BF16)
    parts = [slice(i * merchants, (i + 1) * merchants) for i in range(blocks)]
    for i in range(blocks):
        block = jnp.bitwise_xor(me, _offset(first + i, outer) + shift)
        score = jnp.dot(query[parts[i], :], keys[i], preferred_element_type=F32) / math.sqrt(width)
        score = score + bias_ref[rel_ref[block]]
        mine = (merch_slot[pl.ds(block, 1), :] == row) & (lane < count_ref[block])
        gates[parts[i], :] = jnp.where(mine, jax.nn.sigmoid(score), 0.0).astype(BF16)
    for i in range(blocks):
        sums[parts[i], :] = jnp.dot(
            gates[parts[i], :], values[i], preferred_element_type=F32
        ).astype(sums.dtype)


def aggregate(outer, first, shift, me, rel, count, bias, merch_slot, feats, wq, keys, values, dtype):
    blocks, width, block_len = keys.shape
    rows = feats.shape[0] * blocks // (merch_slot.shape[0] // 2)
    return pl.pallas_call(
        functools.partial(aggregate_kernel, outer, first, shift),
        out_shape=jax.ShapeDtypeStruct((rows, width), dtype),
        in_specs=[SMEM] * 4 + [VMEM] * 5,
        out_specs=VMEM,
        scratch_shapes=[
            pltpu.VMEM((rows, width), BF16),
            pltpu.VMEM((rows, block_len), BF16),
        ],
        compiler_params=_mb(6),
        cost_estimate=_cost(
            4 * rows * block_len * width + 2 * rows * width * width, 6 * 2**20, rows * block_len
        ),
        name="aggregate_odd" if shift else "aggregate_even",
    )(me, rel, count, bias, merch_slot, feats, wq, keys, values)


def combine_kernel(skip, mine, other, *outs):
    rows = outs[0].shape[0]
    for j, out in enumerate(reversed(outs)):
        part = slice(j * rows, (j + 1) * rows)
        theirs = slice(skip + j * rows, skip + (j + 1) * rows)
        out[...] = (mine[part, :] + other[theirs, :].astype(F32)).astype(out.dtype)


def combine(groups, skip, mine, other, dtype):
    rows, width = mine.shape
    return pl.pallas_call(
        functools.partial(combine_kernel, skip),
        out_shape=(jax.ShapeDtypeStruct((rows // groups, width), dtype),) * groups,
        in_specs=[VMEM, VMEM],
        out_specs=(VMEM,) * groups,
        compiler_params=_mb(2),
        cost_estimate=_cost(0, 2 * 2**20),
        name="combine_cores",
    )(mine, other)


def plane_kernel(inner, *refs):
    ins, outs = refs[:inner], refs[inner:]
    rows = outs[0].shape[0]
    for k, out in enumerate(outs):
        part = slice(k * rows, (k + 1) * rows)
        total = ins[0][part, :]
        for other in ins[1:]:
            total = total + other[part, :].astype(F32)
        out[...] = total.astype(out.dtype)


def combine_plane(outer, parts):
    rows, width = parts[0].shape
    return pl.pallas_call(
        functools.partial(plane_kernel, len(parts)),
        out_shape=tuple(
            jax.ShapeDtypeStruct((rows // outer, width), F32 if k == 0 else BF16)
            for k in range(outer)
        ),
        in_specs=[VMEM] * len(parts),
        out_specs=(VMEM,) * outer,
        compiler_params=_mb(2),
        cost_estimate=_cost(0, 2**20),
        name="combine_plane",
    )(*parts)


def finish_kernel(feat, gain, wo, *refs):
    out = refs[-1]
    total = refs[0][...]
    for part in refs[1:-1]:
        total = total + part[...].astype(F32)
    update = feat[...].astype(F32) + jnp.dot(
        total.astype(BF16), wo[...], preferred_element_type=F32
    )
    scale = lax.rsqrt(jnp.mean(update * update, axis=-1, keepdims=True) + 1e-06)
    out[...] = (update * scale * gain[...]).astype(BF16)


def finish(feat, gain, wo, parts):
    return pl.pallas_call(
        finish_kernel,
        out_shape=jax.ShapeDtypeStruct(feat.shape, BF16),
        in_specs=[VMEM] * (3 + len(parts)),
        out_specs=VMEM,
        compiler_params=_mb(2),
        name="finish",
    )(feat, gain.reshape(1, -1), wo, *parts)


def per_device(
    acct_feat,
    merch_feat,
    key_weight,
    msg_weight,
    query_weight,
    out_weight,
    rel_bias,
    out_gain,
    slot_acct,
    slot_merch,
    block_rel,
    block_count,
):
    devices = lax.axis_size(AXES)
    me = lax.axis_index(AXES).astype(jnp.int32).reshape(1)
    inner = 4
    outer = devices // (2 * inner)

    def swap(value, mask):
        return lax.ppermute(value, AXES, [(s, s ^ mask) for s in range(devices)])

    def after(value, *others):
        return lax.optimization_barrier((value,) + others)[0]

    order = [1, 3, 2, 0] + list(range(4, outer))
    feats = assemble(order, [swap(merch_feat, 8 * k + 1) for k in order])
    rows = gather(outer, me, slot_acct, acct_feat)
    feats = after(feats, rows[0])
    feats = jnp.concatenate([feats] + [swap(feats, 2 * j) for j in range(1, inner)], axis=0)

    weights = (key_weight, msg_weight)
    rest = (block_rel, block_count, rel_bias, slot_merch)
    blocks = inner * outer
    odd_keys, odd_values, far_keys, far_values = project(
        outer, ((0, blocks, 1), (outer, blocks, 0)), me, block_rel, rows, *weights
    )
    feats = after(feats, far_keys)
    even_feats = swap(feats, 1)
    odd = aggregate(outer, 0, 1, me, *rest, feats, query_weight, odd_keys, odd_values, BF16)
    other = swap(odd, 1)
    far = aggregate(
        outer, outer, 0, me, *rest, even_feats, query_weight, far_keys, far_values, F32
    )
    parts = combine(inner - 1, outer * merch_feat.shape[0], far, other, BF16)

    here = after(me, *parts)
    near_keys, near_values = project(
        outer, ((0, outer, 0),), here, block_rel, rows[1:], *weights
    )
    near = aggregate(
        outer, 0, 0, here, *rest, even_feats, query_weight, near_keys, near_values, F32
    )
    (near,) = combine(1, 0, near, other, F32)
    parts = combine_plane(
        outer, [near] + [swap(parts[inner - 1 - j], 2 * j) for j in reversed(range(1, inner))]
    )
    parts = [parts[0]] + [swap(parts[k], 8 * k) for k in reversed(range(1, outer))]
    return finish(merch_feat, out_gain, out_weight, parts)


def solution(mesh):
    placed = (
        P(("acct", "merch"), None),
        P(("acct", "merch"), None),
        P(),
        P(),
        P(),
        P(),
        P(),
        P(),
        P(("acct", "merch"), None),
        P(("acct", "merch"), None),
        P(("acct", "merch")),
        P(("acct", "merch")),
    )
    return jax.shard_map(
        per_device,
        mesh=mesh,
        in_specs=placed,
        out_specs=P(("acct", "merch"), None),
        check_vma=False,
    )
```

```python
import functools
import math

import jax
import jax.numpy as jnp
from jax import lax
from jax.experimental import pallas as pl
from jax.experimental.pallas import tpu as pltpu
from jax.sharding import PartitionSpec as P

AXES = ("acct", "merch")
LANES = 128
F32 = jnp.float32
BF16 = jnp.bfloat16
SMEM = pl.BlockSpec(memory_space=pltpu.SMEM)
ANY = pl.BlockSpec(memory_space=pl.ANY)
VMEM = pl.BlockSpec(memory_space=pltpu.VMEM)


def _mb(n):
    return pltpu.CompilerParams(vmem_limit_bytes=n * 2**20)


def _cost(flops, bytes_accessed, transcendentals=0):
    return pl.CostEstimate(
        flops=int(flops), bytes_accessed=int(bytes_accessed), transcendentals=transcendentals
    )


def _offset(i, outer):
    return (i // outer) * 2 + (i % outer) * 8


def gather_kernel(
    outer, me_ref, slots_ref, acct_hbm, odd, far, acct, table, rows0, rows1, sem
):
    accounts, width = acct.shape
    blocks, block_len, _ = odd.shape
    parts = width // LANES
    pitch = table.shape[1]
    batch = 32
    flat = table.reshape(accounts * pitch, LANES)
    me = me_ref[0]
    chunks = sem.shape[0]
    chunk = accounts // chunks
    copies = [
        pltpu.make_async_copy(
            acct_hbm.at[pl.ds(i * chunk, chunk)], acct.at[pl.ds(i * chunk, chunk)], sem.at[i]
        )
        for i in range(chunks)
    ]
    for copy in copies:
        copy.start()
    for i in range(chunks):
        copies[i].wait()

        @pl.loop(0, chunk // 16, unroll=4)
        def _(g):
            first = pl.multiple_of(i * chunk + g * 16, 16)
            tile = acct[pl.ds(first, 16), :].astype(F32)
            for c in range(parts):
                flat[pl.ds(first * pitch + c, 16, stride=pitch), :] = tile[
                    :, c * LANES : (c + 1) * LANES
                ]

    def collect(block, rows):
        for k in range(0, block_len, batch):
            found = [table[slots_ref[block, k + u], :parts, :] for u in range(batch)]
            for u in range(batch):
                rows[(k + u) * parts : (k + u + 1) * parts, :] = found[u]

    def emit(i, rows, out):
        for c in range(parts):
            out[i, :, c * LANES : (c + 1) * LANES] = rows[
                pl.ds(c, block_len, stride=parts), :
            ].astype(BF16)

    def odd_block(i):
        return jnp.bitwise_xor(me, _offset(i, outer) + 1)

    @pl.loop(0, outer // 2)
    def _(h):
        collect(odd_block(2 * h), rows0)
        collect(odd_block(2 * h + 1), rows1)
        emit(2 * h, rows0, odd)
        emit(2 * h + 1, rows1, odd)

    @pl.loop(outer, blocks)
    def _(i):
        collect(odd_block(i), rows0)
        collect(jnp.bitwise_xor(me, _offset(i, outer)), rows1)
        emit(i, rows0, odd)
        emit(i - outer, rows1, far)


def gather(outer, me, slots, acct):
    blocks, block_len = slots.shape
    accounts, width = acct.shape
    parts = width // LANES
    pitch = -(-parts // 8) * 8
    rows = pltpu.VMEM((block_len * parts, LANES), F32)
    half = blocks // 2
    return pl.pallas_call(
        functools.partial(gather_kernel, outer),
        out_shape=(
            jax.ShapeDtypeStruct((half, block_len, width), BF16),
            jax.ShapeDtypeStruct((half - outer, block_len, width), BF16),
        ),
        in_specs=[SMEM, SMEM, ANY],
        out_specs=(VMEM, VMEM),
        scratch_shapes=[
            pltpu.VMEM(acct.shape, BF16),
            pltpu.VMEM((accounts, pitch, LANES), F32),
            rows,
            rows,
            pltpu.SemaphoreType.DMA((8,)),
        ],
        compiler_params=_mb(47 if blocks <= 32 else 28),
        cost_estimate=_cost(0, 20 * 2**20),
        name="gather_slots",
    )(me, slots, acct)


def pick_kernel(outer, me_ref, slots, acct, out, index):
    accounts, width = acct.shape
    block_len = slots.shape[1]
    span = 512
    me = me_ref[0]
    index[...] = jnp.zeros_like(index)
    for i in range(outer):
        block = jnp.bitwise_xor(me, 8 * i)
        index[pl.ds(i, 1), :] = slots[pl.ds(block, 1), :].astype(F32)
    column = index[...].T
    for i in range(outer):
        mine = column[:, i : i + 1]
        lane = lax.broadcasted_iota(jnp.int32, (block_len, span), 1).astype(F32)
        total = jnp.zeros((block_len, width), F32)
        for first in range(0, accounts, span):
            hot = jnp.where(mine - first == lane, 1.0, 0.0).astype(BF16)
            total = total + jnp.dot(
                hot, acct[first : first + span, :], preferred_element_type=F32
            )
        out[i] = total.astype(BF16)


def pick(outer, me, slots, acct):
    block_len = slots.shape[1]
    width = acct.shape[1]
    return pl.pallas_call(
        functools.partial(pick_kernel, outer),
        out_shape=jax.ShapeDtypeStruct((outer, block_len, width), BF16),
        in_specs=[SMEM, VMEM, VMEM],
        out_specs=VMEM,
        scratch_shapes=[pltpu.VMEM((block_len, block_len), F32)],
        compiler_params=_mb(8),
        cost_estimate=_cost(2 * outer * block_len * acct.size, 8 * 2**20),
        name="pick_rows",
    )(me, slots, acct)


def project_kernel(outer, spans, me_ref, rel_ref, kw, mw, *refs):
    width = refs[0].shape[2]
    half = width // 2
    me = me_ref[0]
    count = len(spans)

    def one(i, first, shift, feats, keys, values):
        relation = rel_ref[jnp.bitwise_xor(me, _offset(first + i, outer) + shift)]
        for n in range(0, width, half):
            key = jnp.dot(
                feats[i], kw[relation, :, n : n + half], preferred_element_type=F32
            )
            keys[i, n : n + half, :] = key.astype(BF16).T
            value = jnp.dot(
                feats[i], mw[relation, :, n : n + half], preferred_element_type=F32
            )
            values[i, :, n : n + half] = value.astype(BF16)

    for s, (first, last, shift) in enumerate(spans):
        outs = refs[count + 2 * s : count + 2 * s + 2]

        @pl.loop(0, last - first, unroll=4)
        def _(i):
            one(i, first, shift, refs[s], *outs)


def project(outer, spans, me, rel, feats, kw, mw):
    _, block_len, width = feats[0].shape
    out_shape = []
    for first, last, _ in spans:
        out_shape.append(jax.ShapeDtypeStruct((last - first, width, block_len), BF16))
        out_shape.append(jax.ShapeDtypeStruct((last - first, block_len, width), BF16))
    blocks = sum(last - first for first, last, _ in spans)
    return pl.pallas_call(
        functools.partial(project_kernel, outer, spans),
        out_shape=tuple(out_shape),
        in_specs=[SMEM, SMEM] + [VMEM] * (2 + len(spans)),
        out_specs=(VMEM,) * len(out_shape),
        compiler_params=_mb(4),
        cost_estimate=_cost(4 * blocks * block_len * width * width, blocks * 2**19),
        name="project_slots",
    )(me, rel, kw, mw, *feats)


def assemble_kernel(places, *refs):
    rows = refs[0].shape[0]
    for place, part in zip(places, refs[:-1]):
        refs[-1][place * rows : (place + 1) * rows, :] = part[...]


def assemble(places, parts):
    rows, width = parts[0].shape
    return pl.pallas_call(
        functools.partial(assemble_kernel, places),
        out_shape=jax.ShapeDtypeStruct((len(parts) * rows, width), parts[0].dtype),
        in_specs=[VMEM] * len(parts),
        out_specs=VMEM,
        compiler_params=_mb(2),
        cost_estimate=_cost(1, 1),
        name="assemble",
    )(*parts)


def aggregate_kernel(
    outer, first, shift, me_ref, rel_ref, count_ref, bias_ref, merch_slot, feats, wq, keys, values,
    sums, query, gates,
):
    blocks, width, block_len = keys.shape
    merchants = sums.shape[0] // blocks
    me = me_ref[0]
    row = lax.broadcasted_iota(jnp.int32, (merchants, block_len), 0)
    lane = lax.broadcasted_iota(jnp.int32, (merchants, block_len), 1)
    query[...] = jnp.dot(
        feats[first * merchants : (first + blocks) * merchants, :],
        wq[...],
        preferred_element_type=F32,
    ).astype(BF16)
    parts = [slice(i * merchants, (i + 1) * merchants) for i in range(blocks)]
    for i in range(blocks):
        block = jnp.bitwise_xor(me, _offset(first + i, outer) + shift)
        score = jnp.dot(query[parts[i], :], keys[i], preferred_element_type=F32) / math.sqrt(width)
        score = score + bias_ref[rel_ref[block]]
        mine = (merch_slot[pl.ds(block, 1), :] == row) & (lane < count_ref[block])
        gates[parts[i], :] = jnp.where(mine, jax.nn.sigmoid(score), 0.0).astype(BF16)
    for i in range(blocks):
        sums[parts[i], :] = jnp.dot(
            gates[parts[i], :], values[i], preferred_element_type=F32
        ).astype(sums.dtype)


def aggregate(outer, first, shift, me, rel, count, bias, merch_slot, feats, wq, keys, values, dtype):
    blocks, width, block_len = keys.shape
    rows = feats.shape[0] * blocks // (merch_slot.shape[0] // 2)
    return pl.pallas_call(
        functools.partial(aggregate_kernel, outer, first, shift),
        out_shape=jax.ShapeDtypeStruct((rows, width), dtype),
        in_specs=[SMEM] * 4 + [VMEM] * 5,
        out_specs=VMEM,
        scratch_shapes=[
            pltpu.VMEM((rows, width), BF16),
            pltpu.VMEM((rows, block_len), BF16),
        ],
        compiler_params=_mb(6),
        cost_estimate=_cost(
            4 * rows * block_len * width + 2 * rows * width * width, 6 * 2**20, rows * block_len
        ),
        name="aggregate_odd" if shift else "aggregate_even",
    )(me, rel, count, bias, merch_slot, feats, wq, keys, values)


def combine_kernel(skip, mine, other, *outs):
    rows = outs[0].shape[0]
    for j, out in enumerate(reversed(outs)):
        part = slice(j * rows, (j + 1) * rows)
        theirs = slice(skip + j * rows, skip + (j + 1) * rows)
        out[...] = (mine[part, :] + other[theirs, :].astype(F32)).astype(out.dtype)


def combine(groups, skip, mine, other, dtype):
    rows, width = mine.shape
    return pl.pallas_call(
        functools.partial(combine_kernel, skip),
        out_shape=(jax.ShapeDtypeStruct((rows // groups, width), dtype),) * groups,
        in_specs=[VMEM, VMEM],
        out_specs=(VMEM,) * groups,
        compiler_params=_mb(2),
        cost_estimate=_cost(0, 2 * 2**20),
        name="combine_cores",
    )(mine, other)


def plane_kernel(inner, *refs):
    ins, outs = refs[:inner], refs[inner:]
    rows = outs[0].shape[0]
    for k, out in enumerate(outs):
        part = slice(k * rows, (k + 1) * rows)
        total = ins[0][part, :]
        for other in ins[1:]:
            total = total + other[part, :].astype(F32)
        out[...] = total.astype(out.dtype)


def combine_plane(outer, parts):
    rows, width = parts[0].shape
    return pl.pallas_call(
        functools.partial(plane_kernel, len(parts)),
        out_shape=tuple(
            jax.ShapeDtypeStruct((rows // outer, width), F32 if k == 0 else BF16)
            for k in range(outer)
        ),
        in_specs=[VMEM] * len(parts),
        out_specs=(VMEM,) * outer,
        compiler_params=_mb(2),
        cost_estimate=_cost(0, 2**20),
        name="combine_plane",
    )(*parts)


def finish_kernel(feat, gain, wo, *refs):
    out = refs[-1]
    total = refs[0][...]
    for part in refs[1:-1]:
        total = total + part[...].astype(F32)
    update = feat[...].astype(F32) + jnp.dot(
        total.astype(BF16), wo[...], preferred_element_type=F32
    )
    scale = lax.rsqrt(jnp.mean(update * update, axis=-1, keepdims=True) + 1e-06)
    out[...] = (update * scale * gain[...]).astype(BF16)


def finish(feat, gain, wo, parts):
    return pl.pallas_call(
        finish_kernel,
        out_shape=jax.ShapeDtypeStruct(feat.shape, BF16),
        in_specs=[VMEM] * (3 + len(parts)),
        out_specs=VMEM,
        compiler_params=_mb(2),
        name="finish",
    )(feat, gain.reshape(1, -1), wo, *parts)


def per_device(
    acct_feat,
    merch_feat,
    key_weight,
    msg_weight,
    query_weight,
    out_weight,
    rel_bias,
    out_gain,
    slot_acct,
    slot_merch,
    block_rel,
    block_count,
):
    devices = lax.axis_size(AXES)
    me = lax.axis_index(AXES).astype(jnp.int32).reshape(1)
    inner = 4
    outer = devices // (2 * inner)

    def swap(value, mask):
        return lax.ppermute(value, AXES, [(s, s ^ mask) for s in range(devices)])

    def after(value, *others):
        return lax.optimization_barrier((value,) + others)[0]

    order = [1, 3, 2, 0] + list(range(4, outer))
    feats = assemble(order, [swap(merch_feat, 8 * k + 1) for k in order])
    rows = gather(outer, me, slot_acct, acct_feat)
    feats = after(feats, rows[0])
    feats = jnp.concatenate([feats] + [swap(feats, 2 * j) for j in range(1, inner)], axis=0)

    weights = (key_weight, msg_weight)
    rest = (block_rel, block_count, rel_bias, slot_merch)
    blocks = inner * outer
    odd_keys, odd_values, far_keys, far_values = project(
        outer, ((0, blocks, 1), (outer, blocks, 0)), me, block_rel, rows, *weights
    )
    feats = after(feats, far_keys)
    even_feats = swap(feats, 1)
    odd = aggregate(outer, 0, 1, me, *rest, feats, query_weight, odd_keys, odd_values, BF16)
    other = swap(odd, 1)
    far = aggregate(
        outer, outer, 0, me, *rest, even_feats, query_weight, far_keys, far_values, F32
    )
    parts = combine(inner - 1, outer * merch_feat.shape[0], far, other, BF16)

    here = after(me, *parts)
    picked = (pick(outer, here, slot_acct, acct_feat),)
    near_keys, near_values = project(
        outer, ((0, outer, 0),), here, block_rel, picked, *weights
    )
    near = aggregate(
        outer, 0, 0, here, *rest, even_feats, query_weight, near_keys, near_values, F32
    )
    (near,) = combine(1, 0, near, other, F32)
    parts = combine_plane(
        outer, [near] + [swap(parts[inner - 1 - j], 2 * j) for j in reversed(range(1, inner))]
    )
    parts = [parts[0]] + [swap(parts[k], 8 * k) for k in reversed(range(1, outer))]
    return finish(merch_feat, out_gain, out_weight, parts)


def solution(mesh):
    placed = (
        P(("acct", "merch"), None),
        P(("acct", "merch"), None),
        P(),
        P(),
        P(),
        P(),
        P(),
        P(),
        P(("acct", "merch"), None),
        P(("acct", "merch"), None),
        P(("acct", "merch")),
        P(("acct", "merch")),
    )
    return jax.shard_map(
        per_device,
        mesh=mesh,
        in_specs=placed,
        out_specs=P(("acct", "merch"), None),
        check_vma=False,
    )
```

```python
import functools
import math

import jax
import jax.numpy as jnp
from jax import lax
from jax.experimental import pallas as pl
from jax.experimental.pallas import tpu as pltpu
from jax.sharding import PartitionSpec as P

AXES = ("acct", "merch")
LANES = 128
F32 = jnp.float32
BF16 = jnp.bfloat16
SMEM = pl.BlockSpec(memory_space=pltpu.SMEM)
ANY = pl.BlockSpec(memory_space=pl.ANY)
VMEM = pl.BlockSpec(memory_space=pltpu.VMEM)


def _mb(n):
    return pltpu.CompilerParams(vmem_limit_bytes=n * 2**20)


def _cost(flops, bytes_accessed, transcendentals=0):
    return pl.CostEstimate(
        flops=int(flops), bytes_accessed=int(bytes_accessed), transcendentals=transcendentals
    )


def _offset(i, outer):
    return (i // outer) * 2 + (i % outer) * 8


def gather_kernel(
    outer, me_ref, slots_ref, acct_hbm, odd, far, acct, table, rows0, rows1, sem
):
    accounts, width = acct.shape
    blocks, block_len, _ = odd.shape
    parts = width // LANES
    pitch = table.shape[1]
    batch = 32
    flat = table.reshape(accounts * pitch, LANES)
    me = me_ref[0]
    chunks = sem.shape[0]
    chunk = accounts // chunks
    copies = [
        pltpu.make_async_copy(
            acct_hbm.at[pl.ds(i * chunk, chunk)], acct.at[pl.ds(i * chunk, chunk)], sem.at[i]
        )
        for i in range(chunks)
    ]
    for copy in copies:
        copy.start()
    for i in range(chunks):
        copies[i].wait()

        @pl.loop(0, chunk // 16, unroll=4)
        def _(g):
            first = pl.multiple_of(i * chunk + g * 16, 16)
            tile = acct[pl.ds(first, 16), :].astype(F32)
            for c in range(parts):
                flat[pl.ds(first * pitch + c, 16, stride=pitch), :] = tile[
                    :, c * LANES : (c + 1) * LANES
                ]

    def collect(block, rows):
        for k in range(0, block_len, batch):
            found = [table[slots_ref[block, k + u], :parts, :] for u in range(batch)]
            for u in range(batch):
                rows[(k + u) * parts : (k + u + 1) * parts, :] = found[u]

    def emit(i, rows, out):
        for c in range(parts):
            out[i, :, c * LANES : (c + 1) * LANES] = rows[
                pl.ds(c, block_len, stride=parts), :
            ].astype(BF16)

    def odd_block(i):
        return jnp.bitwise_xor(me, _offset(i, outer) + 1)

    @pl.loop(0, outer // 2)
    def _(h):
        collect(odd_block(2 * h), rows0)
        collect(odd_block(2 * h + 1), rows1)
        emit(2 * h, rows0, odd)
        emit(2 * h + 1, rows1, odd)

    @pl.loop(outer, blocks)
    def _(i):
        collect(odd_block(i), rows0)
        collect(jnp.bitwise_xor(me, _offset(i, outer)), rows1)
        emit(i, rows0, odd)
        emit(i - outer, rows1, far)


def gather(outer, me, slots, acct):
    blocks, block_len = slots.shape
    accounts, width = acct.shape
    parts = width // LANES
    pitch = -(-parts // 8) * 8
    rows = pltpu.VMEM((block_len * parts, LANES), F32)
    half = blocks // 2
    return pl.pallas_call(
        functools.partial(gather_kernel, outer),
        out_shape=(
            jax.ShapeDtypeStruct((half, block_len, width), BF16),
            jax.ShapeDtypeStruct((half - outer, block_len, width), BF16),
        ),
        in_specs=[SMEM, SMEM, ANY],
        out_specs=(VMEM, VMEM),
        scratch_shapes=[
            pltpu.VMEM(acct.shape, BF16),
            pltpu.VMEM((accounts, pitch, LANES), F32),
            rows,
            rows,
            pltpu.SemaphoreType.DMA((8,)),
        ],
        compiler_params=_mb(47 if blocks <= 32 else 28),
        cost_estimate=_cost(0, 20 * 2**20),
        name="gather_slots",
    )(me, slots, acct)


def pick_kernel(outer, me_ref, slots, acct, out, index):
    accounts, width = acct.shape
    block_len = slots.shape[1]
    span = 512
    me = me_ref[0]
    index[...] = jnp.zeros_like(index)
    for i in range(outer):
        block = jnp.bitwise_xor(me, 8 * i)
        index[pl.ds(i, 1), :] = slots[pl.ds(block, 1), :].astype(F32)
    column = index[...].T
    for i in range(outer):
        mine = column[:, i : i + 1]
        lane = lax.broadcasted_iota(jnp.int32, (block_len, span), 1).astype(F32)
        total = jnp.zeros((block_len, width), F32)
        for first in range(0, accounts, span):
            hot = jnp.where(mine - first == lane, 1.0, 0.0).astype(BF16)
            total = total + jnp.dot(
                hot, acct[first : first + span, :], preferred_element_type=F32
            )
        out[i] = total.astype(BF16)


def pick(outer, me, slots, acct):
    block_len = slots.shape[1]
    width = acct.shape[1]
    return pl.pallas_call(
        functools.partial(pick_kernel, outer),
        out_shape=jax.ShapeDtypeStruct((outer, block_len, width), BF16),
        in_specs=[SMEM, VMEM, VMEM],
        out_specs=VMEM,
        scratch_shapes=[pltpu.VMEM((block_len, block_len), F32)],
        compiler_params=_mb(8),
        cost_estimate=_cost(2 * outer * block_len * acct.size, 8 * 2**20),
        name="pick_rows",
    )(me, slots, acct)


def project_kernel(outer, spans, me_ref, rel_ref, kw, mw, *refs):
    me = me_ref[0]
    count = len(spans)

    def one(i, first, shift, feats, keys, values):
        relation = rel_ref[jnp.bitwise_xor(me, _offset(first + i, outer) + shift)]
        key = jnp.dot(feats[i], kw[relation], preferred_element_type=F32)
        keys[i] = key.astype(BF16).T
        value = jnp.dot(feats[i], mw[relation], preferred_element_type=F32)
        values[i] = value.astype(BF16)

    for s, (first, last, shift) in enumerate(spans):
        outs = refs[count + 2 * s : count + 2 * s + 2]

        @pl.loop(0, last - first, unroll=4)
        def _(i):
            one(i, first, shift, refs[s], *outs)


def project(outer, spans, me, rel, feats, kw, mw):
    _, block_len, width = feats[0].shape
    out_shape = []
    for first, last, _ in spans:
        out_shape.append(jax.ShapeDtypeStruct((last - first, width, block_len), BF16))
        out_shape.append(jax.ShapeDtypeStruct((last - first, block_len, width), BF16))
    blocks = sum(last - first for first, last, _ in spans)
    return pl.pallas_call(
        functools.partial(project_kernel, outer, spans),
        out_shape=tuple(out_shape),
        in_specs=[SMEM, SMEM] + [VMEM] * (2 + len(spans)),
        out_specs=(VMEM,) * len(out_shape),
        compiler_params=_mb(4),
        cost_estimate=_cost(4 * blocks * block_len * width * width, blocks * 2**19),
        name="project_slots",
    )(me, rel, kw, mw, *feats)


def assemble_kernel(places, *refs):
    rows = refs[0].shape[0]
    for place, part in zip(places, refs[:-1]):
        refs[-1][place * rows : (place + 1) * rows, :] = part[...]


def assemble(places, parts):
    rows, width = parts[0].shape
    return pl.pallas_call(
        functools.partial(assemble_kernel, places),
        out_shape=jax.ShapeDtypeStruct((len(parts) * rows, width), parts[0].dtype),
        in_specs=[VMEM] * len(parts),
        out_specs=VMEM,
        compiler_params=_mb(2),
        cost_estimate=_cost(1, 1),
        name="assemble",
    )(*parts)


def aggregate_kernel(
    outer, first, shift, me_ref, rel_ref, count_ref, bias_ref, merch_slot, feats, wq, keys, values,
    sums, query, gates,
):
    blocks, width, block_len = keys.shape
    merchants = sums.shape[0] // blocks
    me = me_ref[0]
    row = lax.broadcasted_iota(jnp.int32, (merchants, block_len), 0)
    lane = lax.broadcasted_iota(jnp.int32, (merchants, block_len), 1)
    query[...] = jnp.dot(
        feats[first * merchants : (first + blocks) * merchants, :],
        wq[...],
        preferred_element_type=F32,
    ).astype(BF16)
    parts = [slice(i * merchants, (i + 1) * merchants) for i in range(blocks)]
    for i in range(blocks):
        block = jnp.bitwise_xor(me, _offset(first + i, outer) + shift)
        score = jnp.dot(query[parts[i], :], keys[i], preferred_element_type=F32) / math.sqrt(width)
        score = score + bias_ref[rel_ref[block]]
        mine = (merch_slot[pl.ds(block, 1), :] == row) & (lane < count_ref[block])
        gates[parts[i], :] = jnp.where(mine, jax.nn.sigmoid(score), 0.0).astype(BF16)
    for i in range(blocks):
        sums[parts[i], :] = jnp.dot(
            gates[parts[i], :], values[i], preferred_element_type=F32
        ).astype(sums.dtype)


def aggregate(outer, first, shift, me, rel, count, bias, merch_slot, feats, wq, keys, values, dtype):
    blocks, width, block_len = keys.shape
    rows = feats.shape[0] * blocks // (merch_slot.shape[0] // 2)
    return pl.pallas_call(
        functools.partial(aggregate_kernel, outer, first, shift),
        out_shape=jax.ShapeDtypeStruct((rows, width), dtype),
        in_specs=[SMEM] * 4 + [VMEM] * 5,
        out_specs=VMEM,
        scratch_shapes=[
            pltpu.VMEM((rows, width), BF16),
            pltpu.VMEM((rows, block_len), BF16),
        ],
        compiler_params=_mb(6),
        cost_estimate=_cost(
            4 * rows * block_len * width + 2 * rows * width * width, 6 * 2**20, rows * block_len
        ),
        name="aggregate_odd" if shift else "aggregate_even",
    )(me, rel, count, bias, merch_slot, feats, wq, keys, values)


def combine_kernel(skip, mine, other, *outs):
    rows = outs[0].shape[0]
    for j, out in enumerate(reversed(outs)):
        part = slice(j * rows, (j + 1) * rows)
        theirs = slice(skip + j * rows, skip + (j + 1) * rows)
        out[...] = (mine[part, :] + other[theirs, :].astype(F32)).astype(out.dtype)


def combine(groups, skip, mine, other, dtype):
    rows, width = mine.shape
    return pl.pallas_call(
        functools.partial(combine_kernel, skip),
        out_shape=(jax.ShapeDtypeStruct((rows // groups, width), dtype),) * groups,
        in_specs=[VMEM, VMEM],
        out_specs=(VMEM,) * groups,
        compiler_params=_mb(2),
        cost_estimate=_cost(0, 2 * 2**20),
        name="combine_cores",
    )(mine, other)


def plane_kernel(inner, *refs):
    ins, outs = refs[:inner], refs[inner:]
    rows = outs[0].shape[0]
    for k, out in enumerate(outs):
        part = slice(k * rows, (k + 1) * rows)
        total = ins[0][part, :]
        for other in ins[1:]:
            total = total + other[part, :].astype(F32)
        out[...] = total.astype(out.dtype)


def combine_plane(outer, parts):
    rows, width = parts[0].shape
    return pl.pallas_call(
        functools.partial(plane_kernel, len(parts)),
        out_shape=tuple(
            jax.ShapeDtypeStruct((rows // outer, width), F32 if k == 0 else BF16)
            for k in range(outer)
        ),
        in_specs=[VMEM] * len(parts),
        out_specs=(VMEM,) * outer,
        compiler_params=_mb(2),
        cost_estimate=_cost(0, 2**20),
        name="combine_plane",
    )(*parts)


def finish_kernel(feat, gain, wo, *refs):
    out = refs[-1]
    total = refs[0][...]
    for part in refs[1:-1]:
        total = total + part[...].astype(F32)
    update = feat[...].astype(F32) + jnp.dot(
        total.astype(BF16), wo[...], preferred_element_type=F32
    )
    scale = lax.rsqrt(jnp.mean(update * update, axis=-1, keepdims=True) + 1e-06)
    out[...] = (update * scale * gain[...]).astype(BF16)


def finish(feat, gain, wo, parts):
    return pl.pallas_call(
        finish_kernel,
        out_shape=jax.ShapeDtypeStruct(feat.shape, BF16),
        in_specs=[VMEM] * (3 + len(parts)),
        out_specs=VMEM,
        compiler_params=_mb(2),
        name="finish",
    )(feat, gain.reshape(1, -1), wo, *parts)


def per_device(
    acct_feat,
    merch_feat,
    key_weight,
    msg_weight,
    query_weight,
    out_weight,
    rel_bias,
    out_gain,
    slot_acct,
    slot_merch,
    block_rel,
    block_count,
):
    devices = lax.axis_size(AXES)
    me = lax.axis_index(AXES).astype(jnp.int32).reshape(1)
    inner = 4
    outer = devices // (2 * inner)

    def swap(value, mask):
        return lax.ppermute(value, AXES, [(s, s ^ mask) for s in range(devices)])

    def after(value, *others):
        return lax.optimization_barrier((value,) + others)[0]

    order = [1, 3, 2, 0] + list(range(4, outer))
    feats = assemble(order, [swap(merch_feat, 8 * k + 1) for k in order])
    rows = gather(outer, me, slot_acct, acct_feat)
    feats = after(feats, rows[0])
    feats = jnp.concatenate([feats] + [swap(feats, 2 * j) for j in range(1, inner)], axis=0)

    weights = (key_weight, msg_weight)
    rest = (block_rel, block_count, rel_bias, slot_merch)
    blocks = inner * outer
    odd_keys, odd_values, far_keys, far_values = project(
        outer, ((0, blocks, 1), (outer, blocks, 0)), me, block_rel, rows, *weights
    )
    feats = after(feats, far_keys)
    even_feats = swap(feats, 1)
    odd = aggregate(outer, 0, 1, me, *rest, feats, query_weight, odd_keys, odd_values, BF16)
    other = swap(odd, 1)
    far = aggregate(
        outer, outer, 0, me, *rest, even_feats, query_weight, far_keys, far_values, F32
    )
    parts = combine(inner - 1, outer * merch_feat.shape[0], far, other, BF16)

    here = after(me, *parts)
    picked = (pick(outer, here, slot_acct, acct_feat),)
    near_keys, near_values = project(
        outer, ((0, outer, 0),), here, block_rel, picked, *weights
    )
    near = aggregate(
        outer, 0, 0, here, *rest, even_feats, query_weight, near_keys, near_values, F32
    )
    (near,) = combine(1, 0, near, other, F32)
    parts = combine_plane(
        outer, [near] + [swap(parts[inner - 1 - j], 2 * j) for j in reversed(range(1, inner))]
    )
    parts = [parts[0]] + [swap(parts[k], 8 * k) for k in reversed(range(1, outer))]
    return finish(merch_feat, out_gain, out_weight, parts)


def solution(mesh):
    placed = (
        P(("acct", "merch"), None),
        P(("acct", "merch"), None),
        P(),
        P(),
        P(),
        P(),
        P(),
        P(),
        P(("acct", "merch"), None),
        P(("acct", "merch"), None),
        P(("acct", "merch")),
        P(("acct", "merch")),
    )
    return jax.shard_map(
        per_device,
        mesh=mesh,
        in_specs=placed,
        out_specs=P(("acct", "merch"), None),
        check_vma=False,
    )
```

```python
import functools
import math

import jax
import jax.numpy as jnp
from jax import lax
from jax.experimental import pallas as pl
from jax.experimental.pallas import tpu as pltpu
from jax.sharding import PartitionSpec as P

AXES = ("acct", "merch")
LANES = 128
F32 = jnp.float32
BF16 = jnp.bfloat16
SMEM = pl.BlockSpec(memory_space=pltpu.SMEM)
ANY = pl.BlockSpec(memory_space=pl.ANY)
VMEM = pl.BlockSpec(memory_space=pltpu.VMEM)


def _mb(n):
    return pltpu.CompilerParams(vmem_limit_bytes=n * 2**20)


def _cost(flops, bytes_accessed, transcendentals=0):
    return pl.CostEstimate(
        flops=int(flops), bytes_accessed=int(bytes_accessed), transcendentals=transcendentals
    )


def _offset(i, outer):
    return (i // outer) * 2 + (i % outer) * 8


def gather_kernel(
    outer, me_ref, slots_ref, acct_hbm, odd, far, acct, table, rows0, rows1, sem
):
    accounts, width = acct.shape
    blocks, block_len, _ = odd.shape
    parts = width // LANES
    pitch = table.shape[1]
    batch = 32
    flat = table.reshape(accounts * pitch, LANES)
    me = me_ref[0]
    chunks = sem.shape[0]
    chunk = accounts // chunks
    copies = [
        pltpu.make_async_copy(
            acct_hbm.at[pl.ds(i * chunk, chunk)], acct.at[pl.ds(i * chunk, chunk)], sem.at[i]
        )
        for i in range(chunks)
    ]
    for copy in copies:
        copy.start()
    for i in range(chunks):
        copies[i].wait()

        @pl.loop(0, chunk // 16, unroll=4)
        def _(g):
            first = pl.multiple_of(i * chunk + g * 16, 16)
            tile = acct[pl.ds(first, 16), :].astype(F32)
            for c in range(parts):
                flat[pl.ds(first * pitch + c, 16, stride=pitch), :] = tile[
                    :, c * LANES : (c + 1) * LANES
                ]

    def collect(block, rows):
        for k in range(0, block_len, batch):
            found = [table[slots_ref[block, k + u], :parts, :] for u in range(batch)]
            for u in range(batch):
                rows[(k + u) * parts : (k + u + 1) * parts, :] = found[u]

    def emit(i, rows, out):
        for c in range(parts):
            out[i, :, c * LANES : (c + 1) * LANES] = rows[
                pl.ds(c, block_len, stride=parts), :
            ].astype(BF16)

    def odd_block(i):
        return jnp.bitwise_xor(me, _offset(i, outer) + 1)

    @pl.loop(0, outer // 2)
    def _(h):
        collect(odd_block(2 * h), rows0)
        collect(odd_block(2 * h + 1), rows1)
        emit(2 * h, rows0, odd)
        emit(2 * h + 1, rows1, odd)

    @pl.loop(outer, blocks, unroll=2)
    def _(i):
        collect(odd_block(i), rows0)
        collect(jnp.bitwise_xor(me, _offset(i, outer)), rows1)
        emit(i, rows0, odd)
        emit(i - outer, rows1, far)


def gather(outer, me, slots, acct):
    blocks, block_len = slots.shape
    accounts, width = acct.shape
    parts = width // LANES
    pitch = -(-parts // 8) * 8
    rows = pltpu.VMEM((block_len * parts, LANES), F32)
    half = blocks // 2
    return pl.pallas_call(
        functools.partial(gather_kernel, outer),
        out_shape=(
            jax.ShapeDtypeStruct((half, block_len, width), BF16),
            jax.ShapeDtypeStruct((half - outer, block_len, width), BF16),
        ),
        in_specs=[SMEM, SMEM, ANY],
        out_specs=(VMEM, VMEM),
        scratch_shapes=[
            pltpu.VMEM(acct.shape, BF16),
            pltpu.VMEM((accounts, pitch, LANES), F32),
            rows,
            rows,
            pltpu.SemaphoreType.DMA((8,)),
        ],
        compiler_params=_mb(47 if blocks <= 32 else 28),
        cost_estimate=_cost(0, 20 * 2**20),
        name="gather_slots",
    )(me, slots, acct)


def pick_kernel(outer, me_ref, slots, acct, out, index):
    accounts, width = acct.shape
    block_len = slots.shape[1]
    span = 512
    me = me_ref[0]
    index[...] = jnp.zeros_like(index)
    for i in range(outer):
        block = jnp.bitwise_xor(me, 8 * i)
        index[pl.ds(i, 1), :] = slots[pl.ds(block, 1), :].astype(F32)
    column = index[...].T
    for i in range(outer):
        mine = column[:, i : i + 1]
        lane = lax.broadcasted_iota(jnp.int32, (block_len, span), 1).astype(F32)
        total = jnp.zeros((block_len, width), F32)
        for first in range(0, accounts, span):
            hot = jnp.where(mine - first == lane, 1.0, 0.0).astype(BF16)
            total = total + jnp.dot(
                hot, acct[first : first + span, :], preferred_element_type=F32
            )
        out[i] = total.astype(BF16)


def pick(outer, me, slots, acct):
    block_len = slots.shape[1]
    width = acct.shape[1]
    return pl.pallas_call(
        functools.partial(pick_kernel, outer),
        out_shape=jax.ShapeDtypeStruct((outer, block_len, width), BF16),
        in_specs=[SMEM, VMEM, VMEM],
        out_specs=VMEM,
        scratch_shapes=[pltpu.VMEM((block_len, block_len), F32)],
        compiler_params=_mb(8),
        cost_estimate=_cost(2 * outer * block_len * acct.size, 8 * 2**20),
        name="pick_rows",
    )(me, slots, acct)


def project_kernel(outer, spans, me_ref, rel_ref, kw, mw, *refs):
    me = me_ref[0]
    count = len(spans)

    def one(i, first, shift, feats, keys, values):
        relation = rel_ref[jnp.bitwise_xor(me, _offset(first + i, outer) + shift)]
        key = jnp.dot(feats[i], kw[relation], preferred_element_type=F32)
        keys[i] = key.astype(BF16).T
        value = jnp.dot(feats[i], mw[relation], preferred_element_type=F32)
        values[i] = value.astype(BF16)

    for s, (first, last, shift) in enumerate(spans):
        outs = refs[count + 2 * s : count + 2 * s + 2]

        @pl.loop(0, last - first, unroll=4)
        def _(i):
            one(i, first, shift, refs[s], *outs)


def project(outer, spans, me, rel, feats, kw, mw):
    _, block_len, width = feats[0].shape
    out_shape = []
    for first, last, _ in spans:
        out_shape.append(jax.ShapeDtypeStruct((last - first, width, block_len), BF16))
        out_shape.append(jax.ShapeDtypeStruct((last - first, block_len, width), BF16))
    blocks = sum(last - first for first, last, _ in spans)
    return pl.pallas_call(
        functools.partial(project_kernel, outer, spans),
        out_shape=tuple(out_shape),
        in_specs=[SMEM, SMEM] + [VMEM] * (2 + len(spans)),
        out_specs=(VMEM,) * len(out_shape),
        compiler_params=_mb(4),
        cost_estimate=_cost(4 * blocks * block_len * width * width, blocks * 2**19),
        name="project_slots",
    )(me, rel, kw, mw, *feats)


def assemble_kernel(places, *refs):
    rows = refs[0].shape[0]
    for place, part in zip(places, refs[:-1]):
        refs[-1][place * rows : (place + 1) * rows, :] = part[...]


def assemble(places, parts):
    rows, width = parts[0].shape
    return pl.pallas_call(
        functools.partial(assemble_kernel, places),
        out_shape=jax.ShapeDtypeStruct((len(parts) * rows, width), parts[0].dtype),
        in_specs=[VMEM] * len(parts),
        out_specs=VMEM,
        compiler_params=_mb(2),
        cost_estimate=_cost(1, 1),
        name="assemble",
    )(*parts)


def aggregate_kernel(
    outer, first, shift, me_ref, rel_ref, count_ref, bias_ref, merch_slot, feats, wq, keys, values,
    sums, query, gates,
):
    blocks, width, block_len = keys.shape
    merchants = sums.shape[0] // blocks
    me = me_ref[0]
    row = lax.broadcasted_iota(jnp.int32, (merchants, block_len), 0)
    lane = lax.broadcasted_iota(jnp.int32, (merchants, block_len), 1)
    query[...] = jnp.dot(
        feats[first * merchants : (first + blocks) * merchants, :],
        wq[...],
        preferred_element_type=F32,
    ).astype(BF16)
    parts = [slice(i * merchants, (i + 1) * merchants) for i in range(blocks)]
    for i in range(blocks):
        block = jnp.bitwise_xor(me, _offset(first + i, outer) + shift)
        score = jnp.dot(query[parts[i], :], keys[i], preferred_element_type=F32) / math.sqrt(width)
        score = score + bias_ref[rel_ref[block]]
        mine = (merch_slot[pl.ds(block, 1), :] == row) & (lane < count_ref[block])
        gates[parts[i], :] = jnp.where(mine, jax.nn.sigmoid(score), 0.0).astype(BF16)
    for i in range(blocks):
        sums[parts[i], :] = jnp.dot(
            gates[parts[i], :], values[i], preferred_element_type=F32
        ).astype(sums.dtype)


def aggregate(outer, first, shift, me, rel, count, bias, merch_slot, feats, wq, keys, values, dtype):
    blocks, width, block_len = keys.shape
    rows = feats.shape[0] * blocks // (merch_slot.shape[0] // 2)
    return pl.pallas_call(
        functools.partial(aggregate_kernel, outer, first, shift),
        out_shape=jax.ShapeDtypeStruct((rows, width), dtype),
        in_specs=[SMEM] * 4 + [VMEM] * 5,
        out_specs=VMEM,
        scratch_shapes=[
            pltpu.VMEM((rows, width), BF16),
            pltpu.VMEM((rows, block_len), BF16),
        ],
        compiler_params=_mb(6),
        cost_estimate=_cost(
            4 * rows * block_len * width + 2 * rows * width * width, 6 * 2**20, rows * block_len
        ),
        name="aggregate_odd" if shift else "aggregate_even",
    )(me, rel, count, bias, merch_slot, feats, wq, keys, values)


def combine_kernel(skip, mine, other, *outs):
    rows = outs[0].shape[0]
    for j, out in enumerate(reversed(outs)):
        part = slice(j * rows, (j + 1) * rows)
        theirs = slice(skip + j * rows, skip + (j + 1) * rows)
        out[...] = (mine[part, :] + other[theirs, :].astype(F32)).astype(out.dtype)


def combine(groups, skip, mine, other, dtype):
    rows, width = mine.shape
    return pl.pallas_call(
        functools.partial(combine_kernel, skip),
        out_shape=(jax.ShapeDtypeStruct((rows // groups, width), dtype),) * groups,
        in_specs=[VMEM, VMEM],
        out_specs=(VMEM,) * groups,
        compiler_params=_mb(2),
        cost_estimate=_cost(0, 2 * 2**20),
        name="combine_cores",
    )(mine, other)


def plane_kernel(inner, *refs):
    ins, outs = refs[:inner], refs[inner:]
    rows = outs[0].shape[0]
    for k, out in enumerate(outs):
        part = slice(k * rows, (k + 1) * rows)
        total = ins[0][part, :]
        for other in ins[1:]:
            total = total + other[part, :].astype(F32)
        out[...] = total.astype(out.dtype)


def combine_plane(outer, parts):
    rows, width = parts[0].shape
    return pl.pallas_call(
        functools.partial(plane_kernel, len(parts)),
        out_shape=tuple(
            jax.ShapeDtypeStruct((rows // outer, width), F32 if k == 0 else BF16)
            for k in range(outer)
        ),
        in_specs=[VMEM] * len(parts),
        out_specs=(VMEM,) * outer,
        compiler_params=_mb(2),
        cost_estimate=_cost(0, 2**20),
        name="combine_plane",
    )(*parts)


def finish_kernel(feat, gain, wo, *refs):
    out = refs[-1]
    total = refs[0][...]
    for part in refs[1:-1]:
        total = total + part[...].astype(F32)
    update = feat[...].astype(F32) + jnp.dot(
        total.astype(BF16), wo[...], preferred_element_type=F32
    )
    scale = lax.rsqrt(jnp.mean(update * update, axis=-1, keepdims=True) + 1e-06)
    out[...] = (update * scale * gain[...]).astype(BF16)


def finish(feat, gain, wo, parts):
    return pl.pallas_call(
        finish_kernel,
        out_shape=jax.ShapeDtypeStruct(feat.shape, BF16),
        in_specs=[VMEM] * (3 + len(parts)),
        out_specs=VMEM,
        compiler_params=_mb(2),
        name="finish",
    )(feat, gain.reshape(1, -1), wo, *parts)


def per_device(
    acct_feat,
    merch_feat,
    key_weight,
    msg_weight,
    query_weight,
    out_weight,
    rel_bias,
    out_gain,
    slot_acct,
    slot_merch,
    block_rel,
    block_count,
):
    devices = lax.axis_size(AXES)
    me = lax.axis_index(AXES).astype(jnp.int32).reshape(1)
    inner = 4
    outer = devices // (2 * inner)

    def swap(value, mask):
        return lax.ppermute(value, AXES, [(s, s ^ mask) for s in range(devices)])

    def after(value, *others):
        return lax.optimization_barrier((value,) + others)[0]

    order = [1, 3, 2, 0] + list(range(4, outer))
    feats = assemble(order, [swap(merch_feat, 8 * k + 1) for k in order])
    rows = gather(outer, me, slot_acct, acct_feat)
    feats = after(feats, rows[0])
    feats = jnp.concatenate([feats] + [swap(feats, 2 * j) for j in range(1, inner)], axis=0)

    weights = (key_weight, msg_weight)
    rest = (block_rel, block_count, rel_bias, slot_merch)
    blocks = inner * outer
    odd_keys, odd_values, far_keys, far_values = project(
        outer, ((0, blocks, 1), (outer, blocks, 0)), me, block_rel, rows, *weights
    )
    feats = after(feats, far_keys)
    even_feats = swap(feats, 1)
    odd = aggregate(outer, 0, 1, me, *rest, feats, query_weight, odd_keys, odd_values, BF16)
    other = swap(odd, 1)
    far = aggregate(
        outer, outer, 0, me, *rest, even_feats, query_weight, far_keys, far_values, F32
    )
    parts = combine(inner - 1, outer * merch_feat.shape[0], far, other, BF16)

    here = after(me, *parts)
    picked = (pick(outer, here, slot_acct, acct_feat),)
    near_keys, near_values = project(
        outer, ((0, outer, 0),), here, block_rel, picked, *weights
    )
    near = aggregate(
        outer, 0, 0, here, *rest, even_feats, query_weight, near_keys, near_values, F32
    )
    (near,) = combine(1, 0, near, other, F32)
    parts = combine_plane(
        outer, [near] + [swap(parts[inner - 1 - j], 2 * j) for j in reversed(range(1, inner))]
    )
    parts = [parts[0]] + [swap(parts[k], 8 * k) for k in reversed(range(1, outer))]
    return finish(merch_feat, out_gain, out_weight, parts)


def solution(mesh):
    placed = (
        P(("acct", "merch"), None),
        P(("acct", "merch"), None),
        P(),
        P(),
        P(),
        P(),
        P(),
        P(),
        P(("acct", "merch"), None),
        P(("acct", "merch"), None),
        P(("acct", "merch")),
        P(("acct", "merch")),
    )
    return jax.shard_map(
        per_device,
        mesh=mesh,
        in_specs=placed,
        out_specs=P(("acct", "merch"), None),
        check_vma=False,
    )
```

```python
import functools
import math

import jax
import jax.numpy as jnp
from jax import lax
from jax.experimental import pallas as pl
from jax.experimental.pallas import tpu as pltpu
from jax.sharding import PartitionSpec as P

AXES = ("acct", "merch")
LANES = 128
F32 = jnp.float32
BF16 = jnp.bfloat16
SMEM = pl.BlockSpec(memory_space=pltpu.SMEM)
ANY = pl.BlockSpec(memory_space=pl.ANY)
VMEM = pl.BlockSpec(memory_space=pltpu.VMEM)


def _mb(n):
    return pltpu.CompilerParams(vmem_limit_bytes=n * 2**20)


def _cost(flops, bytes_accessed, transcendentals=0):
    return pl.CostEstimate(
        flops=int(flops), bytes_accessed=int(bytes_accessed), transcendentals=transcendentals
    )


def _offset(i, outer):
    return (i // outer) * 2 + (i % outer) * 8


def gather_kernel(
    outer, me_ref, slots_ref, acct_hbm, odd, far, acct, table, rows0, rows1, sem
):
    accounts, width = acct.shape
    blocks, block_len, _ = odd.shape
    parts = width // LANES
    pitch = table.shape[1]
    batch = 32
    flat = table.reshape(accounts * pitch, LANES)
    me = me_ref[0]
    chunks = sem.shape[0]
    chunk = accounts // chunks
    copies = [
        pltpu.make_async_copy(
            acct_hbm.at[pl.ds(i * chunk, chunk)], acct.at[pl.ds(i * chunk, chunk)], sem.at[i]
        )
        for i in range(chunks)
    ]
    for copy in copies:
        copy.start()
    for i in range(chunks):
        copies[i].wait()

        @pl.loop(0, chunk // 16, unroll=4)
        def _(g):
            first = pl.multiple_of(i * chunk + g * 16, 16)
            tile = acct[pl.ds(first, 16), :].astype(F32)
            for c in range(parts):
                flat[pl.ds(first * pitch + c, 16, stride=pitch), :] = tile[
                    :, c * LANES : (c + 1) * LANES
                ]

    def collect(block, rows):
        for k in range(0, block_len, batch):
            found = [table[slots_ref[block, k + u], :parts, :] for u in range(batch)]
            for u in range(batch):
                rows[(k + u) * parts : (k + u + 1) * parts, :] = found[u]

    def emit(i, rows, out):
        for c in range(parts):
            out[i, :, c * LANES : (c + 1) * LANES] = rows[
                pl.ds(c, block_len, stride=parts), :
            ].astype(BF16)

    def odd_block(i):
        return jnp.bitwise_xor(me, _offset(i, outer) + 1)

    @pl.loop(0, outer // 2)
    def _(h):
        collect(odd_block(2 * h), rows0)
        collect(odd_block(2 * h + 1), rows1)
        emit(2 * h, rows0, odd)
        emit(2 * h + 1, rows1, odd)

    @pl.loop(outer, blocks, unroll=4)
    def _(i):
        collect(odd_block(i), rows0)
        collect(jnp.bitwise_xor(me, _offset(i, outer)), rows1)
        emit(i, rows0, odd)
        emit(i - outer, rows1, far)


def gather(outer, me, slots, acct):
    blocks, block_len = slots.shape
    accounts, width = acct.shape
    parts = width // LANES
    pitch = -(-parts // 8) * 8
    rows = pltpu.VMEM((block_len * parts, LANES), F32)
    half = blocks // 2
    return pl.pallas_call(
        functools.partial(gather_kernel, outer),
        out_shape=(
            jax.ShapeDtypeStruct((half, block_len, width), BF16),
            jax.ShapeDtypeStruct((half - outer, block_len, width), BF16),
        ),
        in_specs=[SMEM, SMEM, ANY],
        out_specs=(VMEM, VMEM),
        scratch_shapes=[
            pltpu.VMEM(acct.shape, BF16),
            pltpu.VMEM((accounts, pitch, LANES), F32),
            rows,
            rows,
            pltpu.SemaphoreType.DMA((8,)),
        ],
        compiler_params=_mb(47 if blocks <= 32 else 28),
        cost_estimate=_cost(0, 20 * 2**20),
        name="gather_slots",
    )(me, slots, acct)


def pick_kernel(outer, me_ref, slots, acct, out, index):
    accounts, width = acct.shape
    block_len = slots.shape[1]
    span = 512
    me = me_ref[0]
    index[...] = jnp.zeros_like(index)
    for i in range(outer):
        block = jnp.bitwise_xor(me, 8 * i)
        index[pl.ds(i, 1), :] = slots[pl.ds(block, 1), :].astype(F32)
    column = index[...].T
    for i in range(outer):
        mine = column[:, i : i + 1]
        lane = lax.broadcasted_iota(jnp.int32, (block_len, span), 1).astype(F32)
        total = jnp.zeros((block_len, width), F32)
        for first in range(0, accounts, span):
            hot = jnp.where(mine - first == lane, 1.0, 0.0).astype(BF16)
            total = total + jnp.dot(
                hot, acct[first : first + span, :], preferred_element_type=F32
            )
        out[i] = total.astype(BF16)


def pick(outer, me, slots, acct):
    block_len = slots.shape[1]
    width = acct.shape[1]
    return pl.pallas_call(
        functools.partial(pick_kernel, outer),
        out_shape=jax.ShapeDtypeStruct((outer, block_len, width), BF16),
        in_specs=[SMEM, VMEM, VMEM],
        out_specs=VMEM,
        scratch_shapes=[pltpu.VMEM((block_len, block_len), F32)],
        compiler_params=_mb(8),
        cost_estimate=_cost(2 * outer * block_len * acct.size, 8 * 2**20),
        name="pick_rows",
    )(me, slots, acct)


def project_kernel(outer, spans, me_ref, rel_ref, kw, mw, *refs):
    me = me_ref[0]
    count = len(spans)

    def one(i, first, shift, feats, keys, values):
        relation = rel_ref[jnp.bitwise_xor(me, _offset(first + i, outer) + shift)]
        key = jnp.dot(feats[i], kw[relation], preferred_element_type=F32)
        keys[i] = key.astype(BF16).T
        value = jnp.dot(feats[i], mw[relation], preferred_element_type=F32)
        values[i] = value.astype(BF16)

    for s, (first, last, shift) in enumerate(spans):
        outs = refs[count + 2 * s : count + 2 * s + 2]

        @pl.loop(0, last - first, unroll=4)
        def _(i):
            one(i, first, shift, refs[s], *outs)


def project(outer, spans, me, rel, feats, kw, mw):
    _, block_len, width = feats[0].shape
    out_shape = []
    for first, last, _ in spans:
        out_shape.append(jax.ShapeDtypeStruct((last - first, width, block_len), BF16))
        out_shape.append(jax.ShapeDtypeStruct((last - first, block_len, width), BF16))
    blocks = sum(last - first for first, last, _ in spans)
    return pl.pallas_call(
        functools.partial(project_kernel, outer, spans),
        out_shape=tuple(out_shape),
        in_specs=[SMEM, SMEM] + [VMEM] * (2 + len(spans)),
        out_specs=(VMEM,) * len(out_shape),
        compiler_params=_mb(4),
        cost_estimate=_cost(4 * blocks * block_len * width * width, blocks * 2**19),
        name="project_slots",
    )(me, rel, kw, mw, *feats)


def assemble_kernel(places, *refs):
    rows = refs[0].shape[0]
    for place, part in zip(places, refs[:-1]):
        refs[-1][place * rows : (place + 1) * rows, :] = part[...]


def assemble(places, parts):
    rows, width = parts[0].shape
    return pl.pallas_call(
        functools.partial(assemble_kernel, places),
        out_shape=jax.ShapeDtypeStruct((len(parts) * rows, width), parts[0].dtype),
        in_specs=[VMEM] * len(parts),
        out_specs=VMEM,
        compiler_params=_mb(2),
        cost_estimate=_cost(1, 1),
        name="assemble",
    )(*parts)


def aggregate_kernel(
    outer, first, shift, me_ref, rel_ref, count_ref, bias_ref, merch_slot, feats, wq, keys, values,
    sums, query, gates,
):
    blocks, width, block_len = keys.shape
    merchants = sums.shape[0] // blocks
    me = me_ref[0]
    row = lax.broadcasted_iota(jnp.int32, (merchants, block_len), 0)
    lane = lax.broadcasted_iota(jnp.int32, (merchants, block_len), 1)
    query[...] = jnp.dot(
        feats[first * merchants : (first + blocks) * merchants, :],
        wq[...],
        preferred_element_type=F32,
    ).astype(BF16)
    parts = [slice(i * merchants, (i + 1) * merchants) for i in range(blocks)]
    for i in range(blocks):
        block = jnp.bitwise_xor(me, _offset(first + i, outer) + shift)
        score = jnp.dot(query[parts[i], :], keys[i], preferred_element_type=F32) / math.sqrt(width)
        score = score + bias_ref[rel_ref[block]]
        mine = (merch_slot[pl.ds(block, 1), :] == row) & (lane < count_ref[block])
        gates[parts[i], :] = jnp.where(mine, jax.nn.sigmoid(score), 0.0).astype(BF16)
    for i in range(blocks):
        sums[parts[i], :] = jnp.dot(
            gates[parts[i], :], values[i], preferred_element_type=F32
        ).astype(sums.dtype)


def aggregate(outer, first, shift, me, rel, count, bias, merch_slot, feats, wq, keys, values, dtype):
    blocks, width, block_len = keys.shape
    rows = feats.shape[0] * blocks // (merch_slot.shape[0] // 2)
    return pl.pallas_call(
        functools.partial(aggregate_kernel, outer, first, shift),
        out_shape=jax.ShapeDtypeStruct((rows, width), dtype),
        in_specs=[SMEM] * 4 + [VMEM] * 5,
        out_specs=VMEM,
        scratch_shapes=[
            pltpu.VMEM((rows, width), BF16),
            pltpu.VMEM((rows, block_len), BF16),
        ],
        compiler_params=_mb(6),
        cost_estimate=_cost(
            4 * rows * block_len * width + 2 * rows * width * width, 6 * 2**20, rows * block_len
        ),
        name="aggregate_odd" if shift else "aggregate_even",
    )(me, rel, count, bias, merch_slot, feats, wq, keys, values)


def combine_kernel(skip, mine, other, *outs):
    rows = outs[0].shape[0]
    for j, out in enumerate(reversed(outs)):
        part = slice(j * rows, (j + 1) * rows)
        theirs = slice(skip + j * rows, skip + (j + 1) * rows)
        out[...] = (mine[part, :] + other[theirs, :].astype(F32)).astype(out.dtype)


def combine(groups, skip, mine, other, dtype):
    rows, width = mine.shape
    return pl.pallas_call(
        functools.partial(combine_kernel, skip),
        out_shape=(jax.ShapeDtypeStruct((rows // groups, width), dtype),) * groups,
        in_specs=[VMEM, VMEM],
        out_specs=(VMEM,) * groups,
        compiler_params=_mb(2),
        cost_estimate=_cost(0, 2 * 2**20),
        name="combine_cores",
    )(mine, other)


def plane_kernel(inner, *refs):
    ins, outs = refs[:inner], refs[inner:]
    rows = outs[0].shape[0]
    for k, out in enumerate(outs):
        part = slice(k * rows, (k + 1) * rows)
        total = ins[0][part, :]
        for other in ins[1:]:
            total = total + other[part, :].astype(F32)
        out[...] = total.astype(out.dtype)


def combine_plane(outer, parts):
    rows, width = parts[0].shape
    return pl.pallas_call(
        functools.partial(plane_kernel, len(parts)),
        out_shape=tuple(
            jax.ShapeDtypeStruct((rows // outer, width), F32 if k == 0 else BF16)
            for k in range(outer)
        ),
        in_specs=[VMEM] * len(parts),
        out_specs=(VMEM,) * outer,
        compiler_params=_mb(2),
        cost_estimate=_cost(0, 2**20),
        name="combine_plane",
    )(*parts)


def finish_kernel(feat, gain, wo, *refs):
    out = refs[-1]
    total = refs[0][...]
    for part in refs[1:-1]:
        total = total + part[...].astype(F32)
    update = feat[...].astype(F32) + jnp.dot(
        total.astype(BF16), wo[...], preferred_element_type=F32
    )
    scale = lax.rsqrt(jnp.mean(update * update, axis=-1, keepdims=True) + 1e-06)
    out[...] = (update * scale * gain[...]).astype(BF16)


def finish(feat, gain, wo, parts):
    return pl.pallas_call(
        finish_kernel,
        out_shape=jax.ShapeDtypeStruct(feat.shape, BF16),
        in_specs=[VMEM] * (3 + len(parts)),
        out_specs=VMEM,
        compiler_params=_mb(2),
        name="finish",
    )(feat, gain.reshape(1, -1), wo, *parts)


def per_device(
    acct_feat,
    merch_feat,
    key_weight,
    msg_weight,
    query_weight,
    out_weight,
    rel_bias,
    out_gain,
    slot_acct,
    slot_merch,
    block_rel,
    block_count,
):
    devices = lax.axis_size(AXES)
    me = lax.axis_index(AXES).astype(jnp.int32).reshape(1)
    inner = 4
    outer = devices // (2 * inner)

    def swap(value, mask):
        return lax.ppermute(value, AXES, [(s, s ^ mask) for s in range(devices)])

    def after(value, *others):
        return lax.optimization_barrier((value,) + others)[0]

    order = [1, 3, 2, 0] + list(range(4, outer))
    feats = assemble(order, [swap(merch_feat, 8 * k + 1) for k in order])
    rows = gather(outer, me, slot_acct, acct_feat)
    feats = after(feats, rows[0])
    feats = jnp.concatenate([feats] + [swap(feats, 2 * j) for j in range(1, inner)], axis=0)

    weights = (key_weight, msg_weight)
    rest = (block_rel, block_count, rel_bias, slot_merch)
    blocks = inner * outer
    odd_keys, odd_values, far_keys, far_values = project(
        outer, ((0, blocks, 1), (outer, blocks, 0)), me, block_rel, rows, *weights
    )
    feats = after(feats, far_keys)
    even_feats = swap(feats, 1)
    odd = aggregate(outer, 0, 1, me, *rest, feats, query_weight, odd_keys, odd_values, BF16)
    other = swap(odd, 1)
    far = aggregate(
        outer, outer, 0, me, *rest, even_feats, query_weight, far_keys, far_values, F32
    )
    parts = combine(inner - 1, outer * merch_feat.shape[0], far, other, BF16)

    here = after(me, *parts)
    picked = (pick(outer, here, slot_acct, acct_feat),)
    near_keys, near_values = project(
        outer, ((0, outer, 0),), here, block_rel, picked, *weights
    )
    near = aggregate(
        outer, 0, 0, here, *rest, even_feats, query_weight, near_keys, near_values, F32
    )
    (near,) = combine(1, 0, near, other, F32)
    parts = combine_plane(
        outer, [near] + [swap(parts[inner - 1 - j], 2 * j) for j in reversed(range(1, inner))]
    )
    parts = [parts[0]] + [swap(parts[k], 8 * k) for k in reversed(range(1, outer))]
    return finish(merch_feat, out_gain, out_weight, parts)


def solution(mesh):
    placed = (
        P(("acct", "merch"), None),
        P(("acct", "merch"), None),
        P(),
        P(),
        P(),
        P(),
        P(),
        P(),
        P(("acct", "merch"), None),
        P(("acct", "merch"), None),
        P(("acct", "merch")),
        P(("acct", "merch")),
    )
    return jax.shard_map(
        per_device,
        mesh=mesh,
        in_specs=placed,
        out_specs=P(("acct", "merch"), None),
        check_vma=False,
    )
```
